32 devices in a mesh: seq: 4 (over y, core), ctx: 2 (over x), fsdp: 4 (over z).
Axes of the slice: x: 2, y: 2, z: 4, core: 2. Of those that a mesh axis runs over, the one named last changes fastest.
Arguments:
- tokens: bfloat16 [16, 1024, 960], P(('seq', 'fsdp'), 'ctx'), may hold values from -6 to 6
- cotangent: bfloat16 [16, 1024, 960], P(('seq', 'fsdp'), 'ctx'), may hold values from -6 to 6
- positions: int32 [16, 1024], P(('seq', 'fsdp'), 'ctx'), may hold values from 0 to 1535, as said below
- doc_ids: int32 [16, 8], P(('seq', 'fsdp')), may hold values from 0 to 3, as said below
- gain_attn: bfloat16 [960], P('fsdp'), may hold values from 0.099609375 to 1.8984375
- w_qkv: bfloat16 [960, 1600], P('fsdp'), may hold values from -0.25 to 0.25
- w_out: bfloat16 [960, 960], P('fsdp'), may hold values from -0.75 to 0.75
- gain_mlp: bfloat16 [960], P('fsdp'), may hold values from 0.099609375 to 1.8984375
- w_gate_up: bfloat16 [960, 5120], P('fsdp'), may hold values from -0.1875 to 0.1875
- w_down: bfloat16 [2560, 960], P('fsdp'), may hold values from -0.125 to 0.125
Outputs:
- output: bfloat16 [16, 1024, 960], P(('seq', 'fsdp'), 'ctx')
- input_grad: bfloat16 [16, 1024, 960], P(('seq', 'fsdp'), 'ctx')
- grad_gain_attn: float32 [960], P('fsdp')
- grad_w_qkv: float32 [960, 1600], P('fsdp')
- grad_w_out: float32 [960, 960], P('fsdp')
- grad_gain_mlp: float32 [960], P('fsdp')
- grad_w_gate_up: float32 [960, 5120], P('fsdp')
- grad_w_down: float32 [2560, 960], P('fsdp')
The draws below stay inside these ranges and needn't reach their ends.
Inputs may be any that keep to these rules, and one draw needn't show every extreme that they name: In each sequence the positions start at 0 and rise by 1 or 2 from each token to the next, by 2 at exactly 512 of the steps, so the last position is the largest. `doc_ids`: in each sequence the document numbers start at 0 and rise by 0 or 1 from block to block; the last block holds the largest.
All inputs are finite; a program needn't handle non-finite values.
Results may differ from the reference program's by a relative error of at most 0.023.
Values may be sent and summed in bfloat16 or wider, within the bound.
No kernel may reach another device: no remote copies, remote signals or barrier semaphores. Data moves between devices by JAX's collectives and lax.ppermute only.
A program may use at most 192 MiB of HBM per device.

```python
import jax
import jax.numpy as jnp
from jax import lax

D = 960
HEADS = 15
KV_HEADS = 5
HEAD_DIM = 64
FF = 2560
BLK = 128
TOK_DEV = 512
KV_DIM = 320
SEQ_LEN = 1024
SEQS = 16
N_CTX = 2


def draw_positions(key, part):
    key = jax.random.fold_in(key, 11)
    seq_keys = jax.random.split(key, SEQS)
    orders = jax.vmap(lambda one_key: jax.random.permutation(one_key, SEQ_LEN - 1))(seq_keys)
    increments = 1 + (orders < SEQ_LEN // 2).astype(jnp.int32)
    steps_sum = jnp.cumsum(increments, axis=1)
    starts = jnp.zeros((SEQS, 1), jnp.int32)
    return jnp.concatenate([starts, steps_sum.astype(jnp.int32)], axis=1).astype(jnp.int32)


def draw_doc_ids(key, part):
    key = jax.random.fold_in(key, 23)
    block_count = SEQ_LEN // BLK
    per_device = block_count // N_CTX
    first_block = jax.random.randint(key, (SEQS, 1), 0, per_device)
    last_block = block_count - per_device + first_block
    block_index = jnp.arange(block_count)[None, :]
    flags = jnp.ones((SEQS, block_count), jnp.int32)
    flags = jnp.where((block_index > first_block) & (block_index <= last_block), 0, flags)
    return (jnp.cumsum(flags, axis=1) - 1).astype(jnp.int32)


def shard_levels(stream_key, shape, shards, least, high):
    loudness = 1.0
    for dim, parts in shards:
        heights = jax.random.uniform(jax.random.fold_in(jax.random.fold_in(stream_key, 6), dim), (parts,), jnp.float32, least / len(shards), high / len(shards))
        loudness = loudness * jnp.repeat(jnp.exp(heights), shape[dim] // parts).reshape((-1,) + (1,) * (len(shape) - 1 - dim))
    return loudness


def bell_draw(rng, extent, scale, bound, shards=(), held_as=jnp.bfloat16):
    entries = scale * jax.random.normal(rng, extent, jnp.float32)
    if shards:
        entries = entries * shard_levels(rng, extent, shards, -0.22, 0.18)
    return jnp.clip(entries, -bound, bound).astype(held_as)


def setup_inputs(seed: int = 0) -> dict:
    streams_of = jax.random.split(jax.random.key(seed), 11)
    tokens = bell_draw(streams_of[0], (SEQS, SEQ_LEN, D), 1.0, 6.0, ((0, 16), (1, 2)))
    cotangent = bell_draw(streams_of[1], (SEQS, SEQ_LEN, D), 1.0, 6.0, ((0, 16), (1, 2)))
    positions = draw_positions(jax.random.fold_in(streams_of[10], 71), 0)
    doc_ids = draw_doc_ids(jax.random.fold_in(streams_of[10], 71), 0)
    gain_attn = jnp.clip(1.0 + 0.18 * jax.random.normal(streams_of[4], (D,), jnp.float32), 0.099609375, 1.8984375).astype(jnp.bfloat16)
    w_qkv = bell_draw(streams_of[5], (D, D + 2 * KV_DIM), (D // 2) ** -0.5, 0.25, ((0, 4),))
    w_out = bell_draw(streams_of[6], (D, D), (D // 16) ** -0.5, 0.75, ((0, 4),))
    gain_mlp = jnp.clip(1.0 + 0.18 * jax.random.normal(streams_of[7], (D,), jnp.float32), 0.099609375, 1.8984375).astype(jnp.bfloat16)
    w_gate_up = bell_draw(streams_of[8], (D, 2 * FF), D ** -0.5, 0.1875, ((0, 4),))
    w_down = bell_draw(streams_of[9], (FF, D), FF ** -0.5, 0.125, ((0, 4),))
    return {"tokens": tokens, "cotangent": cotangent, "positions": positions, "doc_ids": doc_ids, "gain_attn": gain_attn, "w_qkv": w_qkv, "w_out": w_out, "gain_mlp": gain_mlp, "w_gate_up": w_gate_up, "w_down": w_down}


@jax.custom_vjp
def low(v):
    return lax.optimization_barrier(v.astype(jnp.bfloat16)).astype(jnp.float32)

@jax.custom_vjp
def low_back(v):
    return v

def low_keep(v):
    return (low(v), None)

def low_pass(kept, grad):
    return (grad,)

def back_keep(v):
    return (v, None)

def back_low(kept, grad):
    return (low(grad),)
low.defvjp(low_keep, low_pass)
low_back.defvjp(back_keep, back_low)
EPSILON = 1e-05
ROPE_BASE = 100000.0
MASKED_SCORE = -1e+30
HIGHEST = lax.Precision.HIGHEST

def rms_scale(values):
    return lax.rsqrt(lax.optimization_barrier(jnp.mean(values * values, axis=-1, keepdims=True)) + EPSILON)

def frequencies():
    steps = jnp.arange(HEAD_DIM // 2, dtype=jnp.float32) * 2.0 / HEAD_DIM
    return ROPE_BASE ** (-steps)

def rotate(values, angles):
    middle = values.shape[-1] // 2
    cosines = jnp.cos(angles)[:, None, :]
    sines = jnp.sin(angles)[:, None, :]
    lower_half = values[..., :middle]
    upper_half = values[..., middle:]
    return jnp.concatenate([lower_half * cosines - upper_half * sines, upper_half * cosines + lower_half * sines], axis=-1)

def attend_block(query_block, row_start, key_rows, value_rows, token_docs):
    groups = HEADS // KV_HEADS
    grouped = query_block.reshape(TOK_DEV, KV_HEADS, groups, HEAD_DIM)
    raw = jnp.einsum('qhgd,khd->hgqk', grouped, key_rows, precision=HIGHEST)
    scores = low_back(raw * HEAD_DIM ** (-0.5))
    query_index = row_start + jnp.arange(TOK_DEV, dtype=jnp.int32)
    key_index = jnp.arange(SEQ_LEN, dtype=jnp.int32)
    query_docs = lax.dynamic_slice_in_dim(token_docs, row_start, TOK_DEV)
    allowed = (key_index[None, :] <= query_index[:, None]) & (token_docs[None, :] == query_docs[:, None])
    scores = jnp.where(allowed[None, None], scores, MASKED_SCORE)
    probability = low(jax.nn.softmax(scores, axis=-1))
    attended = jnp.einsum('hgqk,khd->qhgd', probability, value_rows, precision=HIGHEST)
    return attended.reshape(TOK_DEV, D)

def layer_forward(tokens, positions, doc_ids, gain_attn, w_qkv, w_out, gain_mlp, w_gate_up, w_down):
    normed = low(tokens * rms_scale(tokens) * gain_attn)
    mixed = low_back(jnp.dot(normed, w_qkv, precision=HIGHEST))
    angles = positions.astype(jnp.float32)[:, None] * frequencies()[None, :]
    queries = low(rotate(mixed[:, :D].reshape(SEQ_LEN, HEADS, HEAD_DIM), angles))
    key_rows = low(rotate(mixed[:, D:D + KV_DIM].reshape(SEQ_LEN, KV_HEADS, HEAD_DIM), angles))
    value_rows = low(mixed[:, D + KV_DIM:].reshape(SEQ_LEN, KV_HEADS, HEAD_DIM))
    token_docs = jnp.repeat(doc_ids, BLK).astype(jnp.int32)
    query_blocks = queries.reshape(N_CTX, TOK_DEV, HEADS, HEAD_DIM)
    row_starts = jnp.arange(N_CTX, dtype=jnp.int32) * TOK_DEV

    def one_block(item):
        return attend_block(item[0], item[1], key_rows, value_rows, token_docs)
    attended = lax.map(jax.checkpoint(one_block), (query_blocks, row_starts)).reshape(SEQ_LEN, D)
    attended = low(low_back(attended))
    hidden = tokens + low_back(jnp.dot(attended, w_out, precision=HIGHEST))
    normed_mlp = low(hidden * rms_scale(hidden) * gain_mlp)
    gate_up = low_back(jnp.dot(normed_mlp, w_gate_up, precision=HIGHEST))
    activated = low(jax.nn.silu(gate_up[:, :FF]) * gate_up[:, FF:])
    return low(hidden + jnp.dot(activated, w_down, precision=HIGHEST))

def reference(tokens, cotangent, positions, doc_ids, gain_attn, w_qkv, w_out, gain_mlp, w_gate_up, w_down):
    weights = tuple((weight.astype(jnp.float32) for weight in (gain_attn, w_qkv, w_out, gain_mlp, w_gate_up, w_down)))

    def one_sequence(summed, inputs):
        seq_tokens, seq_cot, seq_pos, seq_docs = inputs

        def forward_fn(source, *params):
            return layer_forward(source, seq_pos, seq_docs, *params)
        result, pullback = jax.vjp(forward_fn, seq_tokens.astype(jnp.float32), *weights)
        gradients = pullback(seq_cot.astype(jnp.float32))
        summed = tuple((total_grad + new_grad for total_grad, new_grad in zip(summed, gradients[1:])))
        return (summed, (result.astype(jnp.bfloat16), gradients[0].astype(jnp.bfloat16)))
    zeros = tuple((jnp.zeros(weight.shape, jnp.float32) for weight in weights))
    summed, (outputs, input_grads) = lax.scan(one_sequence, zeros, (tokens, cotangent, positions, doc_ids))
    return (outputs, input_grads, summed[0], summed[1], summed[2], summed[3], summed[4], summed[5])
```

```python
import functools

import jax
import jax.numpy as jnp
from jax import lax
from jax.experimental import pallas as pl
from jax.experimental.pallas import tpu as pltpu
from jax.sharding import PartitionSpec as P

D = 960
HEADS = 15
KV_HEADS = 5
HEAD_DIM = 64
FF = 2560
BLK = 128
TOK_DEV = 512
KV_DIM = 320
QKV = D + 2 * KV_DIM
FF_HALF = FF // 2
FF_SHARD = FF // 4
ROWS = D // 4
ROWS_PAD = 256
SLICE = 32
CHUNKS = ((0, 256), (256, 384))
ROW_TILE = 256
VMEM_LIMIT = 56 * 1024 * 1024

EPSILON = 1e-05
ROPE_BASE = 100000.0
MASKED_SCORE = -1e30
AXES = ("seq", "ctx", "fsdp")
F32 = jnp.float32
BF16 = jnp.bfloat16
ANY = pl.BlockSpec(memory_space=pl.ANY)
SMEM = pl.BlockSpec(memory_space=pltpu.SMEM)
VMEM = pl.BlockSpec(memory_space=pltpu.VMEM)


def rms_scale(values):
    return lax.rsqrt(jnp.mean(values * values, axis=-1, keepdims=True) + EPSILON)


def frequencies():
    steps = jnp.arange(HEAD_DIM // 2, dtype=jnp.float32) * 2.0 / HEAD_DIM
    return ROPE_BASE ** (-steps)


def rotate(values, angles):
    middle = values.shape[-1] // 2
    cosines = jnp.cos(angles)[:, None, :]
    sines = jnp.sin(angles)[:, None, :]
    lower_half = values[..., :middle]
    upper_half = values[..., middle:]
    return jnp.concatenate(
        [lower_half * cosines - upper_half * sines, upper_half * cosines + lower_half * sines],
        axis=-1,
    )


def norm_backward(source, scale_rows, gain_vec, d_normed):
    normalized = source * scale_rows
    grad_gain = jnp.sum(d_normed * normalized, axis=0)
    weighted = d_normed * gain_vec
    d_source = scale_rows * (
        weighted - normalized * jnp.mean(weighted * normalized, axis=-1, keepdims=True)
    )
    return (d_source, grad_gain)


def after(value, *earlier):
    return lax.optimization_barrier((value, *earlier))[0]


class Links:
    def __init__(self, sizes):
        self.sizes = sizes

    def index(self, s, c, f):
        return (s * self.sizes[1] + c) * self.sizes[2] + f

    def swap(self, value, ds=0, dc=0, df=0, only=None):
        n_s, n_c, n_f = self.sizes
        pairs = [
            (self.index(s, c, f), self.index(s ^ ds, c ^ dc, f ^ df))
            for s in range(n_s)
            for c in range(n_c)
            for f in range(n_f)
            if only is None or only(s, f)
        ]
        return lax.ppermute(value, AXES, pairs)

    def core(self, value):
        return self.swap(value, ds=1)

    def plane(self, value, bits):
        return self.swap(value, ds=bits & 2, dc=bits & 1)

    def gather_plane(self, own, first=None):
        if first is None:
            return [own] + [self.plane(own, bits) for bits in (1, 2, 3)]
        second = 3 - first
        pieces = [own, None, None, None]
        pieces[first] = self.plane(own, first)
        pieces[second] = self.plane(own, second)
        pieces[3] = self.plane(pieces[first], second)
        return pieces

    def gather_z(self, own):
        return jnp.stack([self.swap(own, df=bits) for bits in (1, 2, 3)])

    def reduce_plane(self, pieces, first):
        second = 3 - first
        far = self.plane(pieces[3], first)
        near = self.plane(pieces[first], first)
        forward = (pieces[second].astype(F32) + far.astype(F32)).astype(BF16)
        last = self.plane(forward, second)
        total = pieces[0].astype(F32) + near.astype(F32) + last.astype(F32)
        total = total.astype(BF16)
        step = 2
        while step < self.sizes[1]:
            total = (total.astype(F32) + self.swap(total, dc=step).astype(F32)).astype(BF16)
            step *= 2
        return total

    def reduce_z(self, total):
        arrived = [self.swap(total[bits], df=bits) for bits in (1, 2, 3)]
        result = total[0].astype(F32)
        for value in arrived:
            result = result + value.astype(F32)
        return result.astype(BF16)


def assemble_rows_kernel(place, own, m0, m1, m2, m3, t0, t1, t2, t3, full, sem):
    p, k, f = place[0], place[1], place[2]
    first = pltpu.make_async_copy(own, full.at[f], sem)
    first.start()
    first.wait()
    for start in (True, False):
        for other, refs in enumerate(((m0, m1, m2, m3), (t0, t1, t2, t3))):
            kk = jnp.bitwise_xor(k, other)
            for q, ref in enumerate(refs):
                pp = jnp.bitwise_xor(p, q)
                row = pl.multiple_of(kk * 128 + pp * SLICE, 16)
                short = (kk * 4 + pp) == 7
                for r in range(3):
                    z = jnp.bitwise_xor(f, r + 1)

                    def go(count, ref=ref, r=r, z=z, row=row):
                        copy = pltpu.make_async_copy(
                            ref.at[r, pl.ds(0, count)], full.at[z, pl.ds(row, count)], sem
                        )
                        if start:
                            copy.start()
                        else:
                            copy.wait()

                    pl.when(short)(functools.partial(go, 16))
                    pl.when(jnp.logical_not(short))(functools.partial(go, SLICE))


def assemble_rows(place, own, mine, theirs):
    width = own.shape[1]
    return pl.pallas_call(
        assemble_rows_kernel,
        out_shape=jax.ShapeDtypeStruct((4, ROWS, width), BF16),
        in_specs=[SMEM] + [ANY] * 9,
        out_specs=VMEM,
        scratch_shapes=[pltpu.SemaphoreType.DMA(())],
        compiler_params=pltpu.CompilerParams(vmem_limit_bytes=VMEM_LIMIT),
        cost_estimate=pl.CostEstimate(flops=0, bytes_accessed=4 * D * width, transcendentals=0),
    )(place, own, *mine, *theirs).reshape(D, width)


def scatter_rows_kernel(place, grad, m0, m1, m2, m3, t0, t1, t2, t3, sem):
    p, k, f = place[0], place[1], place[2]
    for start in (True, False):
        for other, refs in enumerate(((m0, m1, m2, m3), (t0, t1, t2, t3))):
            kk = jnp.bitwise_xor(k, other)
            for q, ref in enumerate(refs):
                pp = jnp.bitwise_xor(p, q)
                row = pl.multiple_of(kk * 128 + pp * SLICE, 16)
                short = (kk * 4 + pp) == 7
                for r in range(4):
                    z = jnp.bitwise_xor(f, r)

                    def go(count, ref=ref, r=r, z=z, row=row):
                        copy = pltpu.make_async_copy(
                            grad.at[z, pl.ds(row, count)], ref.at[r, pl.ds(0, count)], sem
                        )
                        if start:
                            copy.start()
                        else:
                            copy.wait()

                    pl.when(short)(functools.partial(go, 16))
                    pl.when(jnp.logical_not(short))(functools.partial(go, SLICE))


def scatter_rows(place, grad):
    width = grad.shape[1]
    piece = jax.ShapeDtypeStruct((4, SLICE, width), BF16)
    out = pl.pallas_call(
        scatter_rows_kernel,
        out_shape=[piece] * 8,
        in_specs=[SMEM, VMEM],
        out_specs=[ANY] * 8,
        scratch_shapes=[pltpu.SemaphoreType.DMA(())],
        compiler_params=pltpu.CompilerParams(vmem_limit_bytes=VMEM_LIMIT),
        cost_estimate=pl.CostEstimate(flops=0, bytes_accessed=4 * D * width, transcendentals=0),
    )(place, grad.reshape(4, ROWS, width))
    return out[:4], out[4:]


def finish_rows_kernel(place, m0, m1, m2, m3, t0, t1, t2, t3, full):
    p, k = place[0], place[1]
    for other, refs in enumerate(((m0, m1, m2, m3), (t0, t1, t2, t3))):
        kk = jnp.bitwise_xor(k, other)
        for q, ref in enumerate(refs):
            pp = jnp.bitwise_xor(p, q)
            row = pl.multiple_of(kk * 128 + pp * SLICE, 16)
            short = (kk * 4 + pp) == 7

            def go(count, ref=ref, row=row):
                full[pl.ds(row, count), :] = ref[pl.ds(0, count), :].astype(F32)

            pl.when(short)(functools.partial(go, 16))
            pl.when(jnp.logical_not(short))(functools.partial(go, SLICE))


def finish_rows(place, mine, theirs):
    width = mine[0].shape[1]
    return pl.pallas_call(
        finish_rows_kernel,
        out_shape=jax.ShapeDtypeStruct((ROWS, width), F32),
        in_specs=[SMEM] + [VMEM] * 8,
        out_specs=VMEM,
        cost_estimate=pl.CostEstimate(flops=0, bytes_accessed=6 * ROWS * width, transcendentals=0),
    )(place, *mine, *theirs)


def rows_in(rows):
    return (((0,), (0,)), ((), ()))


NT = (((1,), (1,)), ((), ()))
TN = (((0,), (0,)), ((), ()))


def mlp_kernel(
    first,
    last,
    start_col,
    place,
    x_own,
    x_oth,
    dy_own,
    dy_oth,
    gate_up_own,
    u0,
    u1,
    u2,
    u3,
    d0,
    d1,
    d2,
    d3,
    *rest,
):
    if first:
        carried = None
    else:
        carried, rest = rest[:4], rest[4:]
    out_own, out_oth, dn_own, dn_oth = rest[:4]
    gu_out = rest[4:8]
    gd_out = rest[8:12]
    up_w, down_w, act, dgu, gu, gd, x, dy, acc_out, acc_dn, sem = rest[12:]
    width = act.shape[1]
    p, k, f = place[0], place[1], place[2]

    copies = []
    for half, (xs, ds) in enumerate(((x_own, dy_own), (x_oth, dy_oth))):
        rows = pl.ds(half * TOK_DEV, TOK_DEV)
        copies.append(pltpu.make_async_copy(xs, x.at[rows], sem))
        copies.append(pltpu.make_async_copy(ds, dy.at[rows], sem))
    for pp in range(4):
        col = pl.multiple_of((pp // 2) * FF + k * FF_HALF + (pp % 2) * FF_SHARD + start_col, 128)
        copies.append(
            pltpu.make_async_copy(gate_up_own.at[:, pl.ds(col, width)], up_w.at[pp, f], sem)
        )
    for q, ref in enumerate((u0, u1, u2, u3)):
        for r in range(3):
            copies.append(
                pltpu.make_async_copy(
                    ref.at[r], up_w.at[jnp.bitwise_xor(p, q), jnp.bitwise_xor(f, r + 1)], sem
                )
            )
    for q, ref in enumerate((d0, d1, d2, d3)):
        for t in range(2):
            block = jnp.bitwise_xor(jnp.bitwise_and(f, 1), t)
            copies.append(
                pltpu.make_async_copy(ref.at[t], down_w.at[block, jnp.bitwise_xor(p, q)], sem)
            )
    if not first:
        for half in range(2):
            rows = pl.ds(half * TOK_DEV, TOK_DEV)
            copies.append(pltpu.make_async_copy(carried[half], acc_out.at[rows], sem))
            copies.append(pltpu.make_async_copy(carried[2 + half], acc_dn.at[rows], sem))
    for copy in copies:
        copy.start()
    for copy in copies:
        copy.wait()

    for block in range(2):
        gate_w = up_w[block].reshape(D, width)
        lift_w = up_w[2 + block].reshape(D, width)
        drop_w = down_w[block].reshape(width, D)

        @pl.loop(0, 2 * TOK_DEV // ROW_TILE)
        def tile(t):
            rows = pl.ds(pl.multiple_of(t * ROW_TILE, ROW_TILE), ROW_TILE)
            g = jnp.dot(x[rows, :], gate_w, preferred_element_type=F32)
            u = jnp.dot(x[rows, :], lift_w, preferred_element_type=F32)
            da = lax.dot_general(dy[rows, :], drop_w, NT, preferred_element_type=F32)
            sig = jax.nn.sigmoid(g)
            silu = g * sig
            a = (silu * u).astype(BF16)
            dg = (da * u * sig * (1.0 + g * (1.0 - sig))).astype(BF16)
            du = (da * silu).astype(BF16)
            act[rows, :] = a
            dgu[rows, :width] = dg
            dgu[rows, width:] = du
            out = jnp.dot(a, drop_w, preferred_element_type=F32)
            dn = lax.dot_general(dg, gate_w, NT, preferred_element_type=F32)
            dn = dn + lax.dot_general(du, lift_w, NT, preferred_element_type=F32)
            if first and block == 0:
                acc_out[rows, :] = out
                acc_dn[rows, :] = dn
            else:
                acc_out[rows, :] += out
                acc_dn[rows, :] += dn

        grad = lax.dot_general(x[...], dgu[...], TN, preferred_element_type=F32).astype(BF16)
        gu[block] = grad[:, :width].reshape(4, ROWS, width)
        gu[2 + block] = grad[:, width:].reshape(4, ROWS, width)
        grad = lax.dot_general(act[...], dy[...], TN, preferred_element_type=F32).astype(BF16)
        gd[block] = grad.reshape(4, width // 4, D)

    copies = []
    for q, ref in enumerate(gu_out):
        for r in range(4):
            copies.append(
                pltpu.make_async_copy(
                    gu.at[jnp.bitwise_xor(p, q), jnp.bitwise_xor(f, r)], ref.at[r], sem
                )
            )
    for q, ref in enumerate(gd_out):
        for t in range(2):
            block = jnp.bitwise_xor(jnp.bitwise_and(f, 1), t)
            copies.append(
                pltpu.make_async_copy(gd.at[block, jnp.bitwise_xor(p, q)], ref.at[t], sem)
            )
    for copy in copies:
        copy.start()
    out_own[...] = acc_out[:TOK_DEV, :]
    dn_own[...] = acc_dn[:TOK_DEV, :]
    out_oth[...] = acc_out[TOK_DEV:, :].astype(out_oth.dtype)
    dn_oth[...] = acc_dn[TOK_DEV:, :].astype(dn_oth.dtype)
    for copy in copies:
        copy.wait()


def mlp_chunk(place, chunk, tokens, weights, carried):
    start_col, width = CHUNKS[chunk]
    last = chunk == len(CHUNKS) - 1
    first = chunk == 0
    x_own, x_oth, dy_own, dy_oth = tokens
    gate_up_own, up_pieces, down_pieces = weights
    side = jax.ShapeDtypeStruct((TOK_DEV, D), BF16 if last else F32)
    main = jax.ShapeDtypeStruct((TOK_DEV, D), F32)
    part = jax.ShapeDtypeStruct((4, ROWS, width), BF16)
    down = jax.ShapeDtypeStruct((2, width // 4, D), BF16)
    operands = [place, x_own, x_oth, dy_own, dy_oth, gate_up_own, *up_pieces, *down_pieces]
    if not first:
        operands += list(carried)
    flops = 2 * 2 * TOK_DEV * D * 2 * width * 9
    out = pl.pallas_call(
        functools.partial(mlp_kernel, first, last, start_col),
        out_shape=[main, side, main, side] + [part] * 4 + [down] * 4,
        in_specs=[SMEM] + [ANY] * (len(operands) - 1),
        out_specs=[VMEM] * 4 + [ANY] * 8,
        scratch_shapes=[
            pltpu.VMEM((4, 4, ROWS, width), BF16),
            pltpu.VMEM((2, 4, width // 4, D), BF16),
            pltpu.VMEM((2 * TOK_DEV, width), BF16),
            pltpu.VMEM((2 * TOK_DEV, 2 * width), BF16),
            pltpu.VMEM((4, 4, ROWS, width), BF16),
            pltpu.VMEM((2, 4, width // 4, D), BF16),
            pltpu.VMEM((2 * TOK_DEV, D), BF16),
            pltpu.VMEM((2 * TOK_DEV, D), BF16),
            pltpu.VMEM((2 * TOK_DEV, D), F32),
            pltpu.VMEM((2 * TOK_DEV, D), F32),
            pltpu.SemaphoreType.DMA(()),
        ],
        compiler_params=pltpu.CompilerParams(vmem_limit_bytes=VMEM_LIMIT),
        cost_estimate=pl.CostEstimate(
            flops=flops, bytes_accessed=20_000_000, transcendentals=4 * TOK_DEV * width
        ),
    )(*operands)
    return out[:4], out[4:8], out[8:12]


def finish_up_kernel(place, *refs):
    full = refs[-1]
    p, k = place[0], place[1]
    position = 0
    for start_col, width in CHUNKS:
        for other in range(2):
            kk = jnp.bitwise_xor(k, other)
            for q in range(4):
                pp = jnp.bitwise_xor(p, q)
                col = (
                    jnp.right_shift(pp, 1) * FF
                    + kk * FF_HALF
                    + jnp.bitwise_and(pp, 1) * FF_SHARD
                    + start_col
                )
                full[:, pl.ds(pl.multiple_of(col, 128), width)] = refs[position][...].astype(F32)
                position += 1


def finish_up(place, pieces):
    return pl.pallas_call(
        finish_up_kernel,
        out_shape=jax.ShapeDtypeStruct((ROWS, 2 * FF), F32),
        in_specs=[SMEM] + [VMEM] * len(pieces),
        out_specs=VMEM,
        compiler_params=pltpu.CompilerParams(vmem_limit_bytes=VMEM_LIMIT),
        cost_estimate=pl.CostEstimate(flops=0, bytes_accessed=12 * ROWS * FF, transcendentals=0),
    )(place, *pieces)


def finish_down_kernel(place, *refs):
    full = refs[-1]
    p, k = place[0], place[1]
    position = 0
    for start_col, width in CHUNKS:
        for other in range(2):
            kk = jnp.bitwise_xor(k, other)
            for q in range(4):
                pp = jnp.bitwise_xor(p, q)
                row = start_col + pp * (width // 4) + kk * (width // 8)
                full[pl.ds(pl.multiple_of(row, 16), width // 8), :] = refs[position][...].astype(F32)
                position += 1


def finish_down(place, pieces):
    return pl.pallas_call(
        finish_down_kernel,
        out_shape=jax.ShapeDtypeStruct((FF_SHARD, D), F32),
        in_specs=[SMEM] + [VMEM] * len(pieces),
        out_specs=VMEM,
        compiler_params=pltpu.CompilerParams(vmem_limit_bytes=VMEM_LIMIT),
        cost_estimate=pl.CostEstimate(flops=0, bytes_accessed=6 * FF_SHARD * D, transcendentals=0),
    )(place, *pieces)


def block_scores(query_groups, key_block, key_offset, query_index, query_docs, token_docs):
    row_count = key_block.shape[0]
    raw = jnp.einsum("qhgd,khd->hgqk", query_groups, key_block, preferred_element_type=jnp.float32)
    key_index = key_offset + jnp.arange(row_count, dtype=jnp.int32)
    key_docs = lax.dynamic_slice_in_dim(token_docs, key_offset, row_count)
    allowed = (key_index[None, :] <= query_index[:, None]) & (
        key_docs[None, :] == query_docs[:, None]
    )
    return (raw * HEAD_DIM ** (-0.5), allowed[None, None])


def native(s, f):
    return (f >> 1) == (s & 1)


def foreign(s, f):
    return not native(s, f)


def shards(
    links,
    tokens,
    cotangent,
    positions,
    doc_ids,
    gain_attn,
    w_qkv,
    w_out,
    gain_mlp,
    w_gate_up,
    w_down,
):
    seq_at, ctx_at, f = (lax.axis_index(name) for name in AXES)
    k = jnp.bitwise_and(seq_at, 1)
    p = 2 * jnp.right_shift(seq_at, 1) + jnp.bitwise_and(ctx_at, 1)
    place = jnp.stack([p, k, f]).astype(jnp.int32)
    is_native = jnp.right_shift(f, 1) == k

    def row_slice(weight):
        padded = jnp.pad(weight, ((0, ROWS_PAD - ROWS), (0, 0)))
        return lax.dynamic_slice_in_dim(padded, k * 128 + p * SLICE, SLICE, 0)

    def gather_rows(weight, *earlier):
        return links.gather_z(after(row_slice(weight), *earlier))

    gains = jnp.stack([gain_attn, gain_mlp])
    gain_pieces = [gains] + [links.swap(gains, df=bits) for bits in (1, 2, 3)]
    gain_rows = jnp.stack(gain_pieces)
    gain_rows = jnp.stack(
        [lax.dynamic_index_in_dim(gain_rows, jnp.bitwise_xor(f, z), 0, False) for z in range(4)]
    )
    gain_one = gain_rows[:, 0].reshape(D).astype(F32)
    gain_two = gain_rows[:, 1].reshape(D).astype(F32)

    dy_own = cotangent[0]
    qkv_z = gather_rows(w_qkv)
    out_z = gather_rows(w_out, qkv_z)
    qkv_mine = links.gather_plane(qkv_z)
    qkv_theirs = [links.core(piece) for piece in qkv_mine]
    qkv_full = assemble_rows(place, w_qkv, qkv_mine, qkv_theirs)
    out_mine = links.gather_plane(after(out_z, *qkv_mine))
    out_theirs = [links.core(piece) for piece in out_mine]
    out_full = assemble_rows(place, w_out, out_mine, out_theirs)
    dy_oth = links.core(dy_own)

    chunk_weights = []
    before_z = (out_z,)
    before_plane = tuple(out_mine)
    for chunk, (start_col, width) in enumerate(CHUNKS):
        col = (
            jnp.right_shift(p, 1) * FF
            + k * FF_HALF
            + jnp.bitwise_and(p, 1) * FF_SHARD
            + start_col
        )
        up_own = after(lax.dynamic_slice_in_dim(w_gate_up, col, width, 1), *before_z)
        up_z = links.gather_z(up_own)
        short = width // 4
        down_own = lax.dynamic_slice_in_dim(w_down, start_col + p * short, short, 0)
        down_own = after(down_own, *before_z)
        down_1 = links.swap(down_own, df=1, only=native)
        down_2 = links.swap(down_own, ds=1, df=2, only=foreign)
        down_3 = links.swap(down_own, ds=1, df=3, only=foreign)
        down_z = jnp.stack(
            [jnp.where(is_native, down_own, down_2), jnp.where(is_native, down_1, down_3)]
        )
        before_z = (up_z, down_z)
        up_z = after(up_z, *before_plane)
        down_z = after(down_z, *before_plane)
        first = 1 if chunk % 2 == 0 else 2
        up_pieces = links.gather_plane(up_z, first)
        down_pieces = links.gather_plane(down_z, first)
        before_plane = tuple(up_pieces + down_pieces)
        chunk_weights.append((w_gate_up, up_pieces, down_pieces))

    groups = HEADS // KV_HEADS
    seq_length = doc_ids.shape[1] * BLK
    row_start = ctx_at * TOK_DEV
    query_index = row_start + jnp.arange(TOK_DEV, dtype=jnp.int32)
    token_docs = jnp.repeat(doc_ids[0], BLK)
    query_docs = lax.dynamic_slice_in_dim(token_docs, row_start, TOK_DEV)
    source = tokens[0].astype(jnp.float32)
    scale_attn = rms_scale(source)
    normed = (source * scale_attn * gain_one).astype(jnp.bfloat16)
    mixed = jnp.dot(normed, qkv_full, preferred_element_type=jnp.float32)
    angles = positions[0].astype(jnp.float32)[:, None] * frequencies()[None, :]
    queries_b = rotate(mixed[:, :D].reshape(TOK_DEV, HEADS, HEAD_DIM), angles).astype(jnp.bfloat16)
    keys_rot = rotate(mixed[:, D : D + KV_DIM].reshape(TOK_DEV, KV_HEADS, HEAD_DIM), angles)
    key_value = jnp.concatenate(
        [keys_rot.reshape(TOK_DEV, KV_DIM), mixed[:, D + KV_DIM :]], axis=-1
    ).astype(jnp.bfloat16)
    query_groups = queries_b.reshape(TOK_DEV, KV_HEADS, groups, HEAD_DIM)
    start_state = (
        jnp.full((KV_HEADS, groups, TOK_DEV), MASKED_SCORE, jnp.float32),
        jnp.zeros((KV_HEADS, groups, TOK_DEV), jnp.float32),
        jnp.zeros((TOK_DEV, KV_HEADS, groups, HEAD_DIM), jnp.float32),
    )
    slab = lax.all_gather(key_value, "ctx", axis=0, tiled=True)
    block_total = slab.shape[0] // TOK_DEV
    slabs = slab.reshape(block_total, TOK_DEV, 2 * KV_DIM)
    offsets = TOK_DEV * jnp.arange(block_total, dtype=jnp.int32)

    def one_block(state, item):
        block_rows, key_offset = item
        best, totals, accum = state
        key_block = block_rows[:, :KV_DIM].reshape(TOK_DEV, KV_HEADS, HEAD_DIM)
        value_block = block_rows[:, KV_DIM:].reshape(TOK_DEV, KV_HEADS, HEAD_DIM)
        scores, allowed = block_scores(
            query_groups, key_block, key_offset, query_index, query_docs, token_docs
        )
        new_best = jnp.maximum(best, jnp.max(jnp.where(allowed, scores, MASKED_SCORE), axis=-1))
        expo = jnp.where(allowed, jnp.exp(scores - new_best[..., None]), 0.0)
        decay = jnp.exp(best - new_best)
        totals = totals * decay + jnp.sum(expo, axis=-1)
        added = jnp.einsum(
            "hgqk,khd->qhgd",
            expo.astype(jnp.bfloat16),
            value_block,
            preferred_element_type=jnp.float32,
        )
        accum = accum * jnp.transpose(decay, (2, 0, 1))[..., None] + added
        return ((new_best, totals, accum), None)

    best, totals, accum = lax.scan(one_block, start_state, (slabs, offsets))[0]
    attn_groups = accum / jnp.transpose(totals, (2, 0, 1))[..., None]
    log_total = best + jnp.log(totals)
    attended_b = attn_groups.reshape(TOK_DEV, D).astype(jnp.bfloat16)
    hidden = source + jnp.dot(attended_b, out_full, preferred_element_type=jnp.float32)
    scale_mlp = rms_scale(hidden)
    normed_mlp = (hidden * scale_mlp * gain_two).astype(jnp.bfloat16)

    x_oth = links.core(normed_mlp)
    mlp_tokens = (normed_mlp, x_oth, dy_own, dy_oth)
    carried = None
    up_done, down_done = [], []
    for chunk, (start_col, width) in enumerate(CHUNKS):
        carried, up_grads, down_grads = mlp_chunk(
            place, chunk, mlp_tokens, chunk_weights[chunk], carried
        )
        first = 1 if chunk % 2 == 0 else 2
        down_sum = links.reduce_plane(down_grads, first)
        arrived_1 = links.swap(down_sum[1], df=1, only=native)
        arrived_2 = links.swap(down_sum[0], ds=1, df=2, only=foreign)
        arrived_3 = links.swap(down_sum[1], ds=1, df=3, only=foreign)
        down_sum = jnp.where(is_native, down_sum[0], arrived_2).astype(F32) + jnp.where(
            is_native, arrived_1, arrived_3
        ).astype(F32)
        down_sum = down_sum.astype(BF16)
        part = width // 8
        halves = down_sum.reshape(2, part, D)
        keep = lax.dynamic_index_in_dim(halves, k, 0, False)
        give = lax.dynamic_index_in_dim(halves, 1 - k, 0, False)
        down_part = (keep.astype(F32) + links.core(give).astype(F32)).astype(BF16)
        pieces = links.gather_plane(down_part, 3 - first)
        down_done += pieces + [links.core(piece) for piece in pieces]
        up_sum = links.reduce_z(links.reduce_plane(up_grads, first))
        pieces = links.gather_plane(up_sum, 3 - first)
        up_done += pieces + [links.core(piece) for piece in pieces]
    grad_gate_up = finish_up(place, up_done)
    grad_down = finish_down(place, down_done)
    out_own, out_oth, dn_own, dn_oth = carried
    result = hidden + out_own + links.core(out_oth).astype(F32)
    output = result.astype(jnp.bfloat16)[None]
    d_normed_mlp = dn_own + links.core(dn_oth).astype(F32)

    d_from_norm, grad_gain_mlp = norm_backward(hidden, scale_mlp, gain_two, d_normed_mlp)
    d_hidden = dy_own.astype(jnp.float32) + d_from_norm
    d_hidden_b = d_hidden.astype(jnp.bfloat16)
    grad_out_proj = jnp.dot(attended_b.T, d_hidden_b, preferred_element_type=jnp.float32)
    d_attended = jnp.dot(d_hidden_b, out_full.T, preferred_element_type=jnp.float32).astype(
        jnp.bfloat16
    )
    d_out_groups = d_attended.reshape(TOK_DEV, KV_HEADS, groups, HEAD_DIM)
    row_delta = jnp.transpose(
        jnp.sum(d_out_groups.astype(jnp.float32) * attn_groups, axis=-1), (1, 2, 0)
    )

    def back_block(d_query, item):
        block_rows, key_offset = item
        key_block = block_rows[:, :KV_DIM].reshape(TOK_DEV, KV_HEADS, HEAD_DIM)
        value_block = block_rows[:, KV_DIM:].reshape(TOK_DEV, KV_HEADS, HEAD_DIM)
        scores, allowed = block_scores(
            query_groups, key_block, key_offset, query_index, query_docs, token_docs
        )
        probability = jnp.where(allowed, jnp.exp(scores - log_total[..., None]), 0.0)
        d_value = jnp.einsum(
            "hgqk,qhgd->khd",
            probability.astype(jnp.bfloat16),
            d_out_groups,
            preferred_element_type=jnp.float32,
        )
        d_prob = jnp.einsum(
            "qhgd,khd->hgqk", d_out_groups, value_block, preferred_element_type=jnp.float32
        )
        d_scores = (probability * (d_prob - row_delta[..., None])).astype(jnp.bfloat16)
        d_query = d_query + HEAD_DIM ** (-0.5) * jnp.einsum(
            "hgqk,khd->qhgd", d_scores, key_block, preferred_element_type=jnp.float32
        )
        d_key = HEAD_DIM ** (-0.5) * jnp.einsum(
            "hgqk,qhgd->khd", d_scores, query_groups, preferred_element_type=jnp.float32
        )
        return (
            d_query,
            jnp.concatenate(
                [d_key.reshape(TOK_DEV, KV_DIM), d_value.reshape(TOK_DEV, KV_DIM)], axis=-1
            ),
        )

    d_query_zero = jnp.zeros((TOK_DEV, KV_HEADS, groups, HEAD_DIM), jnp.float32)
    d_query, key_terms = lax.scan(back_block, d_query_zero, (slabs, offsets))
    key_grads = lax.psum_scatter(
        key_terms.reshape(seq_length, 2 * KV_DIM).astype(jnp.bfloat16),
        "ctx",
        scatter_dimension=0,
        tiled=True,
    ).astype(jnp.float32)
    d_queries = rotate(d_query.reshape(TOK_DEV, HEADS, HEAD_DIM), -angles).reshape(TOK_DEV, D)
    d_keys = rotate(key_grads[:, :KV_DIM].reshape(TOK_DEV, KV_HEADS, HEAD_DIM), -angles).reshape(
        TOK_DEV, KV_DIM
    )
    d_mixed = jnp.concatenate([d_queries, d_keys, key_grads[:, KV_DIM:]], axis=-1).astype(
        jnp.bfloat16
    )
    grad_qkv = jnp.dot(normed.T, d_mixed, preferred_element_type=jnp.float32)
    d_normed = jnp.dot(d_mixed, qkv_full.T, preferred_element_type=jnp.float32)
    d_source, grad_gain_attn = norm_backward(source, scale_attn, gain_one, d_normed)
    input_grad = (d_hidden + d_source).astype(jnp.bfloat16)[None]

    def reduce_rows(grad, first):
        mine, theirs = scatter_rows(place, grad.astype(BF16))
        arrived = [links.core(piece) for piece in theirs]
        mine = [(a.astype(F32) + b.astype(F32)).astype(BF16) for a, b in zip(mine, arrived)]
        total = links.reduce_z(links.reduce_plane(mine, first))
        pieces = links.gather_plane(total, 3 - first)
        return finish_rows(place, pieces, [links.core(piece) for piece in pieces])

    grad_out = reduce_rows(grad_out_proj, 1)
    pair = jnp.stack([grad_gain_attn, grad_gain_mlp], axis=1)
    widened = jnp.concatenate([grad_qkv, pair], axis=1)
    reduced = reduce_rows(widened, 2)
    return (
        output,
        input_grad,
        reduced[:, QKV],
        reduced[:, :QKV],
        grad_out,
        reduced[:, QKV + 1],
        grad_gate_up,
        grad_down,
    )


def solution(mesh):
    placed = (
        P(("seq", "fsdp"), "ctx", None),
        P(("seq", "fsdp"), "ctx", None),
        P(("seq", "fsdp"), "ctx"),
        P(("seq", "fsdp"), None),
        P("fsdp"),
        P("fsdp", None),
        P("fsdp", None),
        P("fsdp"),
        P("fsdp", None),
        P("fsdp", None),
    )
    links = Links([mesh.shape[name] for name in AXES])
    return jax.shard_map(
        functools.partial(shards, links),
        mesh=mesh,
        in_specs=placed,
        out_specs=(
            P(("seq", "fsdp"), "ctx", None),
            P(("seq", "fsdp"), "ctx", None),
            P("fsdp"),
            P("fsdp", None),
            P("fsdp", None),
            P("fsdp"),
            P("fsdp", None),
            P("fsdp", None),
        ),
        check_vma=False,
    )
```

```python
import functools

import jax
import jax.numpy as jnp
from jax import lax
from jax.experimental import pallas as pl
from jax.experimental.pallas import tpu as pltpu
from jax.sharding import PartitionSpec as P

D = 960
HEADS = 15
KV_HEADS = 5
HEAD_DIM = 64
FF = 2560
BLK = 128
TOK_DEV = 512
KV_DIM = 320
QKV = D + 2 * KV_DIM
QKV_WIDE = 1664
FF_HALF = FF // 2
FF_SHARD = FF // 4
ROWS = D // 4
ROWS_PAD = 256
SLICE = 32
CHUNKS = ((0, 256), (256, 384))
ROW_TILE = 256
VMEM_LIMIT = 56 * 1024 * 1024

EPSILON = 1e-05
ROPE_BASE = 100000.0
MASKED_SCORE = -1e30
AXES = ("seq", "ctx", "fsdp")
F32 = jnp.float32
BF16 = jnp.bfloat16
ANY = pl.BlockSpec(memory_space=pl.ANY)
SMEM = pl.BlockSpec(memory_space=pltpu.SMEM)
VMEM = pl.BlockSpec(memory_space=pltpu.VMEM)


def frequencies():
    steps = jnp.arange(HEAD_DIM // 2, dtype=F32) * 2.0 / HEAD_DIM
    return ROPE_BASE ** (-steps)


def after(value, *earlier):
    return lax.optimization_barrier((value, *earlier))[0]


class Links:
    def __init__(self, sizes):
        self.sizes = sizes

    def index(self, s, c, f):
        return (s * self.sizes[1] + c) * self.sizes[2] + f

    def swap(self, value, ds=0, dc=0, df=0, only=None):
        n_s, n_c, n_f = self.sizes
        pairs = [
            (self.index(s, c, f), self.index(s ^ ds, c ^ dc, f ^ df))
            for s in range(n_s)
            for c in range(n_c)
            for f in range(n_f)
            if only is None or only(s, f)
        ]
        return lax.ppermute(value, AXES, pairs)

    def later(self, value, blocks, sign):
        n_s, n_c, n_f = self.sizes
        pairs = []
        for s in range(n_s):
            for c in range(n_c - blocks):
                for f in range(n_f):
                    pair = (self.index(s, c, f), self.index(s, c + blocks, f))
                    pairs.append(pair if sign > 0 else pair[::-1])
        return lax.ppermute(value, AXES, pairs)

    def core(self, value):
        return self.swap(value, ds=1)

    def plane(self, value, bits):
        return self.swap(value, ds=bits & 2, dc=bits & 1)

    def gather_plane(self, own, first=None):
        if first is None:
            return [own] + [self.plane(own, bits) for bits in (1, 2, 3)]
        second = 3 - first
        pieces = [own, None, None, None]
        pieces[first] = self.plane(own, first)
        pieces[second] = self.plane(own, second)
        pieces[3] = self.plane(pieces[first], second)
        return pieces

    def gather_z(self, own):
        return jnp.stack([self.swap(own, df=bits) for bits in (1, 2, 3)])

    def reduce_plane(self, pieces, first):
        second = 3 - first
        far = self.plane(pieces[3], first)
        near = self.plane(pieces[first], first)
        forward = (pieces[second].astype(F32) + far.astype(F32)).astype(BF16)
        last = self.plane(forward, second)
        total = pieces[0].astype(F32) + near.astype(F32) + last.astype(F32)
        total = total.astype(BF16)
        step = 2
        while step < self.sizes[1]:
            total = (total.astype(F32) + self.swap(total, dc=step).astype(F32)).astype(BF16)
            step *= 2
        return total

    def reduce_z(self, total):
        arrived = [self.swap(total[bits], df=bits) for bits in (1, 2, 3)]
        result = total[0].astype(F32)
        for value in arrived:
            result = result + value.astype(F32)
        return result.astype(BF16)


NT = (((1,), (1,)), ((), ()))
TN = (((0,), (0,)), ((), ()))


def mlp_kernel(
    first,
    last,
    start_col,
    place,
    x_own,
    x_oth,
    dy_own,
    dy_oth,
    gate_up_own,
    u0,
    u1,
    u2,
    u3,
    d0,
    d1,
    d2,
    d3,
    *rest,
):
    if first:
        carried = None
    else:
        carried, rest = rest[:4], rest[4:]
    out_own, out_oth, dn_own, dn_oth = rest[:4]
    gu_out = rest[4:8]
    gd_out = rest[8:12]
    up_w, down_w, act, dgu, gu, gd, x, dy, acc_out, acc_dn, sem = rest[12:]
    width = act.shape[1]
    p, k, f = place[0], place[1], place[2]

    copies = []
    for half, (xs, ds) in enumerate(((x_own, dy_own), (x_oth, dy_oth))):
        rows = pl.ds(half * TOK_DEV, TOK_DEV)
        copies.append(pltpu.make_async_copy(xs, x.at[rows], sem))
        copies.append(pltpu.make_async_copy(ds, dy.at[rows], sem))
    for pp in range(4):
        col = pl.multiple_of((pp // 2) * FF + k * FF_HALF + (pp % 2) * FF_SHARD + start_col, 128)
        copies.append(
            pltpu.make_async_copy(gate_up_own.at[:, pl.ds(col, width)], up_w.at[pp, f], sem)
        )
    for q, ref in enumerate((u0, u1, u2, u3)):
        for r in range(3):
            copies.append(
                pltpu.make_async_copy(
                    ref.at[r], up_w.at[jnp.bitwise_xor(p, q), jnp.bitwise_xor(f, r + 1)], sem
                )
            )
    for q, ref in enumerate((d0, d1, d2, d3)):
        for t in range(2):
            block = jnp.bitwise_xor(jnp.bitwise_and(f, 1), t)
            copies.append(
                pltpu.make_async_copy(ref.at[t], down_w.at[block, jnp.bitwise_xor(p, q)], sem)
            )
    if not first:
        for half in range(2):
            rows = pl.ds(half * TOK_DEV, TOK_DEV)
            copies.append(pltpu.make_async_copy(carried[half], acc_out.at[rows], sem))
            copies.append(pltpu.make_async_copy(carried[2 + half], acc_dn.at[rows], sem))
    for copy in copies:
        copy.start()
    for copy in copies:
        copy.wait()

    for block in range(2):
        gate_w = up_w[block].reshape(D, width)
        lift_w = up_w[2 + block].reshape(D, width)
        drop_w = down_w[block].reshape(width, D)

        @pl.loop(0, 2 * TOK_DEV // ROW_TILE)
        def tile(t):
            rows = pl.ds(pl.multiple_of(t * ROW_TILE, ROW_TILE), ROW_TILE)
            g = jnp.dot(x[rows, :], gate_w, preferred_element_type=F32)
            u = jnp.dot(x[rows, :], lift_w, preferred_element_type=F32)
            da = lax.dot_general(dy[rows, :], drop_w, NT, preferred_element_type=F32)
            sig = jax.nn.sigmoid(g)
            silu = g * sig
            a = (silu * u).astype(BF16)
            dg = (da * u * sig * (1.0 + g * (1.0 - sig))).astype(BF16)
            du = (da * silu).astype(BF16)
            act[rows, :] = a
            dgu[rows, :width] = dg
            dgu[rows, width:] = du
            out = jnp.dot(a, drop_w, preferred_element_type=F32)
            dn = lax.dot_general(dg, gate_w, NT, preferred_element_type=F32)
            dn = dn + lax.dot_general(du, lift_w, NT, preferred_element_type=F32)
            if first and block == 0:
                acc_out[rows, :] = out
                acc_dn[rows, :] = dn
            else:
                acc_out[rows, :] += out
                acc_dn[rows, :] += dn

        grad = lax.dot_general(x[...], dgu[...], TN, preferred_element_type=F32).astype(BF16)
        gu[block] = grad[:, :width].reshape(4, ROWS, width)
        gu[2 + block] = grad[:, width:].reshape(4, ROWS, width)
        grad = lax.dot_general(act[...], dy[...], TN, preferred_element_type=F32).astype(BF16)
        gd[block] = grad.reshape(4, width // 4, D)

    copies = []
    for q, ref in enumerate(gu_out):
        for r in range(4):
            copies.append(
                pltpu.make_async_copy(
                    gu.at[jnp.bitwise_xor(p, q), jnp.bitwise_xor(f, r)], ref.at[r], sem
                )
            )
    for q, ref in enumerate(gd_out):
        for t in range(2):
            block = jnp.bitwise_xor(jnp.bitwise_and(f, 1), t)
            copies.append(
                pltpu.make_async_copy(gd.at[block, jnp.bitwise_xor(p, q)], ref.at[t], sem)
            )
    for copy in copies:
        copy.start()
    out_own[...] = acc_out[:TOK_DEV, :]
    dn_own[...] = acc_dn[:TOK_DEV, :]
    out_oth[...] = acc_out[TOK_DEV:, :].astype(out_oth.dtype)
    dn_oth[...] = acc_dn[TOK_DEV:, :].astype(dn_oth.dtype)
    for copy in copies:
        copy.wait()


def mlp_chunk(place, chunk, tokens, weights, carried):
    start_col, width = CHUNKS[chunk]
    last = chunk == len(CHUNKS) - 1
    first = chunk == 0
    x_own, x_oth, dy_own, dy_oth = tokens
    gate_up_own, up_pieces, down_pieces = weights
    side = jax.ShapeDtypeStruct((TOK_DEV, D), BF16 if last else F32)
    main = jax.ShapeDtypeStruct((TOK_DEV, D), F32)
    part = jax.ShapeDtypeStruct((4, ROWS, width), BF16)
    down = jax.ShapeDtypeStruct((2, width // 4, D), BF16)
    operands = [place, x_own, x_oth, dy_own, dy_oth, gate_up_own, *up_pieces, *down_pieces]
    if not first:
        operands += list(carried)
    flops = 2 * 2 * TOK_DEV * D * 2 * width * 9
    out = pl.pallas_call(
        functools.partial(mlp_kernel, first, last, start_col),
        out_shape=[main, side, main, side] + [part] * 4 + [down] * 4,
        in_specs=[SMEM] + [ANY] * (len(operands) - 1),
        out_specs=[VMEM] * 4 + [ANY] * 8,
        scratch_shapes=[
            pltpu.VMEM((4, 4, ROWS, width), BF16),
            pltpu.VMEM((2, 4, width // 4, D), BF16),
            pltpu.VMEM((2 * TOK_DEV, width), BF16),
            pltpu.VMEM((2 * TOK_DEV, 2 * width), BF16),
            pltpu.VMEM((4, 4, ROWS, width), BF16),
            pltpu.VMEM((2, 4, width // 4, D), BF16),
            pltpu.VMEM((2 * TOK_DEV, D), BF16),
            pltpu.VMEM((2 * TOK_DEV, D), BF16),
            pltpu.VMEM((2 * TOK_DEV, D), F32),
            pltpu.VMEM((2 * TOK_DEV, D), F32),
            pltpu.SemaphoreType.DMA(()),
        ],
        compiler_params=pltpu.CompilerParams(vmem_limit_bytes=VMEM_LIMIT),
        cost_estimate=pl.CostEstimate(
            flops=flops, bytes_accessed=20_000_000, transcendentals=4 * TOK_DEV * width
        ),
    )(*operands)
    return out[:4], out[4:8], out[8:12]


def finish_up_kernel(place, *refs):
    full = refs[-1]
    p, k = place[0], place[1]
    position = 0
    for start_col, width in CHUNKS:
        for other in range(2):
            kk = jnp.bitwise_xor(k, other)
            for q in range(4):
                pp = jnp.bitwise_xor(p, q)
                col = (
                    jnp.right_shift(pp, 1) * FF
                    + kk * FF_HALF
                    + jnp.bitwise_and(pp, 1) * FF_SHARD
                    + start_col
                )
                full[:, pl.ds(pl.multiple_of(col, 128), width)] = refs[position][...].astype(F32)
                position += 1


def finish_up(place, pieces):
    return pl.pallas_call(
        finish_up_kernel,
        out_shape=jax.ShapeDtypeStruct((ROWS, 2 * FF), F32),
        in_specs=[SMEM] + [VMEM] * len(pieces),
        out_specs=VMEM,
        compiler_params=pltpu.CompilerParams(vmem_limit_bytes=VMEM_LIMIT),
        cost_estimate=pl.CostEstimate(flops=0, bytes_accessed=12 * ROWS * FF, transcendentals=0),
    )(place, *pieces)


def finish_down_kernel(place, *refs):
    full = refs[-1]
    p, k = place[0], place[1]
    position = 0
    for start_col, width in CHUNKS:
        for other in range(2):
            kk = jnp.bitwise_xor(k, other)
            for q in range(4):
                pp = jnp.bitwise_xor(p, q)
                row = start_col + pp * (width // 4) + kk * (width // 8)
                full[pl.ds(pl.multiple_of(row, 16), width // 8), :] = refs[position][...].astype(F32)
                position += 1


def finish_down(place, pieces):
    return pl.pallas_call(
        finish_down_kernel,
        out_shape=jax.ShapeDtypeStruct((FF_SHARD, D), F32),
        in_specs=[SMEM] + [VMEM] * len(pieces),
        out_specs=VMEM,
        compiler_params=pltpu.CompilerParams(vmem_limit_bytes=VMEM_LIMIT),
        cost_estimate=pl.CostEstimate(flops=0, bytes_accessed=6 * FF_SHARD * D, transcendentals=0),
    )(place, *pieces)


def load_rows(place, own, mine, theirs, full, sem):
    p, k, f = place[0], place[1], place[2]
    for start in (True, False):

        def run(copy, start=start):
            if start:
                copy.start()
            else:
                copy.wait()

        run(pltpu.make_async_copy(own, full.at[f], sem))
        for other in range(2):
            kk = jnp.bitwise_xor(k, other)
            for q in range(4):
                ref = theirs.at[q] if other else mine[q]
                pp = jnp.bitwise_xor(p, q)
                row = pl.multiple_of(kk * 128 + pp * SLICE, 16)
                short = (kk * 4 + pp) == 7
                for r in range(3):
                    z = jnp.bitwise_xor(f, r + 1)

                    def go(count, ref=ref, r=r, z=z, row=row):
                        run(
                            pltpu.make_async_copy(
                                ref.at[r, pl.ds(0, count)], full.at[z, pl.ds(row, count)], sem
                            )
                        )

                    pl.when(short)(functools.partial(go, 16))
                    pl.when(jnp.logical_not(short))(functools.partial(go, SLICE))


def store_rows(place, grad, mine, theirs, sem):
    p, k, f = place[0], place[1], place[2]
    for start in (True, False):
        for other in range(2):
            kk = jnp.bitwise_xor(k, other)
            for q in range(4):
                ref = theirs.at[q] if other else mine[q]
                pp = jnp.bitwise_xor(p, q)
                row = pl.multiple_of(kk * 128 + pp * SLICE, 16)
                short = (kk * 4 + pp) == 7
                for r in range(4):
                    z = jnp.bitwise_xor(f, r)

                    def go(count, ref=ref, r=r, z=z, row=row):
                        copy = pltpu.make_async_copy(
                            grad.at[z, pl.ds(row, count)], ref.at[r, pl.ds(0, count)], sem
                        )
                        if start:
                            copy.start()
                        else:
                            copy.wait()

                    pl.when(short)(functools.partial(go, 16))
                    pl.when(jnp.logical_not(short))(functools.partial(go, SLICE))


def finish_rows_kernel(place, m0, m1, m2, m3, theirs, *outs):
    p, k = place[0], place[1]
    for other in range(2):
        kk = jnp.bitwise_xor(k, other)
        for q, ref in enumerate((m0, m1, m2, m3)):
            value = (theirs[q] if other else ref[...]).astype(F32)
            pp = jnp.bitwise_xor(p, q)
            row = pl.multiple_of(kk * 128 + pp * SLICE, 16)
            short = (kk * 4 + pp) == 7

            def go(count, value=value, row=row):
                at = 0
                for out in outs:
                    wide = out.shape[1]
                    out[pl.ds(row, count), :] = value[:count, at : at + wide]
                    at += wide

            pl.when(short)(functools.partial(go, 16))
            pl.when(jnp.logical_not(short))(functools.partial(go, SLICE))


def finish_rows(place, mine, theirs, widths):
    return pl.pallas_call(
        finish_rows_kernel,
        out_shape=[jax.ShapeDtypeStruct((ROWS, width), F32) for width in widths],
        in_specs=[SMEM] + [VMEM] * 5,
        out_specs=[VMEM] * len(widths),
        compiler_params=pltpu.CompilerParams(vmem_limit_bytes=VMEM_LIMIT),
        cost_estimate=pl.CostEstimate(
            flops=0, bytes_accessed=6 * ROWS * sum(widths), transcendentals=0
        ),
    )(place, *mine, theirs)


def row_scale(values):
    return lax.rsqrt(jnp.mean(values * values, axis=-1, keepdims=True) + EPSILON)


def project_kernel(
    place, x, gain, cosines, sines, own, m0, m1, m2, m3, theirs, full, normed_t, q_t, kv, sem
):
    source = x[...].astype(F32)
    normed = source * row_scale(source) * gain[...]
    normed_t[...] = normed.T.astype(BF16)
    load_rows(place, own, (m0, m1, m2, m3), theirs, full, sem)
    weight = full[...].reshape(D, QKV)
    mixed = lax.dot_general(weight, normed_t[...], TN, preferred_element_type=F32)
    cos, sin = cosines[...], sines[...]
    half = HEAD_DIM // 2
    for head in range(HEADS + KV_HEADS):
        row = head * HEAD_DIM
        low, high = mixed[row : row + half], mixed[row + half : row + HEAD_DIM]
        low, high = (low * cos - high * sin).astype(BF16), (high * cos + low * sin).astype(BF16)
        if head < HEADS:
            q_t[row : row + half, :] = low
            q_t[row + half : row + HEAD_DIM, :] = high
        else:
            row -= D
            for block in range(TOK_DEV // BLK):
                lanes = slice(block * BLK, (block + 1) * BLK)
                kv[block, row : row + half, :] = low[:, lanes]
                kv[block, row + half : row + HEAD_DIM, :] = high[:, lanes]
    for block in range(TOK_DEV // BLK):
        lanes = slice(block * BLK, (block + 1) * BLK)
        kv[block, KV_DIM:, :] = mixed[D + KV_DIM :, lanes].astype(BF16)


def project(place, x, gain, cosines, sines, own, mine, theirs):
    return pl.pallas_call(
        project_kernel,
        out_shape=[
            jax.ShapeDtypeStruct((4, ROWS, QKV), BF16),
            jax.ShapeDtypeStruct((D, TOK_DEV), BF16),
            jax.ShapeDtypeStruct((D, TOK_DEV), BF16),
            jax.ShapeDtypeStruct((TOK_DEV // BLK, 2 * KV_DIM, BLK), BF16),
        ],
        in_specs=[SMEM] + [VMEM] * 4 + [ANY] * 6,
        out_specs=[VMEM] * 4,
        scratch_shapes=[pltpu.SemaphoreType.DMA(())],
        compiler_params=pltpu.CompilerParams(vmem_limit_bytes=VMEM_LIMIT),
        cost_estimate=pl.CostEstimate(
            flops=2 * TOK_DEV * D * QKV, bytes_accessed=10_000_000, transcendentals=0
        ),
    )(place, x, gain, cosines, sines, own, *mine, theirs)


def three_heads(ref, group, lanes):
    first = group * (HEADS // KV_HEADS) * HEAD_DIM
    return jnp.concatenate(
        [
            ref[first + r * HEAD_DIM : first + (r + 1) * HEAD_DIM, lanes]
            for r in range(HEADS // KV_HEADS)
        ],
        axis=1,
    )


def diagonal_mask():
    shape = (BLK, BLK * (HEADS // KV_HEADS))
    keys = lax.broadcasted_iota(jnp.int32, shape, 0)
    queries = jnp.bitwise_and(lax.broadcasted_iota(jnp.int32, shape, 1), BLK - 1)
    return keys <= queries


def attend_kernel(lows, q_t, *rest):
    spans = rest[:-6]
    attn_t, log_total, kv, best, total, accum = rest[-6:]
    blocks = TOK_DEV // BLK
    for at, ref in enumerate(spans):
        kv[at * blocks : (at + 1) * blocks] = ref[...]
    own_at = (len(spans) - 1) * blocks
    mask = diagonal_mask()
    for i in range(blocks):
        lanes = slice(i * BLK, (i + 1) * BLK)
        queries = [
            three_heads(q_t, group, lanes) * jnp.asarray(HEAD_DIM**-0.5, BF16)
            for group in range(KV_HEADS)
        ]

        def step(j, diagonal, queries=queries):
            for group in range(KV_HEADS):
                keys = kv[j, group * HEAD_DIM : (group + 1) * HEAD_DIM, :]
                values = kv[j, KV_DIM + group * HEAD_DIM : KV_DIM + (group + 1) * HEAD_DIM, :]
                scores = lax.dot_general(keys, queries[group], TN, preferred_element_type=F32)
                if diagonal:
                    scores = jnp.where(mask, scores, MASKED_SCORE)
                    top = jnp.max(scores, axis=0, keepdims=True)
                    expo = jnp.exp(scores - top)
                    total[group] = jnp.sum(expo, axis=0, keepdims=True)
                    accum[group] = jnp.dot(values, expo.astype(BF16), preferred_element_type=F32)
                else:
                    old = best[group]
                    top = jnp.maximum(old, jnp.max(scores, axis=0, keepdims=True))
                    decay = jnp.exp(old - top)
                    expo = jnp.exp(scores - top)
                    total[group] = total[group] * decay + jnp.sum(expo, axis=0, keepdims=True)
                    accum[group] = accum[group] * decay + jnp.dot(
                        values, expo.astype(BF16), preferred_element_type=F32
                    )
                best[group] = top

        step(own_at + i, True)

        @pl.loop(lows[i], own_at + i)
        def earlier(j):
            step(j, False)

        for group in range(KV_HEADS):
            attn = (accum[group] / total[group]).astype(BF16)
            first = group * (HEADS // KV_HEADS) * HEAD_DIM
            for r in range(HEADS // KV_HEADS):
                attn_t[first + r * HEAD_DIM : first + (r + 1) * HEAD_DIM, lanes] = attn[
                    :, r * BLK : (r + 1) * BLK
                ]
            log_total[i * KV_HEADS + group] = best[group] + jnp.log(total[group])


def attend(lows, q_t, spans):
    blocks = TOK_DEV // BLK
    wide = BLK * (HEADS // KV_HEADS)
    return pl.pallas_call(
        attend_kernel,
        out_shape=[
            jax.ShapeDtypeStruct((D, TOK_DEV), BF16),
            jax.ShapeDtypeStruct((blocks * KV_HEADS, 1, wide), F32),
        ],
        in_specs=[SMEM] + [VMEM] * (1 + len(spans)),
        out_specs=[VMEM] * 2,
        scratch_shapes=[
            pltpu.VMEM((len(spans) * blocks, 2 * KV_DIM, BLK), BF16),
            pltpu.VMEM((KV_HEADS, 1, wide), F32),
            pltpu.VMEM((KV_HEADS, 1, wide), F32),
            pltpu.VMEM((KV_HEADS, HEAD_DIM, wide), F32),
        ],
        compiler_params=pltpu.CompilerParams(vmem_limit_bytes=VMEM_LIMIT),
        cost_estimate=pl.CostEstimate(
            flops=8_000_000_000, bytes_accessed=4_000_000, transcendentals=2_000_000
        ),
    )(lows, q_t, *spans)


def out_kernel(place, x, gain, attn_t, own, m0, m1, m2, m3, theirs, full, hidden, normed, sem):
    load_rows(place, own, (m0, m1, m2, m3), theirs, full, sem)
    weight = full[...].reshape(D, D)
    value = x[...].astype(F32) + lax.dot_general(
        attn_t[...], weight, TN, preferred_element_type=F32
    )
    hidden[...] = value
    normed[...] = (value * row_scale(value) * gain[...]).astype(BF16)


def project_out(place, x, gain, attn_t, own, mine, theirs):
    return pl.pallas_call(
        out_kernel,
        out_shape=[
            jax.ShapeDtypeStruct((4, ROWS, D), BF16),
            jax.ShapeDtypeStruct((TOK_DEV, D), F32),
            jax.ShapeDtypeStruct((TOK_DEV, D), BF16),
        ],
        in_specs=[SMEM] + [VMEM] * 3 + [ANY] * 6,
        out_specs=[VMEM] * 3,
        scratch_shapes=[pltpu.SemaphoreType.DMA(())],
        compiler_params=pltpu.CompilerParams(vmem_limit_bytes=VMEM_LIMIT),
        cost_estimate=pl.CostEstimate(
            flops=2 * TOK_DEV * D * D, bytes_accessed=8_000_000, transcendentals=0
        ),
    )(place, x, gain, attn_t, own, *mine, theirs)


def middle_kernel(
    place, hidden, dy, gain, dn_own, dn_oth, attn_t, full, d_hidden, d_attn_t, grad_gain, *rest
):
    mine, theirs, grad, sem = rest[:4], rest[4], rest[5], rest[6]
    value = hidden[...]
    scale = row_scale(value)
    unit = value * scale
    dn = dn_own[...] + dn_oth[...].astype(F32)
    grad_gain[...] = jnp.sum(dn * unit, axis=0, keepdims=True)
    weighted = dn * gain[...]
    dh = dy[...].astype(F32) + scale * (
        weighted - unit * jnp.mean(weighted * unit, axis=-1, keepdims=True)
    )
    d_hidden[...] = dh
    dh = dh.astype(BF16)
    d_attn_t[...] = lax.dot_general(
        full[...].reshape(D, D), dh, NT, preferred_element_type=F32
    ).astype(BF16)
    grad[...] = (
        jnp.dot(attn_t[...], dh, preferred_element_type=F32).astype(BF16).reshape(4, ROWS, D)
    )
    store_rows(place, grad, mine, theirs, sem)


def middle(place, hidden, dy, gain, dn_own, dn_oth, attn_t, full):
    piece = jax.ShapeDtypeStruct((4, SLICE, D), BF16)
    out = pl.pallas_call(
        middle_kernel,
        out_shape=[
            jax.ShapeDtypeStruct((TOK_DEV, D), F32),
            jax.ShapeDtypeStruct((D, TOK_DEV), BF16),
            jax.ShapeDtypeStruct((1, D), F32),
            *[piece] * 4,
            jax.ShapeDtypeStruct((4, 4, SLICE, D), BF16),
        ],
        in_specs=[SMEM] + [VMEM] * 7,
        out_specs=[VMEM] * 3 + [ANY] * 5,
        scratch_shapes=[pltpu.VMEM((4, ROWS, D), BF16), pltpu.SemaphoreType.DMA(())],
        compiler_params=pltpu.CompilerParams(vmem_limit_bytes=VMEM_LIMIT),
        cost_estimate=pl.CostEstimate(
            flops=4 * TOK_DEV * D * D, bytes_accessed=14_000_000, transcendentals=0
        ),
    )(place, hidden, dy, gain, dn_own, dn_oth, attn_t, full)
    return out[0], out[1], out[2], out[3:7], out[7]


def attend_back_kernel(count, lows, q_t, attn_t, d_attn_t, log_total, cosines, sines, *rest):
    spans, rest = rest[:count], rest[count:]
    dq_t, d_spans, (kv, d_kv, d_query) = rest[0], rest[1 : 1 + count], rest[1 + count :]
    blocks = TOK_DEV // BLK
    groups = HEADS // KV_HEADS
    half = HEAD_DIM // 2
    for at, ref in enumerate(spans):
        kv[at * blocks : (at + 1) * blocks] = ref[...]
    d_kv[...] = jnp.zeros_like(d_kv)
    own_at = (count - 1) * blocks
    mask = diagonal_mask()
    for i in range(blocks):
        lanes = slice(i * BLK, (i + 1) * BLK)
        queries, d_outs, deltas = [], [], []
        for group in range(KV_HEADS):
            queries.append(three_heads(q_t, group, lanes) * jnp.asarray(HEAD_DIM**-0.5, BF16))
            d_out = three_heads(d_attn_t, group, lanes)
            attn = three_heads(attn_t, group, lanes)
            d_outs.append(d_out)
            deltas.append(
                jnp.sum(d_out.astype(F32) * attn.astype(F32), axis=0, keepdims=True)
            )

        def step(j, diagonal, i=i, queries=queries, d_outs=d_outs, deltas=deltas):
            for group in range(KV_HEADS):
                key_rows = slice(group * HEAD_DIM, (group + 1) * HEAD_DIM)
                value_rows = slice(KV_DIM + group * HEAD_DIM, KV_DIM + (group + 1) * HEAD_DIM)
                keys, values = kv[j, key_rows, :], kv[j, value_rows, :]
                scores = lax.dot_general(keys, queries[group], TN, preferred_element_type=F32)
                if diagonal:
                    scores = jnp.where(mask, scores, MASKED_SCORE)
                prob = jnp.exp(scores - log_total[i * KV_HEADS + group])
                d_prob = lax.dot_general(values, d_outs[group], TN, preferred_element_type=F32)
                d_scores = (prob * (d_prob - deltas[group])).astype(BF16)
                d_kv[j, value_rows, :] += lax.dot_general(
                    d_outs[group], prob.astype(BF16), NT, preferred_element_type=F32
                )
                d_kv[j, key_rows, :] += lax.dot_general(
                    queries[group], d_scores, NT, preferred_element_type=F32
                )
                more = jnp.dot(keys, d_scores, preferred_element_type=F32)
                if diagonal:
                    d_query[group] = more
                else:
                    d_query[group] += more

        step(own_at + i, True)

        @pl.loop(lows[i], own_at + i)
        def earlier(j):
            step(j, False)

        cos, sin = cosines[:, lanes], sines[:, lanes]
        for group in range(KV_HEADS):
            for r in range(groups):
                row = (group * groups + r) * HEAD_DIM
                side = slice(r * BLK, (r + 1) * BLK)
                low = d_query[group, :half, side] * HEAD_DIM**-0.5
                high = d_query[group, half:, side] * HEAD_DIM**-0.5
                dq_t[row : row + half, lanes] = (low * cos + high * sin).astype(BF16)
                dq_t[row + half : row + HEAD_DIM, lanes] = (high * cos - low * sin).astype(BF16)
    for at, ref in enumerate(d_spans):
        ref[...] = d_kv[at * blocks : (at + 1) * blocks].astype(ref.dtype)


def attend_back(lows, q_t, attn_t, d_attn_t, log_total, cosines, sines, spans):
    blocks = TOK_DEV // BLK
    wide = BLK * (HEADS // KV_HEADS)
    count = len(spans)
    shape = (blocks, 2 * KV_DIM, BLK)
    out = pl.pallas_call(
        functools.partial(attend_back_kernel, count),
        out_shape=[jax.ShapeDtypeStruct((D, TOK_DEV), BF16)]
        + [jax.ShapeDtypeStruct(shape, BF16)] * (count - 1)
        + [jax.ShapeDtypeStruct(shape, F32)],
        in_specs=[SMEM] + [VMEM] * (6 + count),
        out_specs=[VMEM] * (1 + count),
        scratch_shapes=[
            pltpu.VMEM((count * blocks, 2 * KV_DIM, BLK), BF16),
            pltpu.VMEM((count * blocks, 2 * KV_DIM, BLK), F32),
            pltpu.VMEM((KV_HEADS, HEAD_DIM, wide), F32),
        ],
        compiler_params=pltpu.CompilerParams(vmem_limit_bytes=VMEM_LIMIT),
        cost_estimate=pl.CostEstimate(
            flops=16_000_000_000, bytes_accessed=8_000_000, transcendentals=2_000_000
        ),
    )(lows, q_t, attn_t, d_attn_t, log_total, cosines, sines, *spans)
    return out[0], out[1:]


def last_kernel(
    count, place, x, gain, normed_t, dq_t, cosines, sines, full, d_hidden, gain_mlp_grad, d_own, *rest
):
    arrived, rest = rest[:count], rest[count:]
    input_grad, mine, theirs, d_mixed, grad, sem = rest[0], rest[1:5], rest[5], *rest[6:]
    half = HEAD_DIM // 2
    d_mixed[:D, :] = dq_t[...]
    for block in range(TOK_DEV // BLK):
        lanes = slice(block * BLK, (block + 1) * BLK)
        value = d_own[block]
        for ref in arrived:
            value = value + ref[block].astype(F32)
        cos, sin = cosines[:, lanes], sines[:, lanes]
        for head in range(KV_HEADS):
            row = head * HEAD_DIM
            low, high = value[row : row + half], value[row + half : row + HEAD_DIM]
            d_mixed[D + row : D + row + half, lanes] = (low * cos + high * sin).astype(BF16)
            d_mixed[D + row + half : D + row + HEAD_DIM, lanes] = (high * cos - low * sin).astype(
                BF16
            )
        d_mixed[D + KV_DIM :, lanes] = value[KV_DIM:].astype(BF16)
    dn = jnp.dot(full[...].reshape(D, QKV), d_mixed[...], preferred_element_type=F32).T
    source = x[...].astype(F32)
    scale = row_scale(source)
    unit = source * scale
    gain_grad = jnp.sum(dn * unit, axis=0, keepdims=True)
    weighted = dn * gain[...]
    input_grad[...] = (
        d_hidden[...]
        + scale * (weighted - unit * jnp.mean(weighted * unit, axis=-1, keepdims=True))
    ).astype(BF16)
    product = lax.dot_general(normed_t[...], d_mixed[...], NT, preferred_element_type=F32)
    grad[:, :, :QKV] = product.astype(BF16).reshape(4, ROWS, QKV)
    index = lax.broadcasted_iota(jnp.int32, (128, D), 0)
    pair = jnp.where(index == 0, gain_grad, jnp.where(index == 1, gain_mlp_grad[...], 0.0))
    grad[:, :, QKV:] = pair.T[:, : QKV_WIDE - QKV].astype(BF16).reshape(4, ROWS, QKV_WIDE - QKV)
    store_rows(place, grad, mine, theirs, sem)


def last(place, x, gain, normed_t, dq_t, cosines, sines, full, d_hidden, gain_mlp_grad, d_own, arrived):
    piece = jax.ShapeDtypeStruct((4, SLICE, QKV_WIDE), BF16)
    out = pl.pallas_call(
        functools.partial(last_kernel, len(arrived)),
        out_shape=[
            jax.ShapeDtypeStruct((TOK_DEV, D), BF16),
            *[piece] * 4,
            jax.ShapeDtypeStruct((4, 4, SLICE, QKV_WIDE), BF16),
        ],
        in_specs=[SMEM] + [VMEM] * (10 + len(arrived)),
        out_specs=[VMEM] + [ANY] * 5,
        scratch_shapes=[
            pltpu.VMEM((QKV, TOK_DEV), BF16),
            pltpu.VMEM((4, ROWS, QKV_WIDE), BF16),
            pltpu.SemaphoreType.DMA(()),
        ],
        compiler_params=pltpu.CompilerParams(vmem_limit_bytes=VMEM_LIMIT),
        cost_estimate=pl.CostEstimate(
            flops=4 * TOK_DEV * D * QKV, bytes_accessed=14_000_000, transcendentals=0
        ),
    )(place, x, gain, normed_t, dq_t, cosines, sines, full, d_hidden, gain_mlp_grad, d_own, *arrived)
    return out[0], out[1:5], out[5]


def native(s, f):
    return (f >> 1) == (s & 1)


def foreign(s, f):
    return not native(s, f)


def shards(
    links,
    tokens,
    cotangent,
    positions,
    doc_ids,
    gain_attn,
    w_qkv,
    w_out,
    gain_mlp,
    w_gate_up,
    w_down,
):
    seq_at, ctx_at, f = (lax.axis_index(name) for name in AXES)
    k = jnp.bitwise_and(seq_at, 1)
    p = 2 * jnp.right_shift(seq_at, 1) + jnp.bitwise_and(ctx_at, 1)
    place = jnp.stack([p, k, f]).astype(jnp.int32)
    is_native = jnp.right_shift(f, 1) == k

    def row_slice(weight):
        padded = jnp.pad(weight, ((0, ROWS_PAD - ROWS), (0, 0)))
        return lax.dynamic_slice_in_dim(padded, k * 128 + p * SLICE, SLICE, 0)

    def gather_rows(weight, *earlier):
        return links.gather_z(after(row_slice(weight), *earlier))

    gains = jnp.stack([gain_attn, gain_mlp])
    gain_pieces = [gains] + [links.swap(gains, df=bits) for bits in (1, 2, 3)]
    gain_rows = jnp.stack(gain_pieces)
    gain_rows = jnp.stack(
        [lax.dynamic_index_in_dim(gain_rows, jnp.bitwise_xor(f, z), 0, False) for z in range(4)]
    )
    gain_one = gain_rows[:, 0].reshape(1, D).astype(F32)
    gain_two = gain_rows[:, 1].reshape(1, D).astype(F32)
    angles = frequencies()[:, None] * positions[0].astype(F32)[None, :]
    cosines, sines = jnp.cos(angles), jnp.sin(angles)
    blocks = TOK_DEV // BLK
    docs = doc_ids[0]
    own_docs = lax.dynamic_slice_in_dim(docs, ctx_at * blocks, blocks)
    lows = jnp.sum((docs[None, :] < own_docs[:, None]).astype(jnp.int32), axis=1)
    lows = lows + (links.sizes[1] - 1 - ctx_at) * blocks

    dy_own = cotangent[0]
    qkv_z = gather_rows(w_qkv)
    out_z = gather_rows(w_out, qkv_z)
    qkv_mine = links.gather_plane(qkv_z)
    qkv_theirs = links.core(jnp.stack(qkv_mine))
    out_mine = links.gather_plane(after(out_z, *qkv_mine))
    out_theirs = links.core(jnp.stack(out_mine))
    dy_oth = links.core(dy_own)

    chunk_weights = []
    before_z = (out_z,)
    before_plane = tuple(out_mine)
    for chunk, (start_col, width) in enumerate(CHUNKS):
        col = (
            jnp.right_shift(p, 1) * FF
            + k * FF_HALF
            + jnp.bitwise_and(p, 1) * FF_SHARD
            + start_col
        )
        up_own = after(lax.dynamic_slice_in_dim(w_gate_up, col, width, 1), *before_z)
        up_z = links.gather_z(up_own)
        short = width // 4
        down_own = lax.dynamic_slice_in_dim(w_down, start_col + p * short, short, 0)
        down_own = after(down_own, *before_z)
        down_1 = links.swap(down_own, df=1, only=native)
        down_2 = links.swap(down_own, ds=1, df=2, only=foreign)
        down_3 = links.swap(down_own, ds=1, df=3, only=foreign)
        down_z = jnp.stack(
            [jnp.where(is_native, down_own, down_2), jnp.where(is_native, down_1, down_3)]
        )
        before_z = (up_z, down_z)
        up_z = after(up_z, *before_plane)
        down_z = after(down_z, *before_plane)
        first = 1 if chunk % 2 == 0 else 2
        up_pieces = links.gather_plane(up_z, first)
        down_pieces = links.gather_plane(down_z, first)
        before_plane = tuple(up_pieces + down_pieces)
        chunk_weights.append((w_gate_up, up_pieces, down_pieces))

    x_in = tokens[0]
    qkv_full, normed_t, q_t, kv = project(
        place, x_in, gain_one, cosines, sines, w_qkv, qkv_mine, qkv_theirs
    )
    n_ctx = links.sizes[1]
    spans = [links.later(kv, d, 1) for d in range(n_ctx - 1, 0, -1)] + [kv]
    attn_t, log_total = attend(lows, q_t, spans)
    out_full, hidden, normed_mlp = project_out(
        place, x_in, gain_two, attn_t, w_out, out_mine, out_theirs
    )

    x_oth = links.core(normed_mlp)
    mlp_tokens = (normed_mlp, x_oth, dy_own, dy_oth)
    carried = None
    up_done, down_done = [], []
    for chunk, (start_col, width) in enumerate(CHUNKS):
        carried, up_grads, down_grads = mlp_chunk(
            place, chunk, mlp_tokens, chunk_weights[chunk], carried
        )
        first = 1 if chunk % 2 == 0 else 2
        down_sum = links.reduce_plane(down_grads, first)
        arrived_1 = links.swap(down_sum[1], df=1, only=native)
        arrived_2 = links.swap(down_sum[0], ds=1, df=2, only=foreign)
        arrived_3 = links.swap(down_sum[1], ds=1, df=3, only=foreign)
        down_sum = jnp.where(is_native, down_sum[0], arrived_2).astype(F32) + jnp.where(
            is_native, arrived_1, arrived_3
        ).astype(F32)
        down_sum = down_sum.astype(BF16)
        part = width // 8
        halves = down_sum.reshape(2, part, D)
        keep = lax.dynamic_index_in_dim(halves, k, 0, False)
        give = lax.dynamic_index_in_dim(halves, 1 - k, 0, False)
        down_part = (keep.astype(F32) + links.core(give).astype(F32)).astype(BF16)
        pieces = links.gather_plane(down_part, 3 - first)
        down_done += pieces + [links.core(piece) for piece in pieces]
        up_sum = links.reduce_z(links.reduce_plane(up_grads, first))
        pieces = links.gather_plane(up_sum, 3 - first)
        up_done += pieces + [links.core(piece) for piece in pieces]
    grad_gate_up = finish_up(place, up_done)
    grad_down = finish_down(place, down_done)
    out_own, out_oth, dn_own, dn_oth = carried
    result = hidden + out_own + links.core(out_oth).astype(F32)
    output = result.astype(jnp.bfloat16)[None]

    d_hidden, d_attn_t, gain_mlp_grad, out_mine, out_theirs = middle(
        place, hidden, dy_own, gain_two, dn_own, links.core(dn_oth), attn_t, out_full
    )

    def reduce_rows(mine, theirs, first, widths):
        arrived = links.core(theirs)
        mine = [(a.astype(F32) + arrived[q].astype(F32)).astype(BF16) for q, a in enumerate(mine)]
        total = links.reduce_z(links.reduce_plane(mine, first))
        pieces = links.gather_plane(total, 3 - first)
        return finish_rows(place, pieces, links.core(jnp.stack(pieces)), widths)

    (grad_out,) = reduce_rows(out_mine, out_theirs, 1, (D,))
    dq_t, d_spans = attend_back(
        lows, q_t, attn_t, d_attn_t, log_total, cosines, sines, spans
    )
    arrived = [
        links.later(value, d, -1) for value, d in zip(d_spans, range(n_ctx - 1, 0, -1))
    ]
    input_grad, qkv_mine, qkv_theirs = last(
        place,
        x_in,
        gain_one,
        normed_t,
        dq_t,
        cosines,
        sines,
        qkv_full,
        d_hidden,
        gain_mlp_grad,
        d_spans[-1],
        arrived,
    )
    grad_qkv, gain_columns = reduce_rows(qkv_mine, qkv_theirs, 2, (QKV, QKV_WIDE - QKV))
    return (
        output,
        input_grad[None],
        gain_columns[:, 0],
        grad_qkv,
        grad_out,
        gain_columns[:, 1],
        grad_gate_up,
        grad_down,
    )


def solution(mesh):
    placed = (
        P(("seq", "fsdp"), "ctx", None),
        P(("seq", "fsdp"), "ctx", None),
        P(("seq", "fsdp"), "ctx"),
        P(("seq", "fsdp"), None),
        P("fsdp"),
        P("fsdp", None),
        P("fsdp", None),
        P("fsdp"),
        P("fsdp", None),
        P("fsdp", None),
    )
    links = Links([mesh.shape[name] for name in AXES])
    return jax.shard_map(
        functools.partial(shards, links),
        mesh=mesh,
        in_specs=placed,
        out_specs=(
            P(("seq", "fsdp"), "ctx", None),
            P(("seq", "fsdp"), "ctx", None),
            P("fsdp"),
            P("fsdp", None),
            P("fsdp", None),
            P("fsdp"),
            P("fsdp", None),
            P("fsdp", None),
        ),
        check_vma=False,
    )
```

```python
import functools

import jax
import jax.numpy as jnp
from jax import lax
from jax.experimental import pallas as pl
from jax.experimental.pallas import tpu as pltpu
from jax.sharding import PartitionSpec as P

D = 960
HEADS = 15
KV_HEADS = 5
HEAD_DIM = 64
FF = 2560
BLK = 128
TOK_DEV = 512
KV_DIM = 320
QKV = D + 2 * KV_DIM
QKV_WIDE = 1664
FF_SHARD = FF // 4
ROWS = D // 4
ROWS_PAD = 256
SLICE = 32
TILE = 128
HALF = 64
ROW_TILE = 256
VMEM_LIMIT = 56 * 1024 * 1024

EPSILON = 1e-05
ROPE_BASE = 100000.0
MASKED_SCORE = -1e30
AXES = ("seq", "ctx", "fsdp")
F32 = jnp.float32
BF16 = jnp.bfloat16
ANY = pl.BlockSpec(memory_space=pl.ANY)
SMEM = pl.BlockSpec(memory_space=pltpu.SMEM)
VMEM = pl.BlockSpec(memory_space=pltpu.VMEM)
NT = (((1,), (1,)), ((), ()))
TN = (((0,), (0,)), ((), ()))


def frequencies():
    steps = jnp.arange(HEAD_DIM // 2, dtype=F32) * 2.0 / HEAD_DIM
    return ROPE_BASE ** (-steps)


def after(value, *earlier):
    return lax.optimization_barrier((value, *earlier))[0]


def gate(values, *earlier):
    return lax.optimization_barrier((*values, *earlier))[: len(values)]


def add(first, second):
    return (first.astype(F32) + second.astype(F32)).astype(BF16)


def sum_one(keep, arrived):
    pairs = list(zip(keep, arrived))
    stay = [value[0].astype(F32) + more[0].astype(F32) for value, more in pairs]
    return stay, [add(value[1], more[1]) for value, more in pairs]


def sum_z1(left, arrived):
    return add(left[: left.shape[0] // 2], arrived)


class Links:
    def __init__(self, sizes):
        self.sizes = sizes

    def index(self, s, c, f):
        return (s * self.sizes[1] + c) * self.sizes[2] + f

    def swap(self, value, ds=0, dc=0, df=0):
        n_s, n_c, n_f = self.sizes
        pairs = [
            (self.index(s, c, f), self.index(s ^ ds, c ^ dc, f ^ df))
            for s in range(n_s)
            for c in range(n_c)
            for f in range(n_f)
        ]
        return lax.ppermute(value, AXES, pairs)

    def later(self, value, blocks, sign):
        n_s, n_c, n_f = self.sizes
        pairs = []
        for s in range(n_s):
            for c in range(n_c - blocks):
                for f in range(n_f):
                    pair = (self.index(s, c, f), self.index(s, c + blocks, f))
                    pairs.append(pair if sign > 0 else pair[::-1])
        return lax.ppermute(value, AXES, pairs)

    def core(self, value):
        return self.swap(value, ds=1)

    def plane(self, value, bits):
        return self.swap(value, ds=bits & 2, dc=bits & 1)

    def gather_plane(self, own):
        return [own] + [self.plane(own, bits) for bits in (1, 2, 3)]

    def gather_z(self, own):
        return [self.swap(own, df=bits) for bits in (1, 2, 3)]

    def send_one(self, send):
        return [self.plane(value, bits) for value, bits in zip(send, (1, 2))]

    def send_two(self, move):
        return [self.plane(value, bits) for value, bits in zip(move, (2, 1))]

    def sum_two(self, stay, arrived):
        totals = [(value + more.astype(F32)).astype(BF16) for value, more in zip(stay, arrived)]
        step = 2
        while step < self.sizes[1]:
            totals = [add(value, self.swap(value, dc=step)) for value in totals]
            step *= 2
        return totals

    def send_z1(self, left):
        return self.swap(left[left.shape[0] // 2 :], df=1)

    def double_z(self, own, one):
        return self.swap(jnp.concatenate([own, one], axis=0), df=2)

    def gather_pairs(self, own, first):
        near = jnp.stack([own, self.plane(own, first)])
        far = self.plane(near, 3 - first)
        return near, far, self.core(near), self.core(far)


def piece_index(first, q):
    return (q & (3 - first)) // (3 - first), (q & first) // first


UNIT_TILES = (5, 3)
HIDDEN = (768, 512)
DOWN_AT = (3, 2)


def mlp_kernel(chunk, place, x_own, x_oth, dy_own, dy_oth, gate_up, w_down, halves, half_down, *rest):
    messages, rest = rest[:4], rest[4:]
    if chunk:
        carried, rest = rest[:4], rest[4:]
    out_own, out_oth, dn_own, dn_oth, keep_x, keep_y, send_x, send_y = rest[:8]
    weight, drop, drop_half, act, dgu, units, x_t, dy_t, x, dy, acc_out, acc_dn, sem = rest[8:]
    hidden, down_at = HIDDEN[chunk], DOWN_AT[chunk]
    with_half = chunk == 0
    p, k, f = place[0], place[1], place[2]

    copies = []

    def copy(source, target):
        copies.append(pltpu.make_async_copy(source, target, sem))

    for half, (xs, ds) in enumerate(((x_own, dy_own), (x_oth, dy_oth))):
        lanes = pl.ds(half * TOK_DEV, TOK_DEV)
        copy(xs, x_t.at[:, lanes])
        copy(ds, dy_t.at[:, lanes])
    tile_of_core = 2 * k + chunk
    for kind in range(2):
        for z in range(4):
            col = pl.multiple_of(kind * FF + z * FF_SHARD + tile_of_core * TILE, TILE)
            copy(
                gate_up.at[:, pl.ds(col, TILE)],
                weight.at[f, :, pl.ds(kind * hidden + z * TILE, TILE)],
            )
        if with_half:
            copy(
                halves.at[:, pl.ds(kind * 2 * TILE, 2 * TILE)],
                weight.at[f, :, pl.ds(kind * hidden + 4 * TILE, 2 * TILE)],
            )
    copy(
        w_down.at[:, pl.ds(pl.multiple_of(tile_of_core * TILE, TILE), TILE)],
        drop.at[:, pl.ds(pl.multiple_of(f * TILE, TILE), TILE)],
    )
    if with_half:
        copy(half_down, drop_half.at[f])
    for q, ref in enumerate(messages):
        pp = jnp.bitwise_xor(p, q)
        for r in range(3):
            z = jnp.bitwise_xor(f, r + 1)
            rows = pl.ds(r * ROWS, ROWS)
            for kind in range(2):
                lane = pl.multiple_of(kind * hidden + pp * TILE, TILE)
                copy(
                    ref.at[rows, pl.ds(kind * TILE, TILE)], weight.at[z, :, pl.ds(lane, TILE)]
                )
            rows_at = pl.ds(pl.multiple_of(pp * ROWS, 16), ROWS)
            copy(
                ref.at[rows, pl.ds(down_at * TILE, TILE)],
                drop.at[rows_at, pl.ds(pl.multiple_of(z * TILE, TILE), TILE)],
            )
            if with_half:
                lane = jnp.right_shift(pp, 1) * hidden + 4 * TILE + jnp.bitwise_and(pp, 1) * TILE
                copy(
                    ref.at[rows, pl.ds(2 * TILE, TILE)],
                    weight.at[z, :, pl.ds(pl.multiple_of(lane, TILE), TILE)],
                )
                copy(ref.at[rows, pl.ds(4 * TILE, TILE)], drop_half.at[z, rows_at])
    if chunk:
        for half in range(2):
            lanes = pl.ds(half * TOK_DEV, TOK_DEV)
            copy(carried[half], acc_out.at[:, lanes])
            copy(carried[2 + half], acc_dn.at[:, lanes])
    for each in copies:
        each.start()
    for each in copies:
        each.wait()

    x[...] = x_t[...].T
    dy[...] = dy_t[...].T
    if with_half:
        for z in range(4):
            lane = 4 * TILE + z * HALF
            drop[:, lane : lane + HALF] = drop_half[z, :, :HALF]

    def tile(t, carry):
        rows = pl.ds(pl.multiple_of(t * ROW_TILE, ROW_TILE), ROW_TILE)
        both = weight[...].reshape(D, 2 * hidden)
        gu = jnp.dot(x[rows, :], both, preferred_element_type=F32)
        da = jnp.dot(dy[rows, :], drop[...], preferred_element_type=F32)
        g, u = gu[:, :hidden], gu[:, hidden:]
        sig = jax.nn.sigmoid(g)
        silu = g * sig
        a = (silu * u).astype(BF16)
        act[rows, :] = a
        dgu[rows, :hidden] = (da * u * sig * (1.0 + g * (1.0 - sig))).astype(BF16)
        dgu[rows, hidden:] = (da * silu).astype(BF16)
        out = lax.dot_general(drop[...], a, NT, preferred_element_type=F32)
        dn = lax.dot_general(both, dgu[rows, :], NT, preferred_element_type=F32)
        if chunk:
            acc_out[:, rows] += out
            acc_dn[:, rows] += dn
        else:
            acc_out[:, rows] = out
            acc_dn[:, rows] = dn
        return carry

    lax.fori_loop(0, 2 * TOK_DEV // ROW_TILE, tile, 0)

    step = 2 * TILE
    for start in range(0, 2 * hidden, step):
        grad = jnp.dot(
            x_t[...], dgu[:, start : start + step], preferred_element_type=F32
        ).astype(BF16)
        for part in range(2):
            kind, lane = divmod(start + part * TILE, hidden)
            at = lane // TILE
            pp, column = (at, kind) if at < 4 else (2 * kind + at - 4, 2)
            units[pp, :, :, column * TILE : (column + 1) * TILE] = grad[
                :, part * TILE : (part + 1) * TILE
            ].reshape(4, ROWS, TILE)
    for start in range(0, hidden, step):
        grad = jnp.dot(
            dy_t[...], act[:, start : start + step], preferred_element_type=F32
        ).astype(BF16)
        if start < 4 * TILE:
            for part in range(2):
                z = start // TILE + part
                units[:, z, :, down_at * TILE : (down_at + 1) * TILE] = grad[
                    :, part * TILE : (part + 1) * TILE
                ].reshape(4, ROWS, TILE)
        else:
            for z in range(4):
                units[:, z, :, 4 * TILE : 4 * TILE + HALF] = grad[
                    :, z * HALF : (z + 1) * HALF
                ].reshape(4, ROWS, HALF)

    copies.clear()
    for q in range(4):
        pp = jnp.bitwise_xor(p, q)
        left = (keep_x, send_x)[q & 1].at[q >> 1]
        right = (keep_y, send_y)[q >> 1].at[q & 1]
        for r in range(4):
            copy(
                units.at[pp, jnp.bitwise_xor(f, r)],
                (left, right)[r // 2].at[pl.ds((r % 2) * ROWS, ROWS)],
            )
    for each in copies:
        each.start()
    out_own[...] = acc_out[:, :TOK_DEV]
    dn_own[...] = acc_dn[:, :TOK_DEV]
    out_oth[...] = acc_out[:, TOK_DEV:].astype(out_oth.dtype)
    dn_oth[...] = acc_dn[:, TOK_DEV:].astype(dn_oth.dtype)
    for each in copies:
        each.wait()


def mlp_chunk(place, chunk, tokens, weights, messages, carried):
    hidden = HIDDEN[chunk]
    width = UNIT_TILES[chunk] * TILE
    side = jax.ShapeDtypeStruct((D, TOK_DEV), BF16 if chunk else F32)
    main = jax.ShapeDtypeStruct((D, TOK_DEV), F32)
    part = jax.ShapeDtypeStruct((2, 2 * ROWS, width), BF16)
    operands = [place, *tokens, *weights, *messages]
    if chunk:
        operands += list(carried)
    out = pl.pallas_call(
        functools.partial(mlp_kernel, chunk),
        out_shape=[main, side, main, side] + [part] * 4,
        in_specs=[SMEM] + [ANY] * (len(operands) - 1),
        out_specs=[VMEM] * 4 + [ANY] * 4,
        scratch_shapes=[
            pltpu.VMEM((4, ROWS, 2 * hidden), BF16),
            pltpu.VMEM((D, hidden), BF16),
            pltpu.VMEM((4, D, TILE), BF16),
            pltpu.VMEM((2 * TOK_DEV, hidden), BF16),
            pltpu.VMEM((2 * TOK_DEV, 2 * hidden), BF16),
            pltpu.VMEM((4, 4, ROWS, width), BF16),
            pltpu.VMEM((D, 2 * TOK_DEV), BF16),
            pltpu.VMEM((D, 2 * TOK_DEV), BF16),
            pltpu.VMEM((2 * TOK_DEV, D), BF16),
            pltpu.VMEM((2 * TOK_DEV, D), BF16),
            pltpu.VMEM((D, 2 * TOK_DEV), F32),
            pltpu.VMEM((D, 2 * TOK_DEV), F32),
            pltpu.SemaphoreType.DMA(()),
        ],
        compiler_params=pltpu.CompilerParams(vmem_limit_bytes=VMEM_LIMIT),
        cost_estimate=pl.CostEstimate(
            flops=2 * 2 * TOK_DEV * D * hidden * 9, bytes_accessed=20_000_000, transcendentals=0
        ),
    )(*operands)
    return out[:4], out[4:6], out[6:8]


def finish_mlp_kernel(firsts, place, *refs):
    up, down = refs[-2:]
    p, k = place[0], place[1]
    for chunk, first in enumerate(firsts):
        pairs = refs[4 * chunk : 4 * chunk + 4]
        down_at = DOWN_AT[chunk]
        for q in range(4):
            pp = jnp.bitwise_xor(p, q)
            rows = pl.ds(pl.multiple_of(pp * ROWS, 16), ROWS)
            side, at = piece_index(first, q)
            for other in range(2):
                kk = jnp.bitwise_xor(k, other)
                ref = pairs[2 * other + side].at[at]
                for kind in range(2):
                    col = kind * FF + pp * FF_SHARD + (2 * kk + chunk) * TILE
                    up[:, pl.ds(pl.multiple_of(col, TILE), TILE)] = ref[
                        :, kind * TILE : (kind + 1) * TILE
                    ].astype(F32)
                col = pl.multiple_of((2 * kk + chunk) * TILE, TILE)
                down[rows, pl.ds(col, TILE)] = ref[
                    :, down_at * TILE : (down_at + 1) * TILE
                ].astype(F32)
            if chunk == 0:
                own, oth = (
                    pairs[2 * other + side][at, :, 2 * TILE : 3 * TILE] for other in range(2)
                )
                low = jnp.where(k == 0, own, oth).astype(F32)
                high = jnp.where(k == 0, oth, own).astype(F32)
                for half in range(2):
                    lanes = slice(half * HALF, (half + 1) * HALF)
                    z = 2 * jnp.bitwise_and(pp, 1) + half
                    col = jnp.right_shift(pp, 1) * FF + z * FF_SHARD + 4 * TILE
                    up[:, pl.ds(pl.multiple_of(col, TILE), TILE)] = jnp.concatenate(
                        [low[:, lanes], high[:, lanes]], axis=1
                    )
                own, oth = (
                    pairs[2 * other + side][at, :, 4 * TILE : 4 * TILE + HALF].astype(F32)
                    for other in range(2)
                )
                low, high = jnp.where(k == 0, own, oth), jnp.where(k == 0, oth, own)
                down[rows, 4 * TILE :] = jnp.concatenate([low, high], axis=1)


def finish_mlp(place, pieces, firsts):
    return pl.pallas_call(
        functools.partial(finish_mlp_kernel, firsts),
        out_shape=[
            jax.ShapeDtypeStruct((ROWS, 2 * FF), F32),
            jax.ShapeDtypeStruct((D, FF_SHARD), F32),
        ],
        in_specs=[SMEM] + [VMEM] * len(pieces),
        out_specs=[VMEM] * 2,
        compiler_params=pltpu.CompilerParams(vmem_limit_bytes=VMEM_LIMIT),
        cost_estimate=pl.CostEstimate(flops=0, bytes_accessed=24_000_000, transcendentals=0),
    )(place, *pieces)


def load_rows(place, own, mine, theirs, full, sem):
    p, k, f = place[0], place[1], place[2]
    for start in (True, False):

        def run(copy, start=start):
            if start:
                copy.start()
            else:
                copy.wait()

        run(pltpu.make_async_copy(own, full.at[f], sem))
        for other in range(2):
            kk = jnp.bitwise_xor(k, other)
            for q in range(4):
                ref = theirs.at[q] if other else mine[q]
                pp = jnp.bitwise_xor(p, q)
                row = pl.multiple_of(kk * 128 + pp * SLICE, 16)
                short = (kk * 4 + pp) == 7
                for r in range(3):
                    z = jnp.bitwise_xor(f, r + 1)

                    def go(count, ref=ref, r=r, z=z, row=row):
                        run(
                            pltpu.make_async_copy(
                                ref.at[r, pl.ds(0, count)], full.at[z, pl.ds(row, count)], sem
                            )
                        )

                    pl.when(short)(functools.partial(go, 16))
                    pl.when(jnp.logical_not(short))(functools.partial(go, SLICE))


def store_rows(place, grad, halves, theirs, sem):
    p, k, f = place[0], place[1], place[2]
    keep_x, keep_y, send_x, send_y = halves
    for start in (True, False):
        for other in range(2):
            kk = jnp.bitwise_xor(k, other)
            for q in range(4):
                pp = jnp.bitwise_xor(p, q)
                row = pl.multiple_of(kk * 128 + pp * SLICE, 16)
                short = (kk * 4 + pp) == 7
                left = (keep_x, send_x)[q & 1].at[q >> 1]
                right = (keep_y, send_y)[q >> 1].at[q & 1]
                for r in range(4):
                    z = jnp.bitwise_xor(f, r)
                    if not other:
                        target = (left, right)[r // 2]
                    elif r < 2:
                        target = theirs.at[2 * (q & 1), q >> 1]
                    else:
                        target = theirs.at[1 + 2 * (q >> 1), q & 1]
                    target = target.at[pl.ds((r % 2) * SLICE, SLICE)]

                    def go(count, target=target, z=z, row=row):
                        copy = pltpu.make_async_copy(
                            grad.at[z, pl.ds(row, count)], target.at[pl.ds(0, count)], sem
                        )
                        if start:
                            copy.start()
                        else:
                            copy.wait()

                    pl.when(short)(functools.partial(go, 16))
                    pl.when(jnp.logical_not(short))(functools.partial(go, SLICE))


def finish_rows_kernel(first, place, near, far, near_oth, far_oth, *outs):
    p, k = place[0], place[1]
    pairs = (near, far, near_oth, far_oth)
    for other in range(2):
        kk = jnp.bitwise_xor(k, other)
        for q in range(4):
            side, at = piece_index(first, q)
            value = pairs[2 * other + side][at].astype(F32)
            pp = jnp.bitwise_xor(p, q)
            row = pl.multiple_of(kk * 128 + pp * SLICE, 16)
            short = (kk * 4 + pp) == 7

            def go(count, value=value, row=row):
                lane = 0
                for out in outs:
                    wide = out.shape[1]
                    out[pl.ds(row, count), :] = value[:count, lane : lane + wide]
                    lane += wide

            pl.when(short)(functools.partial(go, 16))
            pl.when(jnp.logical_not(short))(functools.partial(go, SLICE))


def finish_rows(place, pairs, first, widths):
    return pl.pallas_call(
        functools.partial(finish_rows_kernel, first),
        out_shape=[jax.ShapeDtypeStruct((ROWS, width), F32) for width in widths],
        in_specs=[SMEM] + [VMEM] * 4,
        out_specs=[VMEM] * len(widths),
        compiler_params=pltpu.CompilerParams(vmem_limit_bytes=VMEM_LIMIT),
        cost_estimate=pl.CostEstimate(
            flops=0, bytes_accessed=6 * ROWS * sum(widths), transcendentals=0
        ),
    )(place, *pairs)


def token_scale(values):
    return lax.rsqrt(jnp.mean(values * values, axis=0, keepdims=True) + EPSILON)


def project_kernel(
    place, x, cosines, sines, own, m0, m1, m2, m3, theirs, full, gains, normed, q_t, kv, sem
):
    load_rows(place, own, (m0, m1, m2, m3), theirs, full, sem)
    weight = full[...].reshape(D, QKV_WIDE)
    columns = weight[:, QKV - HALF :].astype(F32)
    gains[...] = columns
    source = x[...].astype(F32)
    normed[...] = (source * token_scale(source) * columns[:, HALF : HALF + 1]).astype(BF16)
    mixed = lax.dot_general(weight[:, :QKV], normed[...], TN, preferred_element_type=F32)
    cos, sin = cosines[...], sines[...]
    half = HEAD_DIM // 2
    for head in range(HEADS + KV_HEADS):
        row = head * HEAD_DIM
        low, high = mixed[row : row + half], mixed[row + half : row + HEAD_DIM]
        low, high = (low * cos - high * sin).astype(BF16), (high * cos + low * sin).astype(BF16)
        if head < HEADS:
            q_t[row : row + half, :] = low
            q_t[row + half : row + HEAD_DIM, :] = high
        else:
            row -= D
            for block in range(TOK_DEV // BLK):
                lanes = slice(block * BLK, (block + 1) * BLK)
                kv[block, row : row + half, :] = low[:, lanes]
                kv[block, row + half : row + HEAD_DIM, :] = high[:, lanes]
    for block in range(TOK_DEV // BLK):
        lanes = slice(block * BLK, (block + 1) * BLK)
        kv[block, KV_DIM:, :] = mixed[D + KV_DIM :, lanes].astype(BF16)


def project(place, x, cosines, sines, own, mine, theirs):
    return pl.pallas_call(
        project_kernel,
        out_shape=[
            jax.ShapeDtypeStruct((4, ROWS, QKV_WIDE), BF16),
            jax.ShapeDtypeStruct((D, TILE), F32),
            jax.ShapeDtypeStruct((D, TOK_DEV), BF16),
            jax.ShapeDtypeStruct((D, TOK_DEV), BF16),
            jax.ShapeDtypeStruct((TOK_DEV // BLK, 2 * KV_DIM, BLK), BF16),
        ],
        in_specs=[SMEM] + [VMEM] * 3 + [ANY] * 6,
        out_specs=[VMEM] * 5,
        scratch_shapes=[pltpu.SemaphoreType.DMA(())],
        compiler_params=pltpu.CompilerParams(vmem_limit_bytes=VMEM_LIMIT),
        cost_estimate=pl.CostEstimate(
            flops=2 * TOK_DEV * D * QKV, bytes_accessed=10_000_000, transcendentals=0
        ),
    )(place, x, cosines, sines, own, *mine, theirs)


def three_heads(ref, group, lanes):
    first = group * (HEADS // KV_HEADS) * HEAD_DIM
    return jnp.concatenate(
        [
            ref[first + r * HEAD_DIM : first + (r + 1) * HEAD_DIM, lanes]
            for r in range(HEADS // KV_HEADS)
        ],
        axis=1,
    )


def diagonal_mask():
    shape = (BLK, BLK * (HEADS // KV_HEADS))
    keys = lax.broadcasted_iota(jnp.int32, shape, 0)
    queries = jnp.bitwise_and(lax.broadcasted_iota(jnp.int32, shape, 1), BLK - 1)
    return keys <= queries


def attend_kernel(lows, q_t, *rest):
    spans = rest[:-6]
    attn_t, log_total, kv, best, total, accum = rest[-6:]
    blocks = TOK_DEV // BLK
    for at, ref in enumerate(spans):
        kv[at * blocks : (at + 1) * blocks] = ref[...]
    own_at = (len(spans) - 1) * blocks
    mask = diagonal_mask()
    for i in range(blocks):
        lanes = slice(i * BLK, (i + 1) * BLK)
        queries = [
            three_heads(q_t, group, lanes) * jnp.asarray(HEAD_DIM**-0.5, BF16)
            for group in range(KV_HEADS)
        ]

        def step(j, diagonal, queries=queries):
            for group in range(KV_HEADS):
                keys = kv[j, group * HEAD_DIM : (group + 1) * HEAD_DIM, :]
                values = kv[j, KV_DIM + group * HEAD_DIM : KV_DIM + (group + 1) * HEAD_DIM, :]
                scores = lax.dot_general(keys, queries[group], TN, preferred_element_type=F32)
                if diagonal:
                    scores = jnp.where(mask, scores, MASKED_SCORE)
                    top = jnp.max(scores, axis=0, keepdims=True)
                    expo = jnp.exp(scores - top)
                    total[group] = jnp.sum(expo, axis=0, keepdims=True)
                    accum[group] = jnp.dot(values, expo.astype(BF16), preferred_element_type=F32)
                else:
                    old = best[group]
                    top = jnp.maximum(old, jnp.max(scores, axis=0, keepdims=True))
                    decay = jnp.exp(old - top)
                    expo = jnp.exp(scores - top)
                    total[group] = total[group] * decay + jnp.sum(expo, axis=0, keepdims=True)
                    accum[group] = accum[group] * decay + jnp.dot(
                        values, expo.astype(BF16), preferred_element_type=F32
                    )
                best[group] = top

        step(own_at + i, True)

        @pl.loop(lows[i], own_at + i)
        def earlier(j):
            step(j, False)

        for group in range(KV_HEADS):
            attn = (accum[group] / total[group]).astype(BF16)
            first = group * (HEADS // KV_HEADS) * HEAD_DIM
            for r in range(HEADS // KV_HEADS):
                attn_t[first + r * HEAD_DIM : first + (r + 1) * HEAD_DIM, lanes] = attn[
                    :, r * BLK : (r + 1) * BLK
                ]
            log_total[i * KV_HEADS + group] = best[group] + jnp.log(total[group])


def attend(lows, q_t, spans):
    blocks = TOK_DEV // BLK
    wide = BLK * (HEADS // KV_HEADS)
    return pl.pallas_call(
        attend_kernel,
        out_shape=[
            jax.ShapeDtypeStruct((D, TOK_DEV), BF16),
            jax.ShapeDtypeStruct((blocks * KV_HEADS, 1, wide), F32),
        ],
        in_specs=[SMEM] + [VMEM] * (1 + len(spans)),
        out_specs=[VMEM] * 2,
        scratch_shapes=[
            pltpu.VMEM((len(spans) * blocks, 2 * KV_DIM, BLK), BF16),
            pltpu.VMEM((KV_HEADS, 1, wide), F32),
            pltpu.VMEM((KV_HEADS, 1, wide), F32),
            pltpu.VMEM((KV_HEADS, HEAD_DIM, wide), F32),
        ],
        compiler_params=pltpu.CompilerParams(vmem_limit_bytes=VMEM_LIMIT),
        cost_estimate=pl.CostEstimate(
            flops=8_000_000_000, bytes_accessed=4_000_000, transcendentals=2_000_000
        ),
    )(lows, q_t, *spans)


def out_kernel(place, x, gains, attn_t, own, m0, m1, m2, m3, theirs, full, hidden, normed, sem):
    load_rows(place, own, (m0, m1, m2, m3), theirs, full, sem)
    value = x[...].astype(F32) + lax.dot_general(
        full[...].reshape(D, D), attn_t[...], TN, preferred_element_type=F32
    )
    hidden[...] = value
    normed[...] = (value * token_scale(value) * gains[:, HALF + 1 : HALF + 2]).astype(BF16)


def project_out(place, x, gains, attn_t, own, mine, theirs):
    return pl.pallas_call(
        out_kernel,
        out_shape=[
            jax.ShapeDtypeStruct((4, ROWS, D), BF16),
            jax.ShapeDtypeStruct((D, TOK_DEV), F32),
            jax.ShapeDtypeStruct((D, TOK_DEV), BF16),
        ],
        in_specs=[SMEM] + [VMEM] * 3 + [ANY] * 6,
        out_specs=[VMEM] * 3,
        scratch_shapes=[pltpu.SemaphoreType.DMA(())],
        compiler_params=pltpu.CompilerParams(vmem_limit_bytes=VMEM_LIMIT),
        cost_estimate=pl.CostEstimate(
            flops=2 * TOK_DEV * D * D, bytes_accessed=8_000_000, transcendentals=0
        ),
    )(place, x, gains, attn_t, own, *mine, theirs)


def norm_back(value, scale, gain, dn):
    unit = value * scale
    weighted = dn * gain
    d_value = scale * (weighted - unit * jnp.mean(weighted * unit, axis=0, keepdims=True))
    return d_value, jnp.sum(dn * unit, axis=1, keepdims=True)


def middle_kernel(
    place, hidden, dy, gains, dn_own, dn_oth, attn_t, full, d_hidden, d_attn_t, grad_gain, *rest
):
    halves, theirs, grad, sem = rest[:4], rest[4], rest[5], rest[6]
    value = hidden[...]
    dn = dn_own[...] + dn_oth[...].astype(F32)
    d_value, column = norm_back(value, token_scale(value), gains[:, HALF + 1 : HALF + 2], dn)
    grad_gain[...] = jnp.broadcast_to(column, (D, TILE))
    dh = dy[...].astype(F32) + d_value
    d_hidden[...] = dh
    dh = dh.astype(BF16)
    d_attn_t[...] = jnp.dot(
        full[...].reshape(D, D), dh, preferred_element_type=F32
    ).astype(BF16)
    product = lax.dot_general(attn_t[...], dh, NT, preferred_element_type=F32)
    grad[...] = product.astype(BF16).reshape(4, ROWS, D)
    store_rows(place, grad, halves, theirs, sem)


def middle(place, hidden, dy, gains, dn_own, dn_oth, attn_t, full):
    piece = jax.ShapeDtypeStruct((2, 2 * SLICE, D), BF16)
    out = pl.pallas_call(
        middle_kernel,
        out_shape=[
            jax.ShapeDtypeStruct((D, TOK_DEV), F32),
            jax.ShapeDtypeStruct((D, TOK_DEV), BF16),
            jax.ShapeDtypeStruct((D, TILE), F32),
            *[piece] * 4,
            jax.ShapeDtypeStruct((4, 2, 2 * SLICE, D), BF16),
        ],
        in_specs=[SMEM] + [VMEM] * 7,
        out_specs=[VMEM] * 3 + [ANY] * 5,
        scratch_shapes=[pltpu.VMEM((4, ROWS, D), BF16), pltpu.SemaphoreType.DMA(())],
        compiler_params=pltpu.CompilerParams(vmem_limit_bytes=VMEM_LIMIT),
        cost_estimate=pl.CostEstimate(
            flops=4 * TOK_DEV * D * D, bytes_accessed=14_000_000, transcendentals=0
        ),
    )(place, hidden, dy, gains, dn_own, dn_oth, attn_t, full)
    return out[0], out[1], out[2], out[3:7], out[7]


def attend_back_kernel(count, lows, q_t, attn_t, d_attn_t, log_total, cosines, sines, *rest):
    spans, rest = rest[:count], rest[count:]
    dq_t, d_spans, (kv, d_kv, d_query) = rest[0], rest[1 : 1 + count], rest[1 + count :]
    blocks = TOK_DEV // BLK
    groups = HEADS // KV_HEADS
    half = HEAD_DIM // 2
    for at, ref in enumerate(spans):
        kv[at * blocks : (at + 1) * blocks] = ref[...]
    d_kv[...] = jnp.zeros_like(d_kv)
    own_at = (count - 1) * blocks
    mask = diagonal_mask()
    for i in range(blocks):
        lanes = slice(i * BLK, (i + 1) * BLK)
        queries, d_outs, deltas = [], [], []
        for group in range(KV_HEADS):
            queries.append(three_heads(q_t, group, lanes) * jnp.asarray(HEAD_DIM**-0.5, BF16))
            d_out = three_heads(d_attn_t, group, lanes)
            attn = three_heads(attn_t, group, lanes)
            d_outs.append(d_out)
            deltas.append(
                jnp.sum(d_out.astype(F32) * attn.astype(F32), axis=0, keepdims=True)
            )

        def step(j, diagonal, i=i, queries=queries, d_outs=d_outs, deltas=deltas):
            for group in range(KV_HEADS):
                key_rows = slice(group * HEAD_DIM, (group + 1) * HEAD_DIM)
                value_rows = slice(KV_DIM + group * HEAD_DIM, KV_DIM + (group + 1) * HEAD_DIM)
                keys, values = kv[j, key_rows, :], kv[j, value_rows, :]
                scores = lax.dot_general(keys, queries[group], TN, preferred_element_type=F32)
                if diagonal:
                    scores = jnp.where(mask, scores, MASKED_SCORE)
                prob = jnp.exp(scores - log_total[i * KV_HEADS + group])
                d_prob = lax.dot_general(values, d_outs[group], TN, preferred_element_type=F32)
                d_scores = (prob * (d_prob - deltas[group])).astype(BF16)
                d_kv[j, value_rows, :] += lax.dot_general(
                    d_outs[group], prob.astype(BF16), NT, preferred_element_type=F32
                )
                d_kv[j, key_rows, :] += lax.dot_general(
                    queries[group], d_scores, NT, preferred_element_type=F32
                )
                more = jnp.dot(keys, d_scores, preferred_element_type=F32)
                if diagonal:
                    d_query[group] = more
                else:
                    d_query[group] += more

        step(own_at + i, True)

        @pl.loop(lows[i], own_at + i)
        def earlier(j):
            step(j, False)

        cos, sin = cosines[:, lanes], sines[:, lanes]
        for group in range(KV_HEADS):
            for r in range(groups):
                row = (group * groups + r) * HEAD_DIM
                side = slice(r * BLK, (r + 1) * BLK)
                low = d_query[group, :half, side] * HEAD_DIM**-0.5
                high = d_query[group, half:, side] * HEAD_DIM**-0.5
                dq_t[row : row + half, lanes] = (low * cos + high * sin).astype(BF16)
                dq_t[row + half : row + HEAD_DIM, lanes] = (high * cos - low * sin).astype(BF16)
    for at, ref in enumerate(d_spans):
        ref[...] = d_kv[at * blocks : (at + 1) * blocks].astype(ref.dtype)


def attend_back(lows, q_t, attn_t, d_attn_t, log_total, cosines, sines, spans):
    blocks = TOK_DEV // BLK
    wide = BLK * (HEADS // KV_HEADS)
    count = len(spans)
    shape = (blocks, 2 * KV_DIM, BLK)
    out = pl.pallas_call(
        functools.partial(attend_back_kernel, count),
        out_shape=[jax.ShapeDtypeStruct((D, TOK_DEV), BF16)]
        + [jax.ShapeDtypeStruct(shape, BF16)] * (count - 1)
        + [jax.ShapeDtypeStruct(shape, F32)],
        in_specs=[SMEM] + [VMEM] * (6 + count),
        out_specs=[VMEM] * (1 + count),
        scratch_shapes=[
            pltpu.VMEM((count * blocks, 2 * KV_DIM, BLK), BF16),
            pltpu.VMEM((count * blocks, 2 * KV_DIM, BLK), F32),
            pltpu.VMEM((KV_HEADS, HEAD_DIM, wide), F32),
        ],
        compiler_params=pltpu.CompilerParams(vmem_limit_bytes=VMEM_LIMIT),
        cost_estimate=pl.CostEstimate(
            flops=16_000_000_000, bytes_accessed=8_000_000, transcendentals=2_000_000
        ),
    )(lows, q_t, attn_t, d_attn_t, log_total, cosines, sines, *spans)
    return out[0], out[1:]


def last_kernel(
    count, place, x, gains, normed, dq_t, cosines, sines, full, d_hidden, mlp_gain_grad, d_own, *rest
):
    arrived, rest = rest[:count], rest[count:]
    input_grad, halves, theirs, d_mixed, grad, sem = rest[0], rest[1:5], rest[5], *rest[6:]
    half = HEAD_DIM // 2
    d_mixed[:D, :] = dq_t[...]
    for block in range(TOK_DEV // BLK):
        lanes = slice(block * BLK, (block + 1) * BLK)
        value = d_own[block]
        for ref in arrived:
            value = value + ref[block].astype(F32)
        cos, sin = cosines[:, lanes], sines[:, lanes]
        for head in range(KV_HEADS):
            row = head * HEAD_DIM
            low, high = value[row : row + half], value[row + half : row + HEAD_DIM]
            d_mixed[D + row : D + row + half, lanes] = (low * cos + high * sin).astype(BF16)
            d_mixed[D + row + half : D + row + HEAD_DIM, lanes] = (high * cos - low * sin).astype(
                BF16
            )
        d_mixed[D + KV_DIM :, lanes] = value[KV_DIM:].astype(BF16)
    product = lax.dot_general(normed[...], d_mixed[...], NT, preferred_element_type=F32)
    grad[:, :, :QKV] = product.astype(BF16).reshape(4, ROWS, QKV)
    weight = full[...].reshape(D, QKV_WIDE)[:, :QKV]
    dn = jnp.dot(weight, d_mixed[...], preferred_element_type=F32)
    source = x[...].astype(F32)
    d_value, column = norm_back(source, token_scale(source), gains[:, HALF : HALF + 1], dn)
    input_grad[...] = (d_hidden[...] + d_value).astype(BF16)
    lane = lax.broadcasted_iota(jnp.int32, (D, QKV_WIDE - QKV), 1)
    both = jnp.where(lane == 0, column, mlp_gain_grad[:, : QKV_WIDE - QKV])
    grad[:, :, QKV:] = both.astype(BF16).reshape(4, ROWS, QKV_WIDE - QKV)
    store_rows(place, grad, halves, theirs, sem)


def last(place, x, gains, normed, dq_t, cosines, sines, full, d_hidden, mlp_gain_grad, d_own, arrived):
    piece = jax.ShapeDtypeStruct((2, 2 * SLICE, QKV_WIDE), BF16)
    out = pl.pallas_call(
        functools.partial(last_kernel, len(arrived)),
        out_shape=[
            jax.ShapeDtypeStruct((D, TOK_DEV), BF16),
            *[piece] * 4,
            jax.ShapeDtypeStruct((4, 2, 2 * SLICE, QKV_WIDE), BF16),
        ],
        in_specs=[SMEM] + [VMEM] * (10 + len(arrived)),
        out_specs=[VMEM] + [ANY] * 5,
        scratch_shapes=[
            pltpu.VMEM((QKV, TOK_DEV), BF16),
            pltpu.VMEM((4, ROWS, QKV_WIDE), BF16),
            pltpu.SemaphoreType.DMA(()),
        ],
        compiler_params=pltpu.CompilerParams(vmem_limit_bytes=VMEM_LIMIT),
        cost_estimate=pl.CostEstimate(
            flops=4 * TOK_DEV * D * QKV, bytes_accessed=14_000_000, transcendentals=0
        ),
    )(place, x, gains, normed, dq_t, cosines, sines, full, d_hidden, mlp_gain_grad, d_own, *arrived)
    return out[0], out[1:5], out[5]


def shards(
    links,
    tokens,
    cotangent,
    positions,
    doc_ids,
    gain_attn,
    w_qkv,
    w_out,
    gain_mlp,
    w_gate_up,
    w_down,
):
    seq_at, ctx_at, f = (lax.axis_index(name) for name in AXES)
    k = jnp.bitwise_and(seq_at, 1)
    p = 2 * jnp.right_shift(seq_at, 1) + jnp.bitwise_and(ctx_at, 1)
    place = jnp.stack([p, k, f]).astype(jnp.int32)
    n_ctx = links.sizes[1]
    x_in, dy_own = tokens[0].T, cotangent[0].T

    pad = jnp.zeros((ROWS, QKV_WIDE - QKV - 2), BF16)
    qkv_own = jnp.concatenate([w_qkv, gain_attn[:, None], gain_mlp[:, None], pad], axis=1)

    def row_slice(weight):
        padded = jnp.pad(weight, ((0, ROWS_PAD - ROWS), (0, 0)))
        return lax.dynamic_slice_in_dim(padded, k * 128 + p * SLICE, SLICE, 0)

    both_z = links.gather_z(jnp.concatenate([row_slice(qkv_own), row_slice(w_out)], axis=1))
    qkv_mine = links.gather_plane(jnp.stack([value[:, :QKV_WIDE] for value in both_z]))
    out_mine = links.gather_plane(
        jnp.stack([value[:, QKV_WIDE:] for value in after(both_z, *qkv_mine)])
    )
    angles = frequencies()[:, None] * positions[0].astype(F32)[None, :]
    cosines, sines = jnp.cos(angles), jnp.sin(angles)
    blocks = TOK_DEV // BLK
    docs = doc_ids[0]
    own_docs = lax.dynamic_slice_in_dim(docs, ctx_at * blocks, blocks)
    lows = jnp.sum((docs[None, :] < own_docs[:, None]).astype(jnp.int32), axis=1)
    lows = lows + (n_ctx - 1 - ctx_at) * blocks
    qkv_theirs = links.core(jnp.stack(qkv_mine))

    def core_half(pair):
        return jnp.where(k == 0, pair[:, :HALF], pair[:, HALF:])

    halves = jnp.concatenate(
        [core_half(w_gate_up[:, at : at + TILE]) for at in range(4 * TILE, 2 * FF, FF_SHARD)],
        axis=1,
    )
    down_t = w_down.T
    half_down = jnp.pad(core_half(down_t[:, 4 * TILE :]), ((0, 0), (0, HALF)))

    def unit(chunk):
        tiles = []
        for kind in range(2):
            col = kind * FF + p * FF_SHARD + (2 * k + chunk) * TILE
            tiles.append(lax.dynamic_slice_in_dim(w_gate_up, col, TILE, 1))
        if chunk == 0:
            tiles.append(lax.dynamic_slice_in_dim(halves, p * TILE, TILE, 1))
        tiles.append(
            lax.dynamic_slice(down_t, (p * ROWS, (2 * k + chunk) * TILE), (ROWS, TILE))
        )
        if chunk == 0:
            tiles.append(lax.dynamic_slice_in_dim(half_down, p * ROWS, ROWS, 0))
        return jnp.concatenate(tiles, axis=1)

    unit_a, unit_b = unit(0), unit(1)
    one_a = links.swap(after(unit_a, *both_z), df=1)
    (one_a,) = gate([one_a], *qkv_mine)
    pair_a = jnp.concatenate([unit_a, one_a], axis=0)
    two_a = links.swap(pair_a, df=2)

    qkv_full, gains, normed, q_t, kv = project(
        place, x_in, cosines, sines, after(qkv_own, pair_a), qkv_mine, qkv_theirs
    )
    spans = [links.later(kv, d, 1) for d in range(n_ctx - 1, 0, -1)] + [kv]
    one_a, two_a, *out_mine = gate([one_a, two_a, *out_mine], kv)
    out_theirs = links.core(jnp.stack(out_mine))
    first_a = jnp.concatenate([one_a, two_a], axis=0)
    y_a, x_a = links.plane(first_a, 2), links.plane(first_a, 1)
    one_b = links.swap(after(unit_b, first_a), df=1)
    dy_oth = links.core(dy_own)
    attn_t, log_total = attend(lows, after(q_t, first_a), spans)
    x_a, one_b, out_theirs, dy_oth = gate([x_a, one_b, out_theirs, dy_oth], attn_t)
    xy_a = links.plane(x_a, 2)
    pair_b = jnp.concatenate([unit_b, one_b], axis=0)
    two_b = links.swap(pair_b, df=2)
    out_full, hidden, normed_mlp = project_out(
        place, x_in, gains, after(attn_t, x_a, pair_b), w_out, out_mine, out_theirs
    )

    x_oth = links.core(normed_mlp)
    y_a, xy_a, two_b = gate([y_a, xy_a, two_b], hidden)
    first_b = jnp.concatenate([one_b, two_b], axis=0)
    rest_b = [links.plane(first_b, bits) for bits in (1, 2, 3)]
    mlp_weights = (w_gate_up, down_t, halves, half_down)
    carried, keep_a, send_a = mlp_chunk(
        place,
        0,
        (after(normed_mlp, first_b), x_oth, dy_own, dy_oth),
        mlp_weights,
        [first_a, x_a, y_a, xy_a],
        None,
    )
    arrived_a = links.send_one(send_a)
    rest_b = gate(rest_b, *carried)
    (out_own, out_oth, dn_own, dn_oth), keep_b, send_b = mlp_chunk(
        place,
        1,
        (normed_mlp, x_oth, dy_own, dy_oth),
        mlp_weights,
        [first_b, *rest_b],
        carried,
    )

    dn_arrived = links.core(dn_oth)
    stay_a, move_a = sum_one(keep_a, gate(arrived_a, dn_own))
    arrived_a = links.send_two(move_a)
    arrived_b = links.send_one(gate(send_b, *move_a))
    d_hidden, d_attn_t, mlp_gain_grad, halves_o, theirs_o = middle(
        place, hidden, dy_own, gains, dn_own, after(dn_arrived, *move_a), attn_t, out_full
    )
    total_a = links.sum_two(stay_a, gate(arrived_a, d_hidden))
    arrived_a = links.swap(total_a[1], df=2)
    arrived_o = links.core(theirs_o)
    dq_t, d_spans = attend_back(
        lows, q_t, attn_t, after(d_attn_t, *total_a), log_total, cosines, sines, spans
    )
    arrived = [
        links.later(value, d, -1) for value, d in zip(d_spans, range(n_ctx - 1, 0, -1))
    ]
    arrived_a, arrived_o, *arrived_b = gate([arrived_a, arrived_o, *arrived_b], dq_t)
    stay_b, move_b = sum_one(keep_b, arrived_b)
    total_b = links.sum_two(stay_b, links.send_two(move_b))
    left_a = add(total_a[0], arrived_a)
    arrived_a = links.send_z1(left_a)
    arrived_b = links.swap(total_b[1], df=2)
    input_grad, halves_q, theirs_q = last(
        place,
        x_in,
        gains,
        normed,
        after(dq_t, left_a, *total_b),
        cosines,
        sines,
        qkv_full,
        d_hidden,
        mlp_gain_grad,
        d_spans[-1],
        arrived,
    )
    arrived_a, arrived_b, arrived_o = gate([arrived_a, arrived_b, arrived_o], input_grad)
    halves_q = [add(value, more) for value, more in zip(halves_q, links.core(theirs_q))]
    halves_o = [add(value, more) for value, more in zip(halves_o, arrived_o)]

    def reduce_plane(halves):
        stay, move = sum_one(halves[:2], links.send_one(halves[2:]))
        return links.sum_two(stay, links.send_two(move))

    def reduce_z(total):
        left = add(total[0], links.swap(total[1], df=2))
        return sum_z1(left, links.send_z1(left))

    total_q = reduce_plane(halves_q)
    total_o = reduce_plane(halves_o)
    pairs_a = links.gather_pairs(sum_z1(left_a, arrived_a), 1)
    left_b = add(total_b[0], arrived_b)
    pairs_b = links.gather_pairs(sum_z1(left_b, links.send_z1(left_b)), 2)
    pairs_o = links.gather_pairs(reduce_z(total_o), 1)
    pairs_q = links.gather_pairs(reduce_z(total_q), 2)
    grad_gate_up, grad_down = finish_mlp(place, [*pairs_a, *pairs_b], (1, 2))
    (grad_out,) = finish_rows(place, pairs_o, 1, (D,))
    grad_qkv, gain_columns = finish_rows(place, pairs_q, 2, (QKV, QKV_WIDE - QKV))
    result = hidden + out_own + links.core(out_oth).astype(F32)
    return (
        result.astype(BF16).T[None],
        input_grad.T[None],
        gain_columns[:, 0],
        grad_qkv,
        grad_out,
        gain_columns[:, 1],
        grad_gate_up,
        grad_down.T,
    )


def solution(mesh):
    placed = (
        P(("seq", "fsdp"), "ctx", None),
        P(("seq", "fsdp"), "ctx", None),
        P(("seq", "fsdp"), "ctx"),
        P(("seq", "fsdp"), None),
        P("fsdp"),
        P("fsdp", None),
        P("fsdp", None),
        P("fsdp"),
        P("fsdp", None),
        P("fsdp", None),
    )
    links = Links([mesh.shape[name] for name in AXES])
    return jax.shard_map(
        functools.partial(shards, links),
        mesh=mesh,
        in_specs=placed,
        out_specs=(
            P(("seq", "fsdp"), "ctx", None),
            P(("seq", "fsdp"), "ctx", None),
            P("fsdp"),
            P("fsdp", None),
            P("fsdp", None),
            P("fsdp"),
            P("fsdp", None),
            P("fsdp", None),
        ),
        check_vma=False,
    )
```

```python
import functools

import jax
import jax.numpy as jnp
from jax import lax
from jax.experimental import pallas as pl
from jax.experimental.pallas import tpu as pltpu
from jax.sharding import PartitionSpec as P

D = 960
HEADS = 15
KV_HEADS = 5
HEAD_DIM = 64
FF = 2560
BLK = 128
TOK_DEV = 512
KV_DIM = 320
QKV = D + 2 * KV_DIM
QKV_WIDE = 1664
CUT = 896
EARLY_WIDE = 1920
FF_SHARD = FF // 4
ROWS = D // 4
ROWS_PAD = 256
SLICE = 32
TILE = 128
HALF = 64
ROW_TILE = 256
VMEM_LIMIT = 56 * 1024 * 1024

EPSILON = 1e-05
ROPE_BASE = 100000.0
MASKED_SCORE = -1e30
AXES = ("seq", "ctx", "fsdp")
F32 = jnp.float32
BF16 = jnp.bfloat16
ANY = pl.BlockSpec(memory_space=pl.ANY)
SMEM = pl.BlockSpec(memory_space=pltpu.SMEM)
VMEM = pl.BlockSpec(memory_space=pltpu.VMEM)
NT = (((1,), (1,)), ((), ()))
TN = (((0,), (0,)), ((), ()))


def frequencies():
    steps = jnp.arange(HEAD_DIM // 2, dtype=F32) * 2.0 / HEAD_DIM
    return ROPE_BASE ** (-steps)


def after(value, *earlier):
    return lax.optimization_barrier((value, *earlier))[0]


def gate(values, *earlier):
    return lax.optimization_barrier((*values, *earlier))[: len(values)]


def add(first, second):
    return (first.astype(F32) + second.astype(F32)).astype(BF16)


def sum_one(keep, arrived):
    pairs = list(zip(keep, arrived))
    stay = [value[0].astype(F32) + more[0].astype(F32) for value, more in pairs]
    return stay, [add(value[1], more[1]) for value, more in pairs]


def first_half(value):
    return value[: value.shape[0] // 2]


def second_half(value):
    return value[value.shape[0] // 2 :]


class Links:
    def __init__(self, sizes):
        self.sizes = sizes

    def index(self, s, c, f):
        return (s * self.sizes[1] + c) * self.sizes[2] + f

    def swap(self, value, ds=0, dc=0, df=0):
        n_s, n_c, n_f = self.sizes
        pairs = [
            (self.index(s, c, f), self.index(s ^ ds, c ^ dc, f ^ df))
            for s in range(n_s)
            for c in range(n_c)
            for f in range(n_f)
        ]
        return lax.ppermute(value, AXES, pairs)

    def later(self, value, blocks, sign):
        n_s, n_c, n_f = self.sizes
        pairs = []
        for s in range(n_s):
            for c in range(n_c - blocks):
                for f in range(n_f):
                    pair = (self.index(s, c, f), self.index(s, c + blocks, f))
                    pairs.append(pair if sign > 0 else pair[::-1])
        return lax.ppermute(value, AXES, pairs)

    def core(self, value):
        return self.swap(value, ds=1)

    def plane(self, value, bits):
        return self.swap(value, ds=bits & 2, dc=bits & 1)

    def gather_plane(self, own):
        return [own] + [self.plane(own, bits) for bits in (1, 2, 3)]

    def gather_z(self, own):
        return [self.swap(own, df=bits) for bits in (1, 2, 3)]

    def send_one(self, send):
        return [self.plane(value, bits) for value, bits in zip(send, (1, 2))]

    def send_two(self, move):
        return [self.plane(value, bits) for value, bits in zip(move, (2, 1))]

    def sum_two(self, stay, arrived):
        totals = [(value + more.astype(F32)).astype(BF16) for value, more in zip(stay, arrived)]
        step = 2
        while step < self.sizes[1]:
            totals = [add(value, self.swap(value, dc=step)) for value in totals]
            step *= 2
        return totals

    def gather_pairs(self, own, first):
        near = jnp.stack([own, self.plane(own, first)])
        far = self.plane(near, 3 - first)
        return near, far, self.core(near), self.core(far)


def piece_index(first, q):
    return (q & (3 - first)) // (3 - first), (q & first) // first


UNIT_TILES = (5, 3)
HIDDEN = (768, 512)
DOWN_AT = (3, 2)


def mlp_kernel(chunk, place, x_own, x_oth, dy_own, dy_oth, gate_up, w_down, halves, half_down, *rest):
    messages, rest = rest[:4], rest[4:]
    if chunk:
        carried, rest = rest[:2], rest[2:]
    results, (keep_x, keep_y, send_x, send_y), rest = rest[:4], rest[4:8], rest[8:]
    weight, drop, drop_half, act, dgu, units, x_t, dy_t, x, dy, out_t, dn_t, sems = rest
    hidden, down_at = HIDDEN[chunk], DOWN_AT[chunk]
    with_half = chunk == 0
    p, k, f = place[0], place[1], place[2]
    groups = ([], [], [])

    def copy(source, target, group):
        groups[group].append(pltpu.make_async_copy(source, target, sems.at[group]))

    for half, (xs, ds) in enumerate(((x_own, dy_own), (x_oth, dy_oth))):
        lanes = pl.ds(half * TOK_DEV, TOK_DEV)
        copy(xs, x_t.at[:, lanes], 0)
        copy(ds, dy_t.at[:, lanes], 1)
    if chunk:
        for source, target in zip(carried, (out_t, dn_t)):
            copy(source, target.at[:, pl.ds(TOK_DEV, TOK_DEV)], 1)
    tile_of_core = 2 * k + chunk
    for kind in range(2):
        for z in range(4):
            col = pl.multiple_of(kind * FF + z * FF_SHARD + tile_of_core * TILE, TILE)
            copy(
                gate_up.at[:, pl.ds(col, TILE)],
                weight.at[f, :, pl.ds(kind * hidden + z * TILE, TILE)],
                1,
            )
        if with_half:
            copy(
                halves.at[:, pl.ds(kind * 2 * TILE, 2 * TILE)],
                weight.at[f, :, pl.ds(kind * hidden + 4 * TILE, 2 * TILE)],
                1,
            )
    copy(
        w_down.at[:, pl.ds(pl.multiple_of(tile_of_core * TILE, TILE), TILE)],
        drop.at[:, pl.ds(pl.multiple_of(f * TILE, TILE), TILE)],
        1,
    )
    if with_half:
        copy(half_down, drop_half.at[f], 1)
    for q, ref in enumerate(messages):
        pp = jnp.bitwise_xor(p, q)
        for r in range(3):
            z = jnp.bitwise_xor(f, r + 1)
            rows = pl.ds(r * ROWS, ROWS)
            for kind in range(2):
                lane = pl.multiple_of(kind * hidden + pp * TILE, TILE)
                copy(
                    ref.at[rows, pl.ds(kind * TILE, TILE)],
                    weight.at[z, :, pl.ds(lane, TILE)],
                    1,
                )
            rows_at = pl.ds(pl.multiple_of(pp * ROWS, 16), ROWS)
            copy(
                ref.at[rows, pl.ds(down_at * TILE, TILE)],
                drop.at[rows_at, pl.ds(pl.multiple_of(z * TILE, TILE), TILE)],
                1,
            )
            if with_half:
                lane = jnp.right_shift(pp, 1) * hidden + 4 * TILE + jnp.bitwise_and(pp, 1) * TILE
                copy(
                    ref.at[rows, pl.ds(2 * TILE, TILE)],
                    weight.at[z, :, pl.ds(pl.multiple_of(lane, TILE), TILE)],
                    1,
                )
                copy(ref.at[rows, pl.ds(4 * TILE, TILE)], drop_half.at[z, rows_at], 1)
    for group in groups:
        for each in group:
            each.start()
    for each in groups[0]:
        each.wait()
    x[...] = x_t[...].T
    for each in groups[1]:
        each.wait()
    dy[...] = dy_t[...].T
    if with_half:
        for z in range(4):
            lane = 4 * TILE + z * HALF
            drop[:, lane : lane + HALF] = drop_half[z, :, :HALF]

    for t in range(2 * TOK_DEV // ROW_TILE):
        rows = slice(t * ROW_TILE, (t + 1) * ROW_TILE)
        both = weight[...].reshape(D, 2 * hidden)
        gu = jnp.dot(x[rows, :], both, preferred_element_type=F32)
        da = jnp.dot(dy[rows, :], drop[...], preferred_element_type=F32)
        g, u = gu[:, :hidden], gu[:, hidden:]
        sig = jax.nn.sigmoid(g)
        silu = g * sig
        a = (silu * u).astype(BF16)
        act[rows, :] = a
        dgu[rows, :hidden] = (da * u * (sig + silu * (1.0 - sig))).astype(BF16)
        dgu[rows, hidden:] = (da * silu).astype(BF16)
        out = lax.dot_general(drop[...], a, NT, preferred_element_type=F32)
        dn = lax.dot_general(both, dgu[rows, :], NT, preferred_element_type=F32)
        if chunk and t * ROW_TILE >= TOK_DEV:
            out = out + out_t[:, rows].astype(F32)
            dn = dn + dn_t[:, rows].astype(F32)
        out_t[:, rows] = out.astype(BF16)
        dn_t[:, rows] = dn.astype(BF16)

    groups = ([], [], [])
    for at, ref in enumerate((out_t, dn_t)):
        for half in range(2):
            copy(ref.at[:, pl.ds(half * TOK_DEV, TOK_DEV)], results[2 * at + half], 2)
    for each in groups[2]:
        each.start()

    step = 2 * TILE
    for start in range(0, hidden, step):
        grad = jnp.dot(
            dy_t[...], act[:, start : start + step], preferred_element_type=F32
        ).astype(BF16)
        if start < 4 * TILE:
            for part in range(2):
                z = start // TILE + part
                units[:, z, :, down_at * TILE : (down_at + 1) * TILE] = grad[
                    :, part * TILE : (part + 1) * TILE
                ].reshape(4, ROWS, TILE)
        else:
            for z in range(4):
                units[:, z, :, 4 * TILE : 4 * TILE + HALF] = grad[
                    :, z * HALF : (z + 1) * HALF
                ].reshape(4, ROWS, HALF)
    for pair in range(2):
        columns = [(kind * hidden + pair * step, kind) for kind in range(2)]
        if with_half:
            columns.append((pair * hidden + 4 * TILE, 2))
        for start, column in columns:
            grad = jnp.dot(
                x_t[...], dgu[:, start : start + step], preferred_element_type=F32
            ).astype(BF16)
            for part in range(2):
                units[2 * pair + part, :, :, column * TILE : (column + 1) * TILE] = grad[
                    :, part * TILE : (part + 1) * TILE
                ].reshape(4, ROWS, TILE)
        for pp in (2 * pair, 2 * pair + 1):
            q = jnp.bitwise_xor(p, pp)
            for bits in range(4):
                left = (keep_x, send_x)[bits & 1].at[bits >> 1]
                right = (keep_y, send_y)[bits >> 1].at[bits & 1]

                def send(pp=pp, left=left, right=right):
                    for r in range(4):
                        pltpu.make_async_copy(
                            units.at[pp, jnp.bitwise_xor(f, r)],
                            (left, right)[r & 1].at[pl.ds((r >> 1) * ROWS, ROWS)],
                            sems.at[2],
                        ).start()

                pl.when(q == bits)(send)
    for each in groups[2]:
        each.wait()
    for target in (keep_x, keep_y, send_x, send_y):
        for at in range(2):
            for r in range(2):
                pltpu.make_async_copy(
                    units.at[0, 0], target.at[at, pl.ds(r * ROWS, ROWS)], sems.at[2]
                ).wait()


def mlp_chunk(place, chunk, tokens, weights, messages, carried=()):
    hidden = HIDDEN[chunk]
    width = UNIT_TILES[chunk] * TILE
    part = jax.ShapeDtypeStruct((2, 2 * ROWS, width), BF16)
    operands = [place, *tokens, *weights, *messages, *carried]
    out = pl.pallas_call(
        functools.partial(mlp_kernel, chunk),
        out_shape=[jax.ShapeDtypeStruct((D, TOK_DEV), BF16)] * 4 + [part] * 4,
        in_specs=[SMEM] + [ANY] * (len(operands) - 1),
        out_specs=[ANY] * 8,
        scratch_shapes=[
            pltpu.VMEM((4, ROWS, 2 * hidden), BF16),
            pltpu.VMEM((D, hidden), BF16),
            pltpu.VMEM((4, D, TILE), BF16),
            pltpu.VMEM((2 * TOK_DEV, hidden), BF16),
            pltpu.VMEM((2 * TOK_DEV, 2 * hidden), BF16),
            pltpu.VMEM((4, 4, ROWS, width), BF16),
            pltpu.VMEM((D, 2 * TOK_DEV), BF16),
            pltpu.VMEM((D, 2 * TOK_DEV), BF16),
            pltpu.VMEM((2 * TOK_DEV, D), BF16),
            pltpu.VMEM((2 * TOK_DEV, D), BF16),
            pltpu.VMEM((D, 2 * TOK_DEV), BF16),
            pltpu.VMEM((D, 2 * TOK_DEV), BF16),
            pltpu.SemaphoreType.DMA((3,)),
        ],
        compiler_params=pltpu.CompilerParams(vmem_limit_bytes=VMEM_LIMIT),
        cost_estimate=pl.CostEstimate(
            flops=2 * 2 * TOK_DEV * D * hidden * 9, bytes_accessed=20_000_000, transcendentals=0
        ),
    )(*operands)
    return out[:4], out[4:6], out[6:8]


def finish_mlp_kernel(firsts, place, *refs):
    up, down = refs[-2:]
    p, k = place[0], place[1]
    for chunk, first in enumerate(firsts):
        pairs = refs[4 * chunk : 4 * chunk + 4]
        down_at = DOWN_AT[chunk]
        for q in range(4):
            pp = jnp.bitwise_xor(p, q)
            rows = pl.ds(pl.multiple_of(pp * ROWS, 16), ROWS)
            side, at = piece_index(first, q)
            for other in range(2):
                kk = jnp.bitwise_xor(k, other)
                ref = pairs[2 * other + side].at[at]
                for kind in range(2):
                    col = kind * FF + pp * FF_SHARD + (2 * kk + chunk) * TILE
                    up[:, pl.ds(pl.multiple_of(col, TILE), TILE)] = ref[
                        :, kind * TILE : (kind + 1) * TILE
                    ].astype(F32)
                col = pl.multiple_of((2 * kk + chunk) * TILE, TILE)
                down[rows, pl.ds(col, TILE)] = ref[
                    :, down_at * TILE : (down_at + 1) * TILE
                ].astype(F32)
            if chunk == 0:
                own, oth = (
                    pairs[2 * other + side][at, :, 2 * TILE : 3 * TILE] for other in range(2)
                )
                low = jnp.where(k == 0, own, oth).astype(F32)
                high = jnp.where(k == 0, oth, own).astype(F32)
                for half in range(2):
                    lanes = slice(half * HALF, (half + 1) * HALF)
                    z = 2 * jnp.bitwise_and(pp, 1) + half
                    col = jnp.right_shift(pp, 1) * FF + z * FF_SHARD + 4 * TILE
                    up[:, pl.ds(pl.multiple_of(col, TILE), TILE)] = jnp.concatenate(
                        [low[:, lanes], high[:, lanes]], axis=1
                    )
                own, oth = (
                    pairs[2 * other + side][at, :, 4 * TILE : 4 * TILE + HALF].astype(F32)
                    for other in range(2)
                )
                low, high = jnp.where(k == 0, own, oth), jnp.where(k == 0, oth, own)
                down[rows, 4 * TILE :] = jnp.concatenate([low, high], axis=1)


def finish_mlp(place, pieces, firsts):
    return pl.pallas_call(
        functools.partial(finish_mlp_kernel, firsts),
        out_shape=[
            jax.ShapeDtypeStruct((ROWS, 2 * FF), F32),
            jax.ShapeDtypeStruct((D, FF_SHARD), F32),
        ],
        in_specs=[SMEM] + [VMEM] * len(pieces),
        out_specs=[VMEM] * 2,
        compiler_params=pltpu.CompilerParams(vmem_limit_bytes=VMEM_LIMIT),
        cost_estimate=pl.CostEstimate(flops=0, bytes_accessed=24_000_000, transcendentals=0),
    )(place, *pieces)


def load_rows(place, own, mine, theirs, full, sem):
    p, k, f = place[0], place[1], place[2]
    for start in (True, False):

        def run(copy, start=start):
            if start:
                copy.start()
            else:
                copy.wait()

        run(pltpu.make_async_copy(own, full.at[f], sem))
        for other in range(2):
            kk = jnp.bitwise_xor(k, other)
            for q in range(4):
                ref = theirs.at[q] if other else mine[q]
                pp = jnp.bitwise_xor(p, q)
                row = pl.multiple_of(kk * 128 + pp * SLICE, 16)
                short = (kk * 4 + pp) == 7
                for r in range(3):
                    z = jnp.bitwise_xor(f, r + 1)

                    def go(count, ref=ref, r=r, z=z, row=row):
                        run(
                            pltpu.make_async_copy(
                                ref.at[r, pl.ds(0, count)], full.at[z, pl.ds(row, count)], sem
                            )
                        )

                    pl.when(short)(functools.partial(go, 16))
                    pl.when(jnp.logical_not(short))(functools.partial(go, SLICE))


def store_rows(place, grad, halves, theirs, sem):
    p, k, f = place[0], place[1], place[2]
    keep_x, keep_y, send_x, send_y = halves
    for start in (True, False):
        for other in range(2):
            kk = jnp.bitwise_xor(k, other)
            for q in range(4):
                pp = jnp.bitwise_xor(p, q)
                row = pl.multiple_of(kk * 128 + pp * SLICE, 16)
                short = (kk * 4 + pp) == 7
                left = (keep_x, send_x)[q & 1].at[q >> 1]
                right = (keep_y, send_y)[q >> 1].at[q & 1]
                for r in range(4):
                    z = jnp.bitwise_xor(f, r)
                    if not other:
                        target = (left, right)[r & 1]
                    elif r & 1 == 0:
                        target = theirs.at[2 * (q & 1), q >> 1]
                    else:
                        target = theirs.at[1 + 2 * (q >> 1), q & 1]
                    target = target.at[pl.ds((r >> 1) * SLICE, SLICE)]

                    def go(count, target=target, z=z, row=row):
                        copy = pltpu.make_async_copy(
                            grad.at[z, pl.ds(row, count)], target.at[pl.ds(0, count)], sem
                        )
                        if start:
                            copy.start()
                        else:
                            copy.wait()

                    pl.when(short)(functools.partial(go, 16))
                    pl.when(jnp.logical_not(short))(functools.partial(go, SLICE))


def finish_rows_kernel(firsts, place, *refs):
    qkv, out, gain = refs[8:]
    p, k = place[0], place[1]
    for other in range(2):
        kk = jnp.bitwise_xor(k, other)
        for q in range(4):
            pp = jnp.bitwise_xor(p, q)
            row = pl.multiple_of(kk * 128 + pp * SLICE, 16)
            short = (kk * 4 + pp) == 7
            values = []
            for at, first in enumerate(firsts):
                side, index = piece_index(first, q)
                values.append(refs[4 * at + 2 * other + side][index].astype(F32))

            def go(count, values=values, row=row):
                rows = pl.ds(row, count)
                before, behind = values
                qkv[rows, :CUT] = before[:count, :CUT]
                qkv[rows, CUT:] = behind[:count, : QKV - CUT]
                out[rows, :] = before[:count, CUT : CUT + D]
                gain[rows, : QKV_WIDE - QKV] = behind[:count, QKV - CUT :]

            pl.when(short)(functools.partial(go, 16))
            pl.when(jnp.logical_not(short))(functools.partial(go, SLICE))


def finish_rows(place, pairs, firsts):
    return pl.pallas_call(
        functools.partial(finish_rows_kernel, firsts),
        out_shape=[jax.ShapeDtypeStruct((ROWS, width), F32) for width in (QKV, D, TILE)],
        in_specs=[SMEM] + [VMEM] * 8,
        out_specs=[VMEM] * 3,
        compiler_params=pltpu.CompilerParams(vmem_limit_bytes=VMEM_LIMIT),
        cost_estimate=pl.CostEstimate(
            flops=0, bytes_accessed=6 * ROWS * (QKV + D), transcendentals=0
        ),
    )(place, *pairs)


def token_scale(values):
    return lax.rsqrt(jnp.mean(values * values, axis=0, keepdims=True) + EPSILON)


def tables_kernel(positions, frequency, cosines, sines):
    angles = frequency[:, :1] * positions[...].astype(F32)
    cosines[...] = jnp.cos(angles)
    sines[...] = jnp.sin(angles)


def tables(positions):
    frequency = jnp.broadcast_to(frequencies()[:, None], (HEAD_DIM // 2, TILE))
    return pl.pallas_call(
        tables_kernel,
        out_shape=[jax.ShapeDtypeStruct((HEAD_DIM // 2, TOK_DEV), F32)] * 2,
        in_specs=[VMEM] * 2,
        out_specs=[VMEM] * 2,
        cost_estimate=pl.CostEstimate(
            flops=20_000_000_000, bytes_accessed=200_000, transcendentals=32_768
        ),
    )(positions, frequency)


def project_kernel(
    place, x, cosines, sines, own, m0, m1, m2, m3, theirs, full, gains, normed, q_t, kv, sem
):
    load_rows(place, own, (m0, m1, m2, m3), theirs, full, sem)
    weight = full[...].reshape(D, QKV_WIDE)
    columns = weight[:, QKV - HALF :].astype(F32)
    gains[...] = columns
    source = x[...].astype(F32)
    normed[...] = (source * token_scale(source) * columns[:, HALF : HALF + 1]).astype(BF16)
    mixed = lax.dot_general(weight[:, :QKV], normed[...], TN, preferred_element_type=F32)
    cos, sin = cosines[...], sines[...]
    half = HEAD_DIM // 2
    for head in range(HEADS + KV_HEADS):
        row = head * HEAD_DIM
        low, high = mixed[row : row + half], mixed[row + half : row + HEAD_DIM]
        low, high = (low * cos - high * sin).astype(BF16), (high * cos + low * sin).astype(BF16)
        if head < HEADS:
            q_t[row : row + half, :] = low
            q_t[row + half : row + HEAD_DIM, :] = high
        else:
            row -= D
            for block in range(TOK_DEV // BLK):
                lanes = slice(block * BLK, (block + 1) * BLK)
                kv[block, row : row + half, :] = low[:, lanes]
                kv[block, row + half : row + HEAD_DIM, :] = high[:, lanes]
    for block in range(TOK_DEV // BLK):
        lanes = slice(block * BLK, (block + 1) * BLK)
        kv[block, KV_DIM:, :] = mixed[D + KV_DIM :, lanes].astype(BF16)


def project(place, x, cosines, sines, own, mine, theirs):
    return pl.pallas_call(
        project_kernel,
        out_shape=[
            jax.ShapeDtypeStruct((4, ROWS, QKV_WIDE), BF16),
            jax.ShapeDtypeStruct((D, TILE), F32),
            jax.ShapeDtypeStruct((D, TOK_DEV), BF16),
            jax.ShapeDtypeStruct((D, TOK_DEV), BF16),
            jax.ShapeDtypeStruct((TOK_DEV // BLK, 2 * KV_DIM, BLK), BF16),
        ],
        in_specs=[SMEM] + [VMEM] * 3 + [ANY] * 6,
        out_specs=[VMEM] * 5,
        scratch_shapes=[pltpu.SemaphoreType.DMA(())],
        compiler_params=pltpu.CompilerParams(vmem_limit_bytes=VMEM_LIMIT),
        cost_estimate=pl.CostEstimate(
            flops=2 * TOK_DEV * D * QKV, bytes_accessed=10_000_000, transcendentals=0
        ),
    )(place, x, cosines, sines, own, *mine, theirs)


def three_heads(ref, group, lanes):
    first = group * (HEADS // KV_HEADS) * HEAD_DIM
    return jnp.concatenate(
        [
            ref[first + r * HEAD_DIM : first + (r + 1) * HEAD_DIM, lanes]
            for r in range(HEADS // KV_HEADS)
        ],
        axis=1,
    )


def diagonal_mask():
    shape = (BLK, BLK * (HEADS // KV_HEADS))
    keys = lax.broadcasted_iota(jnp.int32, shape, 0)
    queries = jnp.bitwise_and(lax.broadcasted_iota(jnp.int32, shape, 1), BLK - 1)
    return keys <= queries


def attend_kernel(lows, q_t, *rest):
    spans = rest[:-6]
    attn_t, log_total, kv, best, total, accum = rest[-6:]
    blocks = TOK_DEV // BLK
    for at, ref in enumerate(spans):
        kv[at * blocks : (at + 1) * blocks] = ref[...]
    own_at = (len(spans) - 1) * blocks
    mask = diagonal_mask()
    for i in range(blocks):
        lanes = slice(i * BLK, (i + 1) * BLK)
        queries = [
            three_heads(q_t, group, lanes) * jnp.asarray(HEAD_DIM**-0.5, BF16)
            for group in range(KV_HEADS)
        ]

        def step(j, diagonal, queries=queries):
            for group in range(KV_HEADS):
                keys = kv[j, group * HEAD_DIM : (group + 1) * HEAD_DIM, :]
                values = kv[j, KV_DIM + group * HEAD_DIM : KV_DIM + (group + 1) * HEAD_DIM, :]
                scores = lax.dot_general(keys, queries[group], TN, preferred_element_type=F32)
                if diagonal:
                    scores = jnp.where(mask, scores, MASKED_SCORE)
                    top = jnp.max(scores, axis=0, keepdims=True)
                    expo = jnp.exp(scores - top)
                    total[group] = jnp.sum(expo, axis=0, keepdims=True)
                    accum[group] = jnp.dot(values, expo.astype(BF16), preferred_element_type=F32)
                else:
                    old = best[group]
                    top = jnp.maximum(old, jnp.max(scores, axis=0, keepdims=True))
                    decay = jnp.exp(old - top)
                    expo = jnp.exp(scores - top)
                    total[group] = total[group] * decay + jnp.sum(expo, axis=0, keepdims=True)
                    accum[group] = accum[group] * decay + jnp.dot(
                        values, expo.astype(BF16), preferred_element_type=F32
                    )
                best[group] = top

        step(own_at + i, True)

        @pl.loop(lows[i], own_at + i)
        def earlier(j):
            step(j, False)

        for group in range(KV_HEADS):
            attn = (accum[group] / total[group]).astype(BF16)
            first = group * (HEADS // KV_HEADS) * HEAD_DIM
            for r in range(HEADS // KV_HEADS):
                attn_t[first + r * HEAD_DIM : first + (r + 1) * HEAD_DIM, lanes] = attn[
                    :, r * BLK : (r + 1) * BLK
                ]
            log_total[i * KV_HEADS + group] = best[group] + jnp.log(total[group])


def attend(lows, q_t, spans):
    blocks = TOK_DEV // BLK
    wide = BLK * (HEADS // KV_HEADS)
    return pl.pallas_call(
        attend_kernel,
        out_shape=[
            jax.ShapeDtypeStruct((D, TOK_DEV), BF16),
            jax.ShapeDtypeStruct((blocks * KV_HEADS, 1, wide), F32),
        ],
        in_specs=[SMEM] + [VMEM] * (1 + len(spans)),
        out_specs=[VMEM] * 2,
        scratch_shapes=[
            pltpu.VMEM((len(spans) * blocks, 2 * KV_DIM, BLK), BF16),
            pltpu.VMEM((KV_HEADS, 1, wide), F32),
            pltpu.VMEM((KV_HEADS, 1, wide), F32),
            pltpu.VMEM((KV_HEADS, HEAD_DIM, wide), F32),
        ],
        compiler_params=pltpu.CompilerParams(vmem_limit_bytes=VMEM_LIMIT),
        cost_estimate=pl.CostEstimate(
            flops=8_000_000_000, bytes_accessed=4_000_000, transcendentals=2_000_000
        ),
    )(lows, q_t, *spans)


def out_kernel(place, x, gains, attn_t, own, m0, m1, m2, m3, theirs, full, hidden, normed, sem):
    load_rows(place, own, (m0, m1, m2, m3), theirs, full, sem)
    value = x[...].astype(F32) + lax.dot_general(
        full[...].reshape(D, D), attn_t[...], TN, preferred_element_type=F32
    )
    hidden[...] = value
    normed[...] = (value * token_scale(value) * gains[:, HALF + 1 : HALF + 2]).astype(BF16)


def project_out(place, x, gains, attn_t, own, mine, theirs):
    return pl.pallas_call(
        out_kernel,
        out_shape=[
            jax.ShapeDtypeStruct((4, ROWS, D), BF16),
            jax.ShapeDtypeStruct((D, TOK_DEV), F32),
            jax.ShapeDtypeStruct((D, TOK_DEV), BF16),
        ],
        in_specs=[SMEM] + [VMEM] * 3 + [ANY] * 6,
        out_specs=[VMEM] * 3,
        scratch_shapes=[pltpu.SemaphoreType.DMA(())],
        compiler_params=pltpu.CompilerParams(vmem_limit_bytes=VMEM_LIMIT),
        cost_estimate=pl.CostEstimate(
            flops=2 * TOK_DEV * D * D, bytes_accessed=8_000_000, transcendentals=0
        ),
    )(place, x, gains, attn_t, own, *mine, theirs)


def norm_back(value, scale, gain, dn):
    unit = value * scale
    weighted = dn * gain
    d_value = scale * (weighted - unit * jnp.mean(weighted * unit, axis=0, keepdims=True))
    return d_value, jnp.sum(dn * unit, axis=1, keepdims=True)


def middle_kernel(
    hidden, dy, gains, dn0, dn1, dn2, full, d_hidden, d_hidden_b, d_attn_t, grad_gain
):
    value = hidden[...]
    dn = dn0[...].astype(F32) + dn1[...].astype(F32) + dn2[...].astype(F32)
    d_value, column = norm_back(value, token_scale(value), gains[:, HALF + 1 : HALF + 2], dn)
    grad_gain[...] = jnp.broadcast_to(column, (D, TILE))
    dh = dy[...].astype(F32) + d_value
    d_hidden[...] = dh
    dh = dh.astype(BF16)
    d_hidden_b[...] = dh
    d_attn_t[...] = jnp.dot(
        full[...].reshape(D, D), dh, preferred_element_type=F32
    ).astype(BF16)


def middle(hidden, dy, gains, dns, full):
    return pl.pallas_call(
        middle_kernel,
        out_shape=[
            jax.ShapeDtypeStruct((D, TOK_DEV), F32),
            jax.ShapeDtypeStruct((D, TOK_DEV), BF16),
            jax.ShapeDtypeStruct((D, TOK_DEV), BF16),
            jax.ShapeDtypeStruct((D, TILE), F32),
        ],
        in_specs=[VMEM] * 7,
        out_specs=[VMEM] * 4,
        compiler_params=pltpu.CompilerParams(vmem_limit_bytes=VMEM_LIMIT),
        cost_estimate=pl.CostEstimate(
            flops=2 * TOK_DEV * D * D, bytes_accessed=14_000_000, transcendentals=0
        ),
    )(hidden, dy, gains, *dns, full)


def attend_back_kernel(count, lows, q_t, attn_t, d_attn_t, log_total, cosines, sines, *rest):
    spans, rest = rest[:count], rest[count:]
    dq_t, d_spans, (kv, d_kv, d_query) = rest[0], rest[1 : 1 + count], rest[1 + count :]
    blocks = TOK_DEV // BLK
    groups = HEADS // KV_HEADS
    half = HEAD_DIM // 2
    for at, ref in enumerate(spans):
        kv[at * blocks : (at + 1) * blocks] = ref[...]
    d_kv[...] = jnp.zeros_like(d_kv)
    own_at = (count - 1) * blocks
    mask = diagonal_mask()
    for i in range(blocks):
        lanes = slice(i * BLK, (i + 1) * BLK)
        queries, d_outs, deltas = [], [], []
        for group in range(KV_HEADS):
            queries.append(three_heads(q_t, group, lanes) * jnp.asarray(HEAD_DIM**-0.5, BF16))
            d_out = three_heads(d_attn_t, group, lanes)
            attn = three_heads(attn_t, group, lanes)
            d_outs.append(d_out)
            deltas.append(
                jnp.sum(d_out.astype(F32) * attn.astype(F32), axis=0, keepdims=True)
            )

        def step(j, diagonal, i=i, queries=queries, d_outs=d_outs, deltas=deltas):
            for group in range(KV_HEADS):
                key_rows = slice(group * HEAD_DIM, (group + 1) * HEAD_DIM)
                value_rows = slice(KV_DIM + group * HEAD_DIM, KV_DIM + (group + 1) * HEAD_DIM)
                keys, values = kv[j, key_rows, :], kv[j, value_rows, :]
                scores = lax.dot_general(keys, queries[group], TN, preferred_element_type=F32)
                if diagonal:
                    scores = jnp.where(mask, scores, MASKED_SCORE)
                prob = jnp.exp(scores - log_total[i * KV_HEADS + group])
                d_prob = lax.dot_general(values, d_outs[group], TN, preferred_element_type=F32)
                d_scores = (prob * (d_prob - deltas[group])).astype(BF16)
                d_kv[j, value_rows, :] += lax.dot_general(
                    d_outs[group], prob.astype(BF16), NT, preferred_element_type=F32
                )
                d_kv[j, key_rows, :] += lax.dot_general(
                    queries[group], d_scores, NT, preferred_element_type=F32
                )
                more = jnp.dot(keys, d_scores, preferred_element_type=F32)
                if diagonal:
                    d_query[group] = more
                else:
                    d_query[group] += more

        step(own_at + i, True)

        @pl.loop(lows[i], own_at + i)
        def earlier(j):
            step(j, False)

        cos, sin = cosines[:, lanes], sines[:, lanes]
        for group in range(KV_HEADS):
            for r in range(groups):
                row = (group * groups + r) * HEAD_DIM
                side = slice(r * BLK, (r + 1) * BLK)
                low = d_query[group, :half, side] * HEAD_DIM**-0.5
                high = d_query[group, half:, side] * HEAD_DIM**-0.5
                dq_t[row : row + half, lanes] = (low * cos + high * sin).astype(BF16)
                dq_t[row + half : row + HEAD_DIM, lanes] = (high * cos - low * sin).astype(BF16)
    for at, ref in enumerate(d_spans):
        ref[...] = d_kv[at * blocks : (at + 1) * blocks].astype(ref.dtype)


def attend_back(lows, q_t, attn_t, d_attn_t, log_total, cosines, sines, spans):
    blocks = TOK_DEV // BLK
    wide = BLK * (HEADS // KV_HEADS)
    count = len(spans)
    shape = (blocks, 2 * KV_DIM, BLK)
    out = pl.pallas_call(
        functools.partial(attend_back_kernel, count),
        out_shape=[jax.ShapeDtypeStruct((D, TOK_DEV), BF16)]
        + [jax.ShapeDtypeStruct(shape, BF16)] * (count - 1)
        + [jax.ShapeDtypeStruct(shape, F32)],
        in_specs=[SMEM] + [VMEM] * (6 + count),
        out_specs=[VMEM] * (1 + count),
        scratch_shapes=[
            pltpu.VMEM((count * blocks, 2 * KV_DIM, BLK), BF16),
            pltpu.VMEM((count * blocks, 2 * KV_DIM, BLK), F32),
            pltpu.VMEM((KV_HEADS, HEAD_DIM, wide), F32),
        ],
        compiler_params=pltpu.CompilerParams(vmem_limit_bytes=VMEM_LIMIT),
        cost_estimate=pl.CostEstimate(
            flops=16_000_000_000, bytes_accessed=8_000_000, transcendentals=2_000_000
        ),
    )(lows, q_t, attn_t, d_attn_t, log_total, cosines, sines, *spans)
    return out[0], out[1:]


def early_kernel(place, normed, dq_t, attn_t, dh, *rest):
    halves, theirs, grad, sem = rest[:4], rest[4], rest[5], rest[6]
    product = lax.dot_general(attn_t[...], dh[...], NT, preferred_element_type=F32)
    grad[:, :, CUT : CUT + D] = product.astype(BF16).reshape(4, ROWS, D)
    product = lax.dot_general(normed[...], dq_t[:CUT, :], NT, preferred_element_type=F32)
    grad[:, :, :CUT] = product.astype(BF16).reshape(4, ROWS, CUT)
    store_rows(place, grad, halves, theirs, sem)


def early(place, normed, dq_t, attn_t, dh):
    piece = jax.ShapeDtypeStruct((2, 2 * SLICE, EARLY_WIDE), BF16)
    out = pl.pallas_call(
        early_kernel,
        out_shape=[*[piece] * 4, jax.ShapeDtypeStruct((4, 2, 2 * SLICE, EARLY_WIDE), BF16)],
        in_specs=[SMEM] + [VMEM] * 4,
        out_specs=[ANY] * 5,
        scratch_shapes=[pltpu.VMEM((4, ROWS, EARLY_WIDE), BF16), pltpu.SemaphoreType.DMA(())],
        compiler_params=pltpu.CompilerParams(vmem_limit_bytes=VMEM_LIMIT),
        cost_estimate=pl.CostEstimate(
            flops=2 * TOK_DEV * D * EARLY_WIDE, bytes_accessed=8_000_000, transcendentals=0
        ),
    )(place, normed, dq_t, attn_t, dh)
    return out[:4], out[4]


def last_kernel(
    count, place, x, gains, normed, dq_t, cosines, sines, full, d_hidden, mlp_gain_grad, d_own, *rest
):
    arrived, rest = rest[:count], rest[count:]
    input_grad, halves, theirs, d_mixed, grad, sem = rest[0], rest[1:5], rest[5], *rest[6:]
    half = HEAD_DIM // 2
    d_mixed[:D, :] = dq_t[...]
    for block in range(TOK_DEV // BLK):
        lanes = slice(block * BLK, (block + 1) * BLK)
        value = d_own[block]
        for ref in arrived:
            value = value + ref[block].astype(F32)
        cos, sin = cosines[:, lanes], sines[:, lanes]
        for head in range(KV_HEADS):
            row = head * HEAD_DIM
            low, high = value[row : row + half], value[row + half : row + HEAD_DIM]
            d_mixed[D + row : D + row + half, lanes] = (low * cos + high * sin).astype(BF16)
            d_mixed[D + row + half : D + row + HEAD_DIM, lanes] = (high * cos - low * sin).astype(
                BF16
            )
        d_mixed[D + KV_DIM :, lanes] = value[KV_DIM:].astype(BF16)
    product = lax.dot_general(normed[...], d_mixed[CUT:, :], NT, preferred_element_type=F32)
    grad[:, :, : QKV - CUT] = product.astype(BF16).reshape(4, ROWS, QKV - CUT)
    weight = full[...].reshape(D, QKV_WIDE)[:, :QKV]
    dn = jnp.dot(weight, d_mixed[...], preferred_element_type=F32)
    source = x[...].astype(F32)
    d_value, column = norm_back(source, token_scale(source), gains[:, HALF : HALF + 1], dn)
    input_grad[...] = (d_hidden[...] + d_value).astype(BF16)
    lane = lax.broadcasted_iota(jnp.int32, (D, QKV_WIDE - QKV), 1)
    both = jnp.where(lane == 0, column, mlp_gain_grad[:, : QKV_WIDE - QKV])
    grad[:, :, QKV - CUT :] = both.astype(BF16).reshape(4, ROWS, QKV_WIDE - QKV)
    store_rows(place, grad, halves, theirs, sem)


def last(place, x, gains, normed, dq_t, cosines, sines, full, d_hidden, mlp_gain_grad, d_own, arrived):
    width = QKV_WIDE - CUT
    piece = jax.ShapeDtypeStruct((2, 2 * SLICE, width), BF16)
    out = pl.pallas_call(
        functools.partial(last_kernel, len(arrived)),
        out_shape=[
            jax.ShapeDtypeStruct((D, TOK_DEV), BF16),
            *[piece] * 4,
            jax.ShapeDtypeStruct((4, 2, 2 * SLICE, width), BF16),
        ],
        in_specs=[SMEM] + [VMEM] * (10 + len(arrived)),
        out_specs=[VMEM] + [ANY] * 5,
        scratch_shapes=[
            pltpu.VMEM((QKV, TOK_DEV), BF16),
            pltpu.VMEM((4, ROWS, width), BF16),
            pltpu.SemaphoreType.DMA(()),
        ],
        compiler_params=pltpu.CompilerParams(vmem_limit_bytes=VMEM_LIMIT),
        cost_estimate=pl.CostEstimate(
            flops=4 * TOK_DEV * D * QKV, bytes_accessed=14_000_000, transcendentals=0
        ),
    )(place, x, gains, normed, dq_t, cosines, sines, full, d_hidden, mlp_gain_grad, d_own, *arrived)
    return out[0], out[1:5], out[5]


def shards(
    links,
    tokens,
    cotangent,
    positions,
    doc_ids,
    gain_attn,
    w_qkv,
    w_out,
    gain_mlp,
    w_gate_up,
    w_down,
):
    seq_at, ctx_at, f = (lax.axis_index(name) for name in AXES)
    k = jnp.bitwise_and(seq_at, 1)
    p = 2 * jnp.right_shift(seq_at, 1) + jnp.bitwise_and(ctx_at, 1)
    place = jnp.stack([p, k, f]).astype(jnp.int32)
    n_ctx = links.sizes[1]
    x_in, dy_own = tokens[0].T, cotangent[0].T

    def row_slice(weight):
        padded = jnp.pad(weight, ((0, ROWS_PAD - ROWS), (0, 0)))
        return lax.dynamic_slice_in_dim(padded, k * 128 + p * SLICE, SLICE, 0)

    pair = jnp.stack([gain_attn, gain_mlp], axis=1)
    gain_columns = jnp.pad(pair, ((0, 0), (0, QKV_WIDE - QKV - 2)))
    qkv_own = jnp.concatenate([w_qkv, gain_columns], axis=1)
    qkv_slice = jnp.concatenate([row_slice(w_qkv), row_slice(gain_columns)], axis=1)
    out_slice = row_slice(w_out)
    qkv_z = links.gather_z(qkv_slice)
    far_o = links.swap(out_slice, df=2)
    far_o, *qkv_z = gate([far_o, *qkv_z])
    qkv_mine = links.gather_plane(jnp.stack(qkv_z))
    pair_o = jnp.stack([out_slice, far_o])
    near_o = links.swap(pair_o, df=1)
    cosines, sines = tables(after(positions, *qkv_z))
    near_o, *qkv_mine = gate([near_o, *qkv_mine], cosines)
    blocks = TOK_DEV // BLK
    docs = doc_ids[0]
    own_docs = lax.dynamic_slice_in_dim(docs, ctx_at * blocks, blocks)
    lows = jnp.sum((docs[None, :] < own_docs[:, None]).astype(jnp.int32), axis=1)
    lows = lows + (n_ctx - 1 - ctx_at) * blocks
    qkv_theirs = links.core(jnp.stack(qkv_mine))
    out_z = jnp.stack([near_o[0], far_o, near_o[1]])
    out_mine = links.gather_plane(out_z)

    def core_half(pair):
        return jnp.where(k == 0, pair[:, :HALF], pair[:, HALF:])

    halves = jnp.concatenate(
        [core_half(w_gate_up[:, at : at + TILE]) for at in range(4 * TILE, 2 * FF, FF_SHARD)],
        axis=1,
    )
    down_t = w_down.T
    half_down = jnp.pad(core_half(down_t[:, 4 * TILE :]), ((0, 0), (0, HALF)))

    def unit(chunk):
        tiles = []
        for kind in range(2):
            col = kind * FF + p * FF_SHARD + (2 * k + chunk) * TILE
            tiles.append(lax.dynamic_slice_in_dim(w_gate_up, col, TILE, 1))
        if chunk == 0:
            tiles.append(lax.dynamic_slice_in_dim(halves, p * TILE, TILE, 1))
        tiles.append(
            lax.dynamic_slice(down_t, (p * ROWS, (2 * k + chunk) * TILE), (ROWS, TILE))
        )
        if chunk == 0:
            tiles.append(lax.dynamic_slice_in_dim(half_down, p * ROWS, ROWS, 0))
        return jnp.concatenate(tiles, axis=1)

    def three_z(own, far, near):
        return jnp.concatenate([first_half(near), far, second_half(near)], axis=0)

    unit_a, unit_b = unit(0), unit(1)
    far_a = links.swap(after(unit_a, *qkv_z), df=2)
    (far_a,) = gate([far_a], cosines)
    pair_a = jnp.concatenate([unit_a, far_a], axis=0)
    near_a = links.swap(pair_a, df=1)

    qkv_full, gains, normed, q_t, kv = project(
        place, x_in, cosines, sines, after(qkv_own, pair_a, out_z), qkv_mine, qkv_theirs
    )
    spans = [links.later(kv, d, 1) for d in range(n_ctx - 1, 0, -1)] + [kv]
    far_a, near_a, *out_mine = gate([far_a, near_a, *out_mine], kv)
    out_theirs = links.core(jnp.stack(out_mine))
    first_a = three_z(unit_a, far_a, near_a)
    rest_a = [links.plane(first_a, bits) for bits in (1, 2, 3)]
    far_b = links.swap(after(unit_b, first_a), df=2)
    attn_t, log_total = attend(lows, after(q_t, first_a), spans)
    far_b, out_theirs, *rest_a = gate([far_b, out_theirs, *rest_a], attn_t)
    pair_b = jnp.concatenate([unit_b, far_b], axis=0)
    near_b = links.swap(pair_b, df=1)
    dy_oth = links.core(dy_own)
    out_full, hidden, normed_mlp = project_out(
        place, x_in, gains, after(attn_t, pair_b), w_out, out_mine, out_theirs
    )

    x_oth = links.core(normed_mlp)
    near_b, *rest_a = gate([near_b, *rest_a], hidden)
    first_b = three_z(unit_b, far_b, near_b)
    rest_b = [links.plane(first_b, bits) for bits in (1, 2, 3)]
    mlp_weights = (w_gate_up, down_t, halves, half_down)
    tokens_mlp = (after(normed_mlp, first_b), x_oth, dy_own, dy_oth)
    results_a, keep_a, send_a = mlp_chunk(
        place, 0, tokens_mlp, mlp_weights, [first_a, *rest_a]
    )
    arrived_a = links.send_one(send_a)
    rest_b = gate(rest_b, results_a[0])
    results_b, keep_b, send_b = mlp_chunk(
        place,
        1,
        (normed_mlp, x_oth, dy_own, dy_oth),
        mlp_weights,
        [first_b, *rest_b],
        (results_a[1], results_a[3]),
    )

    dn_oth = links.core(results_b[3])
    stay_a, move_a = sum_one(keep_a, gate(arrived_a, results_b[2]))
    arrived_a = links.send_two(move_a)
    arrived_b = links.send_one(gate(send_b, *move_a))
    d_hidden, d_hidden_b, d_attn_t, mlp_gain_grad = middle(
        hidden,
        dy_own,
        gains,
        (results_a[2], after(results_b[2], *move_a), dn_oth),
        out_full,
    )
    total_a = links.sum_two(stay_a, gate(arrived_a, d_hidden))
    arrived_a = links.swap(total_a[1], df=1)
    dq_t, d_spans = attend_back(
        lows, q_t, attn_t, after(d_attn_t, *total_a), log_total, cosines, sines, spans
    )
    arrived = [
        links.later(value, d, -1) for value, d in zip(d_spans, range(n_ctx - 1, 0, -1))
    ]
    arrived_a, *arrived_b = gate([arrived_a, *arrived_b], dq_t)
    stay_b, move_b = sum_one(keep_b, arrived_b)
    arrived_b = links.send_two(move_b)
    left_a = add(total_a[0], arrived_a)
    arrived_a = links.swap(second_half(left_a), df=2)
    halves_o, theirs_o = early(place, normed, after(dq_t, left_a, *move_b), attn_t, d_hidden_b)
    arrived_o = links.core(theirs_o)
    arrived_b = gate(arrived_b, halves_o[0])
    halves_o = [add(value, more) for value, more in zip(halves_o, arrived_o)]
    arrived_o = links.send_one(halves_o[2:])
    total_b = links.sum_two(stay_b, arrived_b)
    arrived_b = links.swap(total_b[1], df=1)
    input_grad, halves_q, theirs_q = last(
        place,
        x_in,
        gains,
        normed,
        after(dq_t, *total_b, *halves_o),
        cosines,
        sines,
        qkv_full,
        d_hidden,
        mlp_gain_grad,
        d_spans[-1],
        arrived,
    )
    arrived_q = links.core(theirs_q)
    arrived_a, arrived_b, *arrived_o = gate([arrived_a, arrived_b, *arrived_o], input_grad)
    total_a = add(first_half(left_a), arrived_a)
    halves_q = [add(value, more) for value, more in zip(halves_q, arrived_q)]
    arrived_q = links.send_one(halves_q[2:])
    stay_o, move_o = sum_one(halves_o[:2], arrived_o)
    total_o = links.sum_two(stay_o, links.send_two(move_o))
    stay_q, move_q = sum_one(halves_q[:2], arrived_q)
    total_q = links.sum_two(stay_q, links.send_two(move_q))
    left_b = add(total_b[0], arrived_b)
    total_b = add(first_half(left_b), links.swap(second_half(left_b), df=2))

    def reduce_z(total):
        left = add(total[0], links.swap(total[1], df=1))
        return add(first_half(left), links.swap(second_half(left), df=2))

    pairs_a = links.gather_pairs(total_a, 1)
    pairs_b = links.gather_pairs(total_b, 2)
    pairs_o = links.gather_pairs(reduce_z(total_o), 1)
    total_q = reduce_z(total_q)
    grad_gate_up, grad_down = finish_mlp(place, [*pairs_a, *pairs_b], (1, 2))
    result = hidden + results_a[0].astype(F32) + results_b[0].astype(F32)
    result = result + links.core(results_b[1]).astype(F32)
    output = result.astype(BF16).T[None]
    total_q = after(total_q, grad_gate_up, output)
    pairs_q = links.gather_pairs(total_q, 2)
    grad_qkv, grad_out, gain_columns = finish_rows(place, [*pairs_o, *pairs_q], (1, 2))
    return (
        output,
        input_grad.T[None],
        gain_columns[:, 0],
        grad_qkv,
        grad_out,
        gain_columns[:, 1],
        grad_gate_up,
        grad_down.T,
    )


def solution(mesh):
    placed = (
        P(("seq", "fsdp"), "ctx", None),
        P(("seq", "fsdp"), "ctx", None),
        P(("seq", "fsdp"), "ctx"),
        P(("seq", "fsdp"), None),
        P("fsdp"),
        P("fsdp", None),
        P("fsdp", None),
        P("fsdp"),
        P("fsdp", None),
        P("fsdp", None),
    )
    links = Links([mesh.shape[name] for name in AXES])
    return jax.shard_map(
        functools.partial(shards, links),
        mesh=mesh,
        in_specs=placed,
        out_specs=(
            P(("seq", "fsdp"), "ctx", None),
            P(("seq", "fsdp"), "ctx", None),
            P("fsdp"),
            P("fsdp", None),
            P("fsdp", None),
            P("fsdp"),
            P("fsdp", None),
            P("fsdp", None),
        ),
        check_vma=False,
    )
```

```python
import functools

import jax
import jax.numpy as jnp
from jax import lax
from jax.experimental import pallas as pl
from jax.experimental.pallas import tpu as pltpu
from jax.sharding import PartitionSpec as P

D = 960
HEADS = 15
KV_HEADS = 5
HEAD_DIM = 64
FF = 2560
BLK = 128
TOK_DEV = 512
KV_DIM = 320
QKV = D + 2 * KV_DIM
QKV_WIDE = 1664
CUT = 896
EARLY_WIDE = 1920
FF_SHARD = FF // 4
ROWS = D // 4
ROWS_PAD = 256
SLICE = 32
TILE = 128
HALF = 64
ROW_TILE = 256
VMEM_LIMIT = 56 * 1024 * 1024

EPSILON = 1e-05
ROPE_BASE = 100000.0
MASKED_SCORE = -1e30
AXES = ("seq", "ctx", "fsdp")
F32 = jnp.float32
BF16 = jnp.bfloat16
ANY = pl.BlockSpec(memory_space=pl.ANY)
SMEM = pl.BlockSpec(memory_space=pltpu.SMEM)
VMEM = pl.BlockSpec(memory_space=pltpu.VMEM)
LONG = pl.CostEstimate(flops=40_000_000_000, bytes_accessed=1000, transcendentals=0)
SHORT = pl.CostEstimate(flops=1000, bytes_accessed=1000, transcendentals=0)
NT = (((1,), (1,)), ((), ()))
TN = (((0,), (0,)), ((), ()))


def frequencies():
    steps = jnp.arange(HEAD_DIM // 2, dtype=F32) * 2.0 / HEAD_DIM
    return ROPE_BASE ** (-steps)


def after(value, *earlier):
    return lax.optimization_barrier((value, *earlier))[0]


def gate(values, *earlier):
    return [after(value, *earlier) for value in values]


def step_kernel(before, behind):
    behind[...] = before[...]


def step(*needed):
    shape = jax.ShapeDtypeStruct((8, 128), F32)
    token = after(jnp.zeros(shape.shape, F32), *needed)
    return pl.pallas_call(
        step_kernel, out_shape=shape, in_specs=[VMEM], out_specs=VMEM, cost_estimate=LONG
    )(token)


def add(first, second):
    return (first.astype(F32) + second.astype(F32)).astype(BF16)


def sum_one(keep, arrived):
    pairs = list(zip(keep, arrived))
    stay = [value[0].astype(F32) + more[0].astype(F32) for value, more in pairs]
    return stay, [add(value[1], more[1]) for value, more in pairs]


def first_half(value):
    return value[: value.shape[0] // 2]


def second_half(value):
    return value[value.shape[0] // 2 :]


class Links:
    def __init__(self, sizes):
        self.sizes = sizes

    def index(self, s, c, f):
        return (s * self.sizes[1] + c) * self.sizes[2] + f

    def swap(self, value, ds=0, dc=0, df=0):
        n_s, n_c, n_f = self.sizes
        pairs = [
            (self.index(s, c, f), self.index(s ^ ds, c ^ dc, f ^ df))
            for s in range(n_s)
            for c in range(n_c)
            for f in range(n_f)
        ]
        return lax.ppermute(value, AXES, pairs)

    def later(self, value, blocks, sign):
        n_s, n_c, n_f = self.sizes
        pairs = []
        for s in range(n_s):
            for c in range(n_c - blocks):
                for f in range(n_f):
                    pair = (self.index(s, c, f), self.index(s, c + blocks, f))
                    pairs.append(pair if sign > 0 else pair[::-1])
        return lax.ppermute(value, AXES, pairs)

    def core(self, value):
        return self.swap(value, ds=1)

    def plane(self, value, bits):
        return self.swap(value, ds=bits & 2, dc=bits & 1)

    def gather_plane(self, own):
        return [own] + [self.plane(own, bits) for bits in (1, 2, 3)]

    def gather_z(self, own):
        return [self.swap(own, df=bits) for bits in (1, 2, 3)]

    def send_one(self, send):
        return [self.plane(value, bits) for value, bits in zip(send, (1, 2))]

    def send_two(self, move):
        return [self.plane(value, bits) for value, bits in zip(move, (2, 1))]

    def sum_two(self, stay, arrived):
        pairs = zip(stay, arrived)
        return [self.sum_ctx((value + more.astype(F32)).astype(BF16)) for value, more in pairs]

    def sum_ctx(self, value):
        step = 2
        while step < self.sizes[1]:
            value = add(value, self.swap(value, dc=step))
            step *= 2
        return value

    def gather_pairs(self, own, first):
        near = jnp.stack([own, self.plane(own, first)])
        far = self.plane(near, 3 - first)
        return near, far, self.core(near), self.core(far)


def piece_index(first, q):
    return (q & (3 - first)) // (3 - first), (q & first) // first


UNIT_TILES = (5, 3)
HIDDEN = (768, 512)
DOWN_AT = (3, 2)


def mlp_kernel(chunk, place, x_own, x_oth, dy_own, dy_oth, gate_up, w_down, halves, half_down, *rest):
    messages, rest = rest[:4], rest[4:]
    if chunk:
        carried, rest = rest[:2], rest[2:]
    results, (keep_x, keep_y, send_x, send_y), rest = rest[:4], rest[4:8], rest[8:]
    weight, drop, drop_half, act, dgu, units, x_t, dy_t, x, dy, out_t, dn_t, sems = rest
    hidden, down_at = HIDDEN[chunk], DOWN_AT[chunk]
    with_half = chunk == 0
    p, k, f = place[0], place[1], place[2]
    groups = ([], [], [])

    def copy(source, target, group):
        groups[group].append(pltpu.make_async_copy(source, target, sems.at[group]))

    for half, (xs, ds) in enumerate(((x_own, dy_own), (x_oth, dy_oth))):
        lanes = pl.ds(half * TOK_DEV, TOK_DEV)
        copy(xs, x_t.at[:, lanes], 0)
        copy(ds, dy_t.at[:, lanes], 1)
    if chunk:
        for source, target in zip(carried, (out_t, dn_t)):
            copy(source, target.at[:, pl.ds(TOK_DEV, TOK_DEV)], 1)
    tile_of_core = 2 * k + chunk
    for kind in range(2):
        for z in range(4):
            col = pl.multiple_of(kind * FF + z * FF_SHARD + tile_of_core * TILE, TILE)
            copy(
                gate_up.at[:, pl.ds(col, TILE)],
                weight.at[f, :, pl.ds(kind * hidden + z * TILE, TILE)],
                1,
            )
        if with_half:
            copy(
                halves.at[:, pl.ds(kind * 2 * TILE, 2 * TILE)],
                weight.at[f, :, pl.ds(kind * hidden + 4 * TILE, 2 * TILE)],
                1,
            )
    copy(
        w_down.at[:, pl.ds(pl.multiple_of(tile_of_core * TILE, TILE), TILE)],
        drop.at[:, pl.ds(pl.multiple_of(f * TILE, TILE), TILE)],
        1,
    )
    if with_half:
        copy(half_down, drop_half.at[f], 1)
    for q, ref in enumerate(messages):
        pp = jnp.bitwise_xor(p, q)
        for r in range(3):
            z = jnp.bitwise_xor(f, r + 1)
            rows = pl.ds(r * ROWS, ROWS)
            for kind in range(2):
                lane = pl.multiple_of(kind * hidden + pp * TILE, TILE)
                copy(
                    ref.at[rows, pl.ds(kind * TILE, TILE)],
                    weight.at[z, :, pl.ds(lane, TILE)],
                    1,
                )
            rows_at = pl.ds(pl.multiple_of(pp * ROWS, 16), ROWS)
            copy(
                ref.at[rows, pl.ds(down_at * TILE, TILE)],
                drop.at[rows_at, pl.ds(pl.multiple_of(z * TILE, TILE), TILE)],
                1,
            )
            if with_half:
                lane = jnp.right_shift(pp, 1) * hidden + 4 * TILE + jnp.bitwise_and(pp, 1) * TILE
                copy(
                    ref.at[rows, pl.ds(2 * TILE, TILE)],
                    weight.at[z, :, pl.ds(pl.multiple_of(lane, TILE), TILE)],
                    1,
                )
                copy(ref.at[rows, pl.ds(4 * TILE, TILE)], drop_half.at[z, rows_at], 1)
    for group in groups:
        for each in group:
            each.start()
    for each in groups[0]:
        each.wait()
    x[...] = x_t[...].T
    for each in groups[1]:
        each.wait()
    dy[...] = dy_t[...].T
    if with_half:
        for z in range(4):
            lane = 4 * TILE + z * HALF
            drop[:, lane : lane + HALF] = drop_half[z, :, :HALF]

    for t in range(2 * TOK_DEV // ROW_TILE):
        rows = slice(t * ROW_TILE, (t + 1) * ROW_TILE)
        both = weight[...].reshape(D, 2 * hidden)
        gu = jnp.dot(x[rows, :], both, preferred_element_type=F32)
        da = jnp.dot(dy[rows, :], drop[...], preferred_element_type=F32)
        g, u = gu[:, :hidden], gu[:, hidden:]
        sig = jax.nn.sigmoid(g)
        silu = g * sig
        a = (silu * u).astype(BF16)
        act[rows, :] = a
        dgu[rows, :hidden] = (da * u * (sig + silu * (1.0 - sig))).astype(BF16)
        dgu[rows, hidden:] = (da * silu).astype(BF16)
        out = lax.dot_general(drop[...], a, NT, preferred_element_type=F32)
        dn = lax.dot_general(both, dgu[rows, :], NT, preferred_element_type=F32)
        if chunk and t * ROW_TILE >= TOK_DEV:
            out = out + out_t[:, rows].astype(F32)
            dn = dn + dn_t[:, rows].astype(F32)
        out_t[:, rows] = out.astype(BF16)
        dn_t[:, rows] = dn.astype(BF16)

    groups = ([], [], [])
    for at, ref in enumerate((out_t, dn_t)):
        for half in range(2):
            copy(ref.at[:, pl.ds(half * TOK_DEV, TOK_DEV)], results[2 * at + half], 2)
    for each in groups[2]:
        each.start()

    step = 2 * TILE
    for start in range(0, hidden, step):
        grad = jnp.dot(
            dy_t[...], act[:, start : start + step], preferred_element_type=F32
        ).astype(BF16)
        if start < 4 * TILE:
            for part in range(2):
                z = start // TILE + part
                units[:, z, :, down_at * TILE : (down_at + 1) * TILE] = grad[
                    :, part * TILE : (part + 1) * TILE
                ].reshape(4, ROWS, TILE)
        else:
            for z in range(4):
                units[:, z, :, 4 * TILE : 4 * TILE + HALF] = grad[
                    :, z * HALF : (z + 1) * HALF
                ].reshape(4, ROWS, HALF)
    for pair in range(2):
        columns = [(kind * hidden + pair * step, kind) for kind in range(2)]
        if with_half:
            columns.append((pair * hidden + 4 * TILE, 2))
        for start, column in columns:
            grad = jnp.dot(
                x_t[...], dgu[:, start : start + step], preferred_element_type=F32
            ).astype(BF16)
            for part in range(2):
                units[2 * pair + part, :, :, column * TILE : (column + 1) * TILE] = grad[
                    :, part * TILE : (part + 1) * TILE
                ].reshape(4, ROWS, TILE)
        for pp in (2 * pair, 2 * pair + 1):
            q = jnp.bitwise_xor(p, pp)
            for bits in range(4):
                left = (keep_x, send_x)[bits & 1].at[bits >> 1]
                right = (keep_y, send_y)[bits >> 1].at[bits & 1]

                def send(pp=pp, left=left, right=right):
                    for r in range(4):
                        pltpu.make_async_copy(
                            units.at[pp, jnp.bitwise_xor(f, r)],
                            (left, right)[r & 1].at[pl.ds((r >> 1) * ROWS, ROWS)],
                            sems.at[2],
                        ).start()

                pl.when(q == bits)(send)
    for each in groups[2]:
        each.wait()
    for target in (keep_x, keep_y, send_x, send_y):
        for at in range(2):
            for r in range(2):
                pltpu.make_async_copy(
                    units.at[0, 0], target.at[at, pl.ds(r * ROWS, ROWS)], sems.at[2]
                ).wait()


def mlp_chunk(place, chunk, tokens, weights, messages, carried=()):
    hidden = HIDDEN[chunk]
    width = UNIT_TILES[chunk] * TILE
    part = jax.ShapeDtypeStruct((2, 2 * ROWS, width), BF16)
    operands = [place, *tokens, *weights, *messages, *carried]
    out = pl.pallas_call(
        functools.partial(mlp_kernel, chunk),
        out_shape=[jax.ShapeDtypeStruct((D, TOK_DEV), BF16)] * 4 + [part] * 4,
        in_specs=[SMEM] + [ANY] * (len(operands) - 1),
        out_specs=[ANY] * 8,
        scratch_shapes=[
            pltpu.VMEM((4, ROWS, 2 * hidden), BF16),
            pltpu.VMEM((D, hidden), BF16),
            pltpu.VMEM((4, D, TILE), BF16),
            pltpu.VMEM((2 * TOK_DEV, hidden), BF16),
            pltpu.VMEM((2 * TOK_DEV, 2 * hidden), BF16),
            pltpu.VMEM((4, 4, ROWS, width), BF16),
            pltpu.VMEM((D, 2 * TOK_DEV), BF16),
            pltpu.VMEM((D, 2 * TOK_DEV), BF16),
            pltpu.VMEM((2 * TOK_DEV, D), BF16),
            pltpu.VMEM((2 * TOK_DEV, D), BF16),
            pltpu.VMEM((D, 2 * TOK_DEV), BF16),
            pltpu.VMEM((D, 2 * TOK_DEV), BF16),
            pltpu.SemaphoreType.DMA((3,)),
        ],
        compiler_params=pltpu.CompilerParams(vmem_limit_bytes=VMEM_LIMIT),
        cost_estimate=LONG,
    )(*operands)
    return out[:4], out[4:6], out[6:8]


def finish_mlp_kernel(first, place, near, far, near_oth, far_oth, up, down):
    p, k = place[0], place[1]
    for q in range(4):
        side, index = piece_index(first, q)
        mine, theirs = ((near, far)[side].at[index], (near_oth, far_oth)[side].at[index])
        pp = jnp.bitwise_xor(p, q)
        rows = pl.ds(pl.multiple_of(pp * ROWS, 16), ROWS)
        for other, ref in enumerate((mine, theirs)):
            kk = jnp.bitwise_xor(k, other)
            for chunk in range(2):
                at = chunk * UNIT_TILES[0] * TILE
                for kind in range(2):
                    col = kind * FF + pp * FF_SHARD + (2 * kk + chunk) * TILE
                    lane = at + kind * TILE
                    up[:, pl.ds(pl.multiple_of(col, TILE), TILE)] = ref[
                        :, lane : lane + TILE
                    ].astype(F32)
                lane = at + DOWN_AT[chunk] * TILE
                col = pl.multiple_of((2 * kk + chunk) * TILE, TILE)
                down[rows, pl.ds(col, TILE)] = ref[:, lane : lane + TILE].astype(F32)
        own, oth = (ref[:, 2 * TILE : 3 * TILE].astype(F32) for ref in (mine, theirs))
        low, high = jnp.where(k == 0, own, oth), jnp.where(k == 0, oth, own)
        for half in range(2):
            lanes = slice(half * HALF, (half + 1) * HALF)
            z = 2 * jnp.bitwise_and(pp, 1) + half
            col = jnp.right_shift(pp, 1) * FF + z * FF_SHARD + 4 * TILE
            up[:, pl.ds(pl.multiple_of(col, TILE), TILE)] = jnp.concatenate(
                [low[:, lanes], high[:, lanes]], axis=1
            )
        lanes = slice(4 * TILE, 4 * TILE + HALF)
        own, oth = (ref[:, lanes].astype(F32) for ref in (mine, theirs))
        low, high = jnp.where(k == 0, own, oth), jnp.where(k == 0, oth, own)
        down[rows, 4 * TILE :] = jnp.concatenate([low, high], axis=1)


def finish_mlp(place, pairs, first):
    return pl.pallas_call(
        functools.partial(finish_mlp_kernel, first),
        out_shape=[
            jax.ShapeDtypeStruct((ROWS, 2 * FF), F32),
            jax.ShapeDtypeStruct((D, FF_SHARD), F32),
        ],
        in_specs=[SMEM] + [VMEM] * 4,
        out_specs=[VMEM] * 2,
        compiler_params=pltpu.CompilerParams(vmem_limit_bytes=VMEM_LIMIT),
        cost_estimate=SHORT,
    )(place, *pairs)


def load_rows(place, own, mine, theirs, full, sem):
    p, k, f = place[0], place[1], place[2]
    for start in (True, False):

        def run(copy, start=start):
            if start:
                copy.start()
            else:
                copy.wait()

        run(pltpu.make_async_copy(own, full.at[f], sem))
        for other in range(2):
            kk = jnp.bitwise_xor(k, other)
            for q in range(4):
                ref = theirs.at[q] if other else mine[q]
                pp = jnp.bitwise_xor(p, q)
                row = pl.multiple_of(kk * 128 + pp * SLICE, 16)
                short = (kk * 4 + pp) == 7
                for r in range(3):
                    z = jnp.bitwise_xor(f, r + 1)

                    def go(count, ref=ref, r=r, z=z, row=row):
                        run(
                            pltpu.make_async_copy(
                                ref.at[r, pl.ds(0, count)], full.at[z, pl.ds(row, count)], sem
                            )
                        )

                    pl.when(short)(functools.partial(go, 16))
                    pl.when(jnp.logical_not(short))(functools.partial(go, SLICE))


def store_rows(place, grad, halves, theirs, sem):
    p, k, f = place[0], place[1], place[2]

    def target_of(other, q, r):
        at, index = (2 * (q & 1), q >> 1) if r & 1 == 0 else (1 + 2 * (q >> 1), q & 1)
        half = theirs.at[at] if other else halves[at]
        return half.at[index, pl.ds((r >> 1) * SLICE, SLICE)]

    for start in (True, False):
        for other in range(2):
            kk = jnp.bitwise_xor(k, other)
            for q in range(4):
                pp = jnp.bitwise_xor(p, q)
                row = pl.multiple_of(kk * 128 + pp * SLICE, 16)
                short = (kk * 4 + pp) == 7
                for r in range(4):
                    z = jnp.bitwise_xor(f, r)

                    def go(count, target=target_of(other, q, r), z=z, row=row):
                        copy = pltpu.make_async_copy(
                            grad.at[z, pl.ds(row, count)], target.at[pl.ds(0, count)], sem
                        )
                        if start:
                            copy.start()
                        else:
                            copy.wait()

                    pl.when(short)(functools.partial(go, 16))
                    pl.when(jnp.logical_not(short))(functools.partial(go, SLICE))


def finish_rows_kernel(first, place, near, far, near_oth, far_oth, qkv, out, gain):
    p, k = place[0], place[1]
    pairs = (near, far, near_oth, far_oth)
    for other in range(2):
        kk = jnp.bitwise_xor(k, other)
        for q in range(4):
            pp = jnp.bitwise_xor(p, q)
            row = pl.multiple_of(kk * 128 + pp * SLICE, 16)
            short = (kk * 4 + pp) == 7
            side, index = piece_index(first, q)
            value = pairs[2 * other + side][index].astype(F32)

            def go(count, value=value, row=row):
                rows = pl.ds(row, count)
                qkv[rows, :CUT] = value[:count, :CUT]
                qkv[rows, CUT:] = value[:count, EARLY_WIDE : EARLY_WIDE + QKV - CUT]
                out[rows, :] = value[:count, CUT : CUT + D]
                gain[rows, : QKV_WIDE - QKV] = value[:count, EARLY_WIDE + QKV - CUT :]

            pl.when(short)(functools.partial(go, 16))
            pl.when(jnp.logical_not(short))(functools.partial(go, SLICE))


def finish_rows(place, pairs, first):
    return pl.pallas_call(
        functools.partial(finish_rows_kernel, first),
        out_shape=[jax.ShapeDtypeStruct((ROWS, width), F32) for width in (QKV, D, TILE)],
        in_specs=[SMEM] + [VMEM] * 4,
        out_specs=[VMEM] * 3,
        compiler_params=pltpu.CompilerParams(vmem_limit_bytes=VMEM_LIMIT),
        cost_estimate=SHORT,
    )(place, *pairs)


def token_scale(values):
    return lax.rsqrt(jnp.mean(values * values, axis=0, keepdims=True) + EPSILON)


def tables_kernel(positions, frequency, cosines, sines):
    angles = frequency[:, :1] * positions[...].astype(F32)
    cosines[...] = jnp.cos(angles)
    sines[...] = jnp.sin(angles)


def tables(positions):
    frequency = jnp.broadcast_to(frequencies()[:, None], (HEAD_DIM // 2, TILE))
    return pl.pallas_call(
        tables_kernel,
        out_shape=[jax.ShapeDtypeStruct((HEAD_DIM // 2, TOK_DEV), F32)] * 2,
        in_specs=[VMEM] * 2,
        out_specs=[VMEM] * 2,
        cost_estimate=LONG,
    )(positions, frequency)


def project_kernel(
    place, x, cosines, sines, own, m0, m1, m2, m3, theirs, full, gains, normed, q_t, kv, sem
):
    load_rows(place, own, (m0, m1, m2, m3), theirs, full, sem)
    weight = full[...].reshape(D, QKV_WIDE)
    columns = weight[:, QKV - HALF :].astype(F32)
    gains[...] = columns
    source = x[...].astype(F32)
    normed[...] = (source * token_scale(source) * columns[:, HALF : HALF + 1]).astype(BF16)
    mixed = lax.dot_general(weight[:, :QKV], normed[...], TN, preferred_element_type=F32)
    cos, sin = cosines[...], sines[...]
    half = HEAD_DIM // 2
    for head in range(HEADS + KV_HEADS):
        row = head * HEAD_DIM
        low, high = mixed[row : row + half], mixed[row + half : row + HEAD_DIM]
        low, high = (low * cos - high * sin).astype(BF16), (high * cos + low * sin).astype(BF16)
        if head < HEADS:
            q_t[row : row + half, :] = low
            q_t[row + half : row + HEAD_DIM, :] = high
        else:
            row -= D
            for block in range(TOK_DEV // BLK):
                lanes = slice(block * BLK, (block + 1) * BLK)
                kv[block, row : row + half, :] = low[:, lanes]
                kv[block, row + half : row + HEAD_DIM, :] = high[:, lanes]
    for block in range(TOK_DEV // BLK):
        lanes = slice(block * BLK, (block + 1) * BLK)
        kv[block, KV_DIM:, :] = mixed[D + KV_DIM :, lanes].astype(BF16)


def project(place, x, cosines, sines, own, mine, theirs):
    return pl.pallas_call(
        project_kernel,
        out_shape=[
            jax.ShapeDtypeStruct((4, ROWS, QKV_WIDE), BF16),
            jax.ShapeDtypeStruct((D, TILE), F32),
            jax.ShapeDtypeStruct((D, TOK_DEV), BF16),
            jax.ShapeDtypeStruct((D, TOK_DEV), BF16),
            jax.ShapeDtypeStruct((TOK_DEV // BLK, 2 * KV_DIM, BLK), BF16),
        ],
        in_specs=[SMEM] + [VMEM] * 3 + [ANY] * 6,
        out_specs=[VMEM] * 5,
        scratch_shapes=[pltpu.SemaphoreType.DMA(())],
        compiler_params=pltpu.CompilerParams(vmem_limit_bytes=VMEM_LIMIT),
        cost_estimate=LONG,
    )(place, x, cosines, sines, own, *mine, theirs)


def three_heads(ref, group, lanes):
    first = group * (HEADS // KV_HEADS) * HEAD_DIM
    return jnp.concatenate(
        [
            ref[first + r * HEAD_DIM : first + (r + 1) * HEAD_DIM, lanes]
            for r in range(HEADS // KV_HEADS)
        ],
        axis=1,
    )


def diagonal_mask():
    shape = (BLK, BLK * (HEADS // KV_HEADS))
    keys = lax.broadcasted_iota(jnp.int32, shape, 0)
    queries = jnp.bitwise_and(lax.broadcasted_iota(jnp.int32, shape, 1), BLK - 1)
    return keys <= queries


def attend_kernel(lows, q_t, *rest):
    spans = rest[:-6]
    attn_t, log_total, kv, best, total, accum = rest[-6:]
    blocks = TOK_DEV // BLK
    for at, ref in enumerate(spans):
        kv[at * blocks : (at + 1) * blocks] = ref[...]
    own_at = (len(spans) - 1) * blocks
    mask = diagonal_mask()
    for i in range(blocks):
        lanes = slice(i * BLK, (i + 1) * BLK)
        queries = [
            three_heads(q_t, group, lanes) * jnp.asarray(HEAD_DIM**-0.5, BF16)
            for group in range(KV_HEADS)
        ]

        def step(j, diagonal, queries=queries):
            for group in range(KV_HEADS):
                keys = kv[j, group * HEAD_DIM : (group + 1) * HEAD_DIM, :]
                values = kv[j, KV_DIM + group * HEAD_DIM : KV_DIM + (group + 1) * HEAD_DIM, :]
                scores = lax.dot_general(keys, queries[group], TN, preferred_element_type=F32)
                if diagonal:
                    scores = jnp.where(mask, scores, MASKED_SCORE)
                    top = jnp.max(scores, axis=0, keepdims=True)
                    expo = jnp.exp(scores - top)
                    total[group] = jnp.sum(expo, axis=0, keepdims=True)
                    accum[group] = jnp.dot(values, expo.astype(BF16), preferred_element_type=F32)
                else:
                    old = best[group]
                    top = jnp.maximum(old, jnp.max(scores, axis=0, keepdims=True))
                    decay = jnp.exp(old - top)
                    expo = jnp.exp(scores - top)
                    total[group] = total[group] * decay + jnp.sum(expo, axis=0, keepdims=True)
                    accum[group] = accum[group] * decay + jnp.dot(
                        values, expo.astype(BF16), preferred_element_type=F32
                    )
                best[group] = top

        step(own_at + i, True)

        @pl.loop(lows[i], own_at + i)
        def earlier(j):
            step(j, False)

        for group in range(KV_HEADS):
            attn = (accum[group] / total[group]).astype(BF16)
            first = group * (HEADS // KV_HEADS) * HEAD_DIM
            for r in range(HEADS // KV_HEADS):
                attn_t[first + r * HEAD_DIM : first + (r + 1) * HEAD_DIM, lanes] = attn[
                    :, r * BLK : (r + 1) * BLK
                ]
            log_total[i * KV_HEADS + group] = best[group] + jnp.log(total[group])


def attend(lows, q_t, spans):
    blocks = TOK_DEV // BLK
    wide = BLK * (HEADS // KV_HEADS)
    return pl.pallas_call(
        attend_kernel,
        out_shape=[
            jax.ShapeDtypeStruct((D, TOK_DEV), BF16),
            jax.ShapeDtypeStruct((blocks * KV_HEADS, 1, wide), F32),
        ],
        in_specs=[SMEM] + [VMEM] * (1 + len(spans)),
        out_specs=[VMEM] * 2,
        scratch_shapes=[
            pltpu.VMEM((len(spans) * blocks, 2 * KV_DIM, BLK), BF16),
            pltpu.VMEM((KV_HEADS, 1, wide), F32),
            pltpu.VMEM((KV_HEADS, 1, wide), F32),
            pltpu.VMEM((KV_HEADS, HEAD_DIM, wide), F32),
        ],
        compiler_params=pltpu.CompilerParams(vmem_limit_bytes=VMEM_LIMIT),
        cost_estimate=LONG,
    )(lows, q_t, *spans)


def out_kernel(place, x, gains, attn_t, own, m0, m1, m2, m3, theirs, full, hidden, normed, sem):
    load_rows(place, own, (m0, m1, m2, m3), theirs, full, sem)
    value = x[...].astype(F32) + lax.dot_general(
        full[...].reshape(D, D), attn_t[...], TN, preferred_element_type=F32
    )
    hidden[...] = value
    normed[...] = (value * token_scale(value) * gains[:, HALF + 1 : HALF + 2]).astype(BF16)


def project_out(place, x, gains, attn_t, own, mine, theirs):
    return pl.pallas_call(
        out_kernel,
        out_shape=[
            jax.ShapeDtypeStruct((4, ROWS, D), BF16),
            jax.ShapeDtypeStruct((D, TOK_DEV), F32),
            jax.ShapeDtypeStruct((D, TOK_DEV), BF16),
        ],
        in_specs=[SMEM] + [VMEM] * 3 + [ANY] * 6,
        out_specs=[VMEM] * 3,
        scratch_shapes=[pltpu.SemaphoreType.DMA(())],
        compiler_params=pltpu.CompilerParams(vmem_limit_bytes=VMEM_LIMIT),
        cost_estimate=SHORT,
    )(place, x, gains, attn_t, own, *mine, theirs)


def norm_back(value, scale, gain, dn):
    unit = value * scale
    weighted = dn * gain
    d_value = scale * (weighted - unit * jnp.mean(weighted * unit, axis=0, keepdims=True))
    return d_value, jnp.sum(dn * unit, axis=1, keepdims=True)


def middle_kernel(
    hidden, dy, gains, dn0, dn1, dn2, dn3, full, d_hidden, d_hidden_b, d_attn_t, grad_gain
):
    value = hidden[...]
    dn = jnp.concatenate([dn2[...], dn3[...]], axis=0).astype(F32)
    dn = dn0[...].astype(F32) + dn1[...].astype(F32) + dn
    d_value, column = norm_back(value, token_scale(value), gains[:, HALF + 1 : HALF + 2], dn)
    grad_gain[...] = jnp.broadcast_to(column, (D, TILE))
    dh = dy[...].astype(F32) + d_value
    d_hidden[...] = dh
    dh = dh.astype(BF16)
    d_hidden_b[...] = dh
    d_attn_t[...] = jnp.dot(
        full[...].reshape(D, D), dh, preferred_element_type=F32
    ).astype(BF16)


def middle(hidden, dy, gains, dns, full):
    return pl.pallas_call(
        middle_kernel,
        out_shape=[
            jax.ShapeDtypeStruct((D, TOK_DEV), F32),
            jax.ShapeDtypeStruct((D, TOK_DEV), BF16),
            jax.ShapeDtypeStruct((D, TOK_DEV), BF16),
            jax.ShapeDtypeStruct((D, TILE), F32),
        ],
        in_specs=[VMEM] * 8,
        out_specs=[VMEM] * 4,
        compiler_params=pltpu.CompilerParams(vmem_limit_bytes=VMEM_LIMIT),
        cost_estimate=SHORT,
    )(hidden, dy, gains, *dns, full)


def attend_back_kernel(count, lows, q_t, attn_t, d_attn_t, log_total, cosines, sines, *rest):
    spans, rest = rest[:count], rest[count:]
    dq_t, d_spans, (kv, d_kv, d_query) = rest[0], rest[1 : 1 + count], rest[1 + count :]
    blocks = TOK_DEV // BLK
    groups = HEADS // KV_HEADS
    half = HEAD_DIM // 2
    for at, ref in enumerate(spans):
        kv[at * blocks : (at + 1) * blocks] = ref[...]
    d_kv[...] = jnp.zeros_like(d_kv)
    own_at = (count - 1) * blocks
    mask = diagonal_mask()
    for i in range(blocks):
        lanes = slice(i * BLK, (i + 1) * BLK)
        queries, d_outs, deltas = [], [], []
        for group in range(KV_HEADS):
            queries.append(three_heads(q_t, group, lanes) * jnp.asarray(HEAD_DIM**-0.5, BF16))
            d_out = three_heads(d_attn_t, group, lanes)
            attn = three_heads(attn_t, group, lanes)
            d_outs.append(d_out)
            deltas.append(
                jnp.sum(d_out.astype(F32) * attn.astype(F32), axis=0, keepdims=True)
            )

        def step(j, diagonal, i=i, queries=queries, d_outs=d_outs, deltas=deltas):
            for group in range(KV_HEADS):
                key_rows = slice(group * HEAD_DIM, (group + 1) * HEAD_DIM)
                value_rows = slice(KV_DIM + group * HEAD_DIM, KV_DIM + (group + 1) * HEAD_DIM)
                keys, values = kv[j, key_rows, :], kv[j, value_rows, :]
                scores = lax.dot_general(keys, queries[group], TN, preferred_element_type=F32)
                if diagonal:
                    scores = jnp.where(mask, scores, MASKED_SCORE)
                prob = jnp.exp(scores - log_total[i * KV_HEADS + group])
                d_prob = lax.dot_general(values, d_outs[group], TN, preferred_element_type=F32)
                d_scores = (prob * (d_prob - deltas[group])).astype(BF16)
                d_kv[j, value_rows, :] += lax.dot_general(
                    d_outs[group], prob.astype(BF16), NT, preferred_element_type=F32
                )
                d_kv[j, key_rows, :] += lax.dot_general(
                    queries[group], d_scores, NT, preferred_element_type=F32
                )
                more = jnp.dot(keys, d_scores, preferred_element_type=F32)
                if diagonal:
                    d_query[group] = more
                else:
                    d_query[group] += more

        step(own_at + i, True)

        @pl.loop(lows[i], own_at + i)
        def earlier(j):
            step(j, False)

        cos, sin = cosines[:, lanes], sines[:, lanes]
        for group in range(KV_HEADS):
            for r in range(groups):
                row = (group * groups + r) * HEAD_DIM
                side = slice(r * BLK, (r + 1) * BLK)
                low = d_query[group, :half, side] * HEAD_DIM**-0.5
                high = d_query[group, half:, side] * HEAD_DIM**-0.5
                dq_t[row : row + half, lanes] = (low * cos + high * sin).astype(BF16)
                dq_t[row + half : row + HEAD_DIM, lanes] = (high * cos - low * sin).astype(BF16)
    for at, ref in enumerate(d_spans):
        ref[...] = d_kv[at * blocks : (at + 1) * blocks].astype(ref.dtype)


def attend_back(lows, q_t, attn_t, d_attn_t, log_total, cosines, sines, spans):
    blocks = TOK_DEV // BLK
    wide = BLK * (HEADS // KV_HEADS)
    count = len(spans)
    shape = (blocks, 2 * KV_DIM, BLK)
    out = pl.pallas_call(
        functools.partial(attend_back_kernel, count),
        out_shape=[jax.ShapeDtypeStruct((D, TOK_DEV), BF16)]
        + [jax.ShapeDtypeStruct(shape, BF16)] * (count - 1)
        + [jax.ShapeDtypeStruct(shape, F32)],
        in_specs=[SMEM] + [VMEM] * (6 + count),
        out_specs=[VMEM] * (1 + count),
        scratch_shapes=[
            pltpu.VMEM((count * blocks, 2 * KV_DIM, BLK), BF16),
            pltpu.VMEM((count * blocks, 2 * KV_DIM, BLK), F32),
            pltpu.VMEM((KV_HEADS, HEAD_DIM, wide), F32),
        ],
        compiler_params=pltpu.CompilerParams(vmem_limit_bytes=VMEM_LIMIT),
        cost_estimate=LONG,
    )(lows, q_t, attn_t, d_attn_t, log_total, cosines, sines, *spans)
    return out[0], out[1:]


def early_kernel(place, normed, dq_t, attn_t, dh, *rest):
    halves, theirs, grad, sem = rest[:4], rest[4], rest[5], rest[6]
    product = lax.dot_general(attn_t[...], dh[...], NT, preferred_element_type=F32)
    grad[:, :, CUT : CUT + D] = product.astype(BF16).reshape(4, ROWS, D)
    product = lax.dot_general(normed[...], dq_t[:CUT, :], NT, preferred_element_type=F32)
    grad[:, :, :CUT] = product.astype(BF16).reshape(4, ROWS, CUT)
    store_rows(place, grad, halves, theirs, sem)


def early(place, normed, dq_t, attn_t, dh):
    piece = jax.ShapeDtypeStruct((2, 2 * SLICE, EARLY_WIDE), BF16)
    out = pl.pallas_call(
        early_kernel,
        out_shape=[*[piece] * 4, jax.ShapeDtypeStruct((4, 2, 2 * SLICE, EARLY_WIDE), BF16)],
        in_specs=[SMEM] + [VMEM] * 4,
        out_specs=[ANY] * 5,
        scratch_shapes=[pltpu.VMEM((4, ROWS, EARLY_WIDE), BF16), pltpu.SemaphoreType.DMA(())],
        compiler_params=pltpu.CompilerParams(vmem_limit_bytes=VMEM_LIMIT),
        cost_estimate=LONG,
    )(place, normed, dq_t, attn_t, dh)
    return out[:4], out[4]


def last_kernel(
    count, place, x, gains, normed, dq_t, cosines, sines, full, d_hidden, mlp_gain_grad, d_own, *rest
):
    arrived, rest = rest[:count], rest[count:]
    input_grad, halves, theirs, d_mixed, grad, sem = rest[0], rest[1:5], rest[5], *rest[6:]
    half = HEAD_DIM // 2
    d_mixed[:D, :] = dq_t[...]
    for block in range(TOK_DEV // BLK):
        lanes = slice(block * BLK, (block + 1) * BLK)
        value = d_own[block]
        for ref in arrived:
            value = value + ref[block].astype(F32)
        cos, sin = cosines[:, lanes], sines[:, lanes]
        for head in range(KV_HEADS):
            row = head * HEAD_DIM
            low, high = value[row : row + half], value[row + half : row + HEAD_DIM]
            d_mixed[D + row : D + row + half, lanes] = (low * cos + high * sin).astype(BF16)
            d_mixed[D + row + half : D + row + HEAD_DIM, lanes] = (high * cos - low * sin).astype(
                BF16
            )
        d_mixed[D + KV_DIM :, lanes] = value[KV_DIM:].astype(BF16)
    product = lax.dot_general(normed[...], d_mixed[CUT:, :], NT, preferred_element_type=F32)
    grad[:, :, : QKV - CUT] = product.astype(BF16).reshape(4, ROWS, QKV - CUT)
    weight = full[...].reshape(D, QKV_WIDE)[:, :QKV]
    dn = jnp.dot(weight, d_mixed[...], preferred_element_type=F32)
    source = x[...].astype(F32)
    d_value, column = norm_back(source, token_scale(source), gains[:, HALF : HALF + 1], dn)
    input_grad[...] = (d_hidden[...] + d_value).astype(BF16)
    lane = lax.broadcasted_iota(jnp.int32, (D, QKV_WIDE - QKV), 1)
    both = jnp.where(lane == 0, column, mlp_gain_grad[:, : QKV_WIDE - QKV])
    grad[:, :, QKV - CUT :] = both.astype(BF16).reshape(4, ROWS, QKV_WIDE - QKV)
    store_rows(place, grad, halves, theirs, sem)


def last(place, x, gains, normed, dq_t, cosines, sines, full, d_hidden, mlp_gain_grad, d_own, arrived):
    width = QKV_WIDE - CUT
    piece = jax.ShapeDtypeStruct((2, 2 * SLICE, width), BF16)
    out = pl.pallas_call(
        functools.partial(last_kernel, len(arrived)),
        out_shape=[
            jax.ShapeDtypeStruct((D, TOK_DEV), BF16),
            *[piece] * 4,
            jax.ShapeDtypeStruct((4, 2, 2 * SLICE, width), BF16),
        ],
        in_specs=[SMEM] + [VMEM] * (10 + len(arrived)),
        out_specs=[VMEM] + [ANY] * 5,
        scratch_shapes=[
            pltpu.VMEM((QKV, TOK_DEV), BF16),
            pltpu.VMEM((4, ROWS, width), BF16),
            pltpu.SemaphoreType.DMA(()),
        ],
        compiler_params=pltpu.CompilerParams(vmem_limit_bytes=VMEM_LIMIT),
        cost_estimate=LONG,
    )(place, x, gains, normed, dq_t, cosines, sines, full, d_hidden, mlp_gain_grad, d_own, *arrived)
    return out[0], out[1:5], out[5]


def shards(
    links,
    tokens,
    cotangent,
    positions,
    doc_ids,
    gain_attn,
    w_qkv,
    w_out,
    gain_mlp,
    w_gate_up,
    w_down,
):
    seq_at, ctx_at, f = (lax.axis_index(name) for name in AXES)
    k = jnp.bitwise_and(seq_at, 1)
    p = 2 * jnp.right_shift(seq_at, 1) + jnp.bitwise_and(ctx_at, 1)
    place = jnp.stack([p, k, f]).astype(jnp.int32)
    n_ctx = links.sizes[1]
    x_in, dy_own = tokens[0].T, cotangent[0].T

    def row_slice(weight):
        padded = jnp.pad(weight, ((0, ROWS_PAD - ROWS), (0, 0)))
        return lax.dynamic_slice_in_dim(padded, k * 128 + p * SLICE, SLICE, 0)

    def core_half(pair):
        return jnp.where(k == 0, pair[:, :HALF], pair[:, HALF:])

    halves = jnp.concatenate(
        [core_half(w_gate_up[:, at : at + TILE]) for at in range(4 * TILE, 2 * FF, FF_SHARD)],
        axis=1,
    )
    down_t = w_down.T
    half_down = jnp.pad(core_half(down_t[:, 4 * TILE :]), ((0, 0), (0, HALF)))

    def unit(chunk):
        tiles = []
        for kind in range(2):
            col = kind * FF + p * FF_SHARD + (2 * k + chunk) * TILE
            tiles.append(lax.dynamic_slice_in_dim(w_gate_up, col, TILE, 1))
        if chunk == 0:
            tiles.append(lax.dynamic_slice_in_dim(halves, p * TILE, TILE, 1))
        tiles.append(
            lax.dynamic_slice(down_t, (p * ROWS, (2 * k + chunk) * TILE), (ROWS, TILE))
        )
        if chunk == 0:
            tiles.append(lax.dynamic_slice_in_dim(half_down, p * ROWS, ROWS, 0))
        return jnp.concatenate(tiles, axis=1)

    pair = jnp.stack([gain_attn, gain_mlp], axis=1)
    gain_columns = jnp.pad(pair, ((0, 0), (0, QKV_WIDE - QKV - 2)))
    qkv_own = jnp.concatenate([w_qkv, gain_columns], axis=1)
    qkv_slice = jnp.concatenate([row_slice(w_qkv), row_slice(gain_columns)], axis=1)
    out_slice = row_slice(w_out)
    unit_a, unit_b = unit(0), unit(1)
    qkv_z = links.gather_z(qkv_slice)
    far_o = links.swap(out_slice, df=2)
    qkv_mine = links.gather_plane(jnp.stack(qkv_z))
    near_a = links.swap(after(unit_a, *qkv_z), df=1)
    cosines, sines = tables(after(positions, *qkv_z))
    near_a, far_o, *qkv_mine = gate([near_a, far_o, *qkv_mine], cosines)
    qkv_sent = jnp.stack(qkv_mine)
    pair_a = jnp.concatenate([unit_a, near_a], axis=0)
    pair_o = jnp.stack([out_slice, far_o])
    qkv_theirs = links.core(qkv_sent)
    far_a = links.swap(pair_a, df=2)
    near_o = links.swap(pair_o, df=1)
    token = step(qkv_sent, pair_a, pair_o)
    qkv_theirs, near_o = gate([qkv_theirs, near_o], token)
    blocks = TOK_DEV // BLK
    docs = doc_ids[0]
    own_docs = lax.dynamic_slice_in_dim(docs, ctx_at * blocks, blocks)
    lows = jnp.sum((docs[None, :] < own_docs[:, None]).astype(jnp.int32), axis=1)
    lows = lows + (n_ctx - 1 - ctx_at) * blocks
    out_z = jnp.stack([near_o[0], far_o, near_o[1]])
    out_mine = links.gather_plane(out_z)

    def three_z(own, far, near):
        return jnp.concatenate([first_half(near), far, second_half(near)], axis=0)

    qkv_full, gains, normed, q_t, kv = project(
        place, x_in, cosines, sines, after(qkv_own, token, out_z), qkv_mine, qkv_theirs
    )
    spans = [links.later(kv, d, 1) for d in range(n_ctx - 1, 0, -1)] + [kv]
    token = step(kv)
    *spans, far_a = gate([*spans[:-1], far_a], token)
    spans = [*spans, kv]
    out_mine = gate(out_mine, token)
    out_theirs = links.core(jnp.stack(out_mine))
    first_a = jnp.concatenate([near_a, far_a], axis=0)
    rest_a = [links.plane(first_a, bits) for bits in (1, 2, 3)]
    far_b = links.swap(after(unit_b, first_a), df=2)
    attn_t, log_total = attend(lows, after(q_t, first_a), spans)
    far_b, out_theirs = gate([far_b, out_theirs], attn_t)
    pair_b = jnp.concatenate([unit_b, far_b], axis=0)
    near_b = links.swap(pair_b, df=1)
    dy_oth = links.core(dy_own)
    out_full, hidden, normed_mlp = project_out(
        place, x_in, gains, after(attn_t, step(pair_b)), w_out, out_mine, out_theirs
    )

    x_oth = links.core(normed_mlp)
    near_b, *rest_a = gate([near_b, *rest_a], hidden)
    first_b = three_z(unit_b, far_b, near_b)
    rest_b = [links.plane(first_b, bits) for bits in (1, 2, 3)]
    mlp_weights = (w_gate_up, down_t, halves, half_down)
    tokens_mlp = (after(normed_mlp, first_b), x_oth, dy_own, dy_oth)
    results_a, keep_a, send_a = mlp_chunk(
        place, 0, tokens_mlp, mlp_weights, [first_a, *rest_a]
    )
    arrived_a = links.send_one(send_a)
    rest_b = gate(rest_b, results_a[0])
    results_b, keep_b, send_b = mlp_chunk(
        place,
        1,
        (normed_mlp, x_oth, dy_own, dy_oth),
        mlp_weights,
        [first_b, *rest_b],
        (results_a[1], results_a[3]),
    )

    dn_oth = [links.core(part) for part in (first_half(results_b[3]), second_half(results_b[3]))]
    out_oth = links.core(results_b[1])
    d_hidden, d_hidden_b, d_attn_t, mlp_gain_grad = middle(
        hidden, dy_own, gains, (results_a[2], results_b[2], *dn_oth), out_full
    )
    stay_a, move_a = sum_one(keep_a, gate(arrived_a, d_hidden))
    arrived_a = links.send_two(move_a)
    arrived_b = links.send_one(gate(send_b, *move_a))
    dq_t, d_spans = attend_back(
        lows, q_t, attn_t, after(d_attn_t, *move_a), log_total, cosines, sines, spans
    )
    arrived = [
        links.later(value, d, -1) for value, d in zip(d_spans, range(n_ctx - 1, 0, -1))
    ]
    total_a = links.sum_two(stay_a, gate(arrived_a, dq_t))
    arrived_a = links.swap(total_a[1], df=1)
    stay_b, move_b = sum_one(keep_b, gate(arrived_b, dq_t))
    arrived_b = links.send_two(move_b)
    halves_o, theirs_o = early(
        place, normed, after(dq_t, *total_a, *move_b), attn_t, d_hidden_b
    )
    arrived_o = links.core(theirs_o)
    left_a = add(total_a[0], after(arrived_a, halves_o[0]))
    arrived_a = links.swap(second_half(left_a), df=2)
    total_b = links.sum_two(stay_b, gate(arrived_b, halves_o[0]))
    arrived_b = links.swap(total_b[1], df=1)
    halves_o = [add(value, more) for value, more in zip(halves_o, arrived_o)]
    arrived_o = links.send_one(halves_o[2:])
    input_grad, halves_q, theirs_q = last(
        place,
        x_in,
        gains,
        normed,
        after(dq_t, left_a, *total_b, *halves_o),
        cosines,
        sines,
        qkv_full,
        d_hidden,
        mlp_gain_grad,
        d_spans[-1],
        arrived,
    )
    arrived_q = links.core(theirs_q)
    stay_o, move_o = sum_one(halves_o[:2], gate(arrived_o, input_grad))
    arrived_o = links.send_two(move_o)
    left_b = add(total_b[0], after(arrived_b, input_grad))
    arrived_b = links.swap(second_half(left_b), df=2)
    total_a = add(first_half(left_a), after(arrived_a, input_grad))
    halves_q = [add(value, more) for value, more in zip(halves_q, arrived_q)]
    arrived_q = links.send_one(halves_q[2:])
    token = step(*halves_q, *move_o, left_b, total_a)
    stay_q, move_q = sum_one(halves_q[:2], gate(arrived_q, token))
    arrived_q = links.send_two(move_q)
    total_o = links.sum_two(stay_o, gate(arrived_o, token))
    arrived_o = links.swap(total_o[1], df=1)
    total_b = add(first_half(left_b), after(arrived_b, token))
    unit_mlp = jnp.concatenate([total_a, total_b], axis=1)
    mlp_x = links.plane(unit_mlp, 1)
    token = step(*move_q, *total_o, unit_mlp)
    total_q = links.sum_two(stay_q, gate(arrived_q, token))
    units_q = [first_half(total_q[0]), first_half(total_q[1])]
    units_q += [second_half(total_q[0]), second_half(total_q[1])]
    arrived_q = [links.swap(units_q[bits], df=bits) for bits in (1, 2, 3)]
    left_o = add(total_o[0], after(arrived_o, token))
    arrived_o = links.swap(second_half(left_o), df=2)
    mlp_near = jnp.stack([unit_mlp, after(mlp_x, token)])
    mlp_far = links.plane(mlp_near, 2)
    token = step(*units_q, left_o, mlp_near)
    done_q = units_q[0].astype(F32)
    for value in gate(arrived_q, token):
        done_q = done_q + value.astype(F32)
    done_o = add(first_half(left_o), after(arrived_o, token))
    rows = jnp.concatenate([done_o, done_q.astype(BF16)], axis=1)
    row_far = links.plane(rows, 1)
    mlp_near_oth = links.core(mlp_near)
    token = step(rows)
    near = jnp.stack([rows, after(row_far, token)])
    far = links.plane(near, 2)
    near_oth = links.core(near)
    mlp_far, mlp_near_oth = gate([mlp_far, mlp_near_oth], token)
    mlp_far_oth = links.core(mlp_far)
    token = step(near, mlp_far)
    far, near_oth, mlp_far_oth = gate([far, near_oth, mlp_far_oth], token)
    far_oth = links.core(far)
    grad_gate_up, grad_down = finish_mlp(
        place, [mlp_near, mlp_far, mlp_near_oth, mlp_far_oth], 1
    )
    result = hidden + results_a[0].astype(F32) + results_b[0].astype(F32)
    result = result + after(out_oth, d_hidden).astype(F32)
    output = result.astype(BF16).T[None]
    grad_qkv, grad_out, gain_columns = finish_rows(place, [near, far, near_oth, far_oth], 1)
    return (
        output,
        input_grad.T[None],
        gain_columns[:, 0],
        grad_qkv,
        grad_out,
        gain_columns[:, 1],
        grad_gate_up,
        grad_down.T,
    )


def solution(mesh):
    placed = (
        P(("seq", "fsdp"), "ctx", None),
        P(("seq", "fsdp"), "ctx", None),
        P(("seq", "fsdp"), "ctx"),
        P(("seq", "fsdp"), None),
        P("fsdp"),
        P("fsdp", None),
        P("fsdp", None),
        P("fsdp"),
        P("fsdp", None),
        P("fsdp", None),
    )
    links = Links([mesh.shape[name] for name in AXES])
    return jax.shard_map(
        functools.partial(shards, links),
        mesh=mesh,
        in_specs=placed,
        out_specs=(
            P(("seq", "fsdp"), "ctx", None),
            P(("seq", "fsdp"), "ctx", None),
            P("fsdp"),
            P("fsdp", None),
            P("fsdp", None),
            P("fsdp"),
            P("fsdp", None),
            P("fsdp", None),
        ),
        check_vma=False,
    )
```

```python
import functools

import jax
import jax.numpy as jnp
from jax import lax
from jax.experimental import pallas as pl
from jax.experimental.pallas import tpu as pltpu
from jax.sharding import PartitionSpec as P

D = 960
HEADS = 15
KV_HEADS = 5
HEAD_DIM = 64
FF = 2560
BLK = 128
TOK_DEV = 512
KV_DIM = 320
QKV = D + 2 * KV_DIM
QKV_WIDE = 1664
CUT = 896
EARLY_WIDE = 1920
FF_SHARD = FF // 4
ROWS = D // 4
ROWS_PAD = 256
SLICE = 32
TILE = 128
HALF = 64
ROW_TILE = 256
VMEM_LIMIT = 56 * 1024 * 1024

EPSILON = 1e-05
ROPE_BASE = 100000.0
MASKED_SCORE = -1e30
AXES = ("seq", "ctx", "fsdp")
F32 = jnp.float32
BF16 = jnp.bfloat16
ANY = pl.BlockSpec(memory_space=pl.ANY)
SMEM = pl.BlockSpec(memory_space=pltpu.SMEM)
VMEM = pl.BlockSpec(memory_space=pltpu.VMEM)
LONG = pl.CostEstimate(flops=40_000_000_000, bytes_accessed=1000, transcendentals=0)
SHORT = pl.CostEstimate(flops=1000, bytes_accessed=1000, transcendentals=0)
NT = (((1,), (1,)), ((), ()))
TN = (((0,), (0,)), ((), ()))


def frequencies():
    steps = jnp.arange(HEAD_DIM // 2, dtype=F32) * 2.0 / HEAD_DIM
    return ROPE_BASE ** (-steps)


def after(value, *earlier):
    return lax.optimization_barrier((value, *earlier))[0]


def gate(values, *earlier):
    return [after(value, *earlier) for value in values]


def step_kernel(before, behind):
    behind[...] = before[...]


def step(*needed):
    shape = jax.ShapeDtypeStruct((8, 128), F32)
    token = after(jnp.zeros(shape.shape, F32), *needed)
    return pl.pallas_call(
        step_kernel, out_shape=shape, in_specs=[VMEM], out_specs=VMEM, cost_estimate=LONG
    )(token)


def add(first, second):
    return (first.astype(F32) + second.astype(F32)).astype(BF16)


def sum_one(keep, arrived):
    pairs = list(zip(keep, arrived))
    stay = [value[0].astype(F32) + more[0].astype(F32) for value, more in pairs]
    return stay, [add(value[1], more[1]) for value, more in pairs]


def first_half(value):
    return value[: value.shape[0] // 2]


def second_half(value):
    return value[value.shape[0] // 2 :]


class Links:
    def __init__(self, sizes):
        self.sizes = sizes

    def index(self, s, c, f):
        return (s * self.sizes[1] + c) * self.sizes[2] + f

    def swap(self, value, ds=0, dc=0, df=0):
        n_s, n_c, n_f = self.sizes
        pairs = [
            (self.index(s, c, f), self.index(s ^ ds, c ^ dc, f ^ df))
            for s in range(n_s)
            for c in range(n_c)
            for f in range(n_f)
        ]
        return lax.ppermute(value, AXES, pairs)

    def later(self, value, blocks, sign):
        n_s, n_c, n_f = self.sizes
        pairs = []
        for s in range(n_s):
            for c in range(n_c - blocks):
                for f in range(n_f):
                    pair = (self.index(s, c, f), self.index(s, c + blocks, f))
                    pairs.append(pair if sign > 0 else pair[::-1])
        return lax.ppermute(value, AXES, pairs)

    def core(self, value):
        return self.swap(value, ds=1)

    def plane(self, value, bits):
        return self.swap(value, ds=bits & 2, dc=bits & 1)

    def gather_plane(self, own):
        return [own] + [self.plane(own, bits) for bits in (1, 2, 3)]

    def gather_z(self, own):
        return [self.swap(own, df=bits) for bits in (1, 2, 3)]

    def send_one(self, send):
        return [self.plane(value, bits) for value, bits in zip(send, (1, 2))]

    def send_two(self, move):
        return [self.plane(value, bits) for value, bits in zip(move, (2, 1))]

    def sum_two(self, stay, arrived):
        pairs = zip(stay, arrived)
        return [self.sum_ctx((value + more.astype(F32)).astype(BF16)) for value, more in pairs]

    def sum_ctx(self, value):
        step = 2
        while step < self.sizes[1]:
            value = add(value, self.swap(value, dc=step))
            step *= 2
        return value

    def gather_pairs(self, own, first):
        near = jnp.stack([own, self.plane(own, first)])
        far = self.plane(near, 3 - first)
        return near, far, self.core(near), self.core(far)


def piece_index(first, q):
    return (q & (3 - first)) // (3 - first), (q & first) // first


UNIT_TILES = (5, 3)
HIDDEN = (768, 512)
DOWN_AT = (3, 2)


def mlp_kernel(chunk, place, x_own, x_oth, dy_own, dy_oth, gate_up, w_down, halves, half_down, *rest):
    messages, rest = rest[:4], rest[4:]
    if chunk:
        carried, rest = rest[:2], rest[2:]
    results, (keep_x, keep_y, send_x, send_y), rest = rest[:4], rest[4:8], rest[8:]
    weight, drop, drop_half, act, dgu, units, x_t, dy_t, x, dy, out_t, dn_t, sems = rest
    hidden, down_at = HIDDEN[chunk], DOWN_AT[chunk]
    with_half = chunk == 0
    p, k, f = place[0], place[1], place[2]
    groups = ([], [], [])

    def copy(source, target, group):
        groups[group].append(pltpu.make_async_copy(source, target, sems.at[group]))

    for half, (xs, ds) in enumerate(((x_own, dy_own), (x_oth, dy_oth))):
        lanes = pl.ds(half * TOK_DEV, TOK_DEV)
        copy(xs, x_t.at[:, lanes], 0)
        copy(ds, dy_t.at[:, lanes], 1)
    if chunk:
        for source, target in zip(carried, (out_t, dn_t)):
            copy(source, target.at[:, pl.ds(TOK_DEV, TOK_DEV)], 1)
    tile_of_core = 2 * k + chunk
    for kind in range(2):
        for z in range(4):
            col = pl.multiple_of(kind * FF + z * FF_SHARD + tile_of_core * TILE, TILE)
            copy(
                gate_up.at[:, pl.ds(col, TILE)],
                weight.at[f, :, pl.ds(kind * hidden + z * TILE, TILE)],
                1,
            )
        if with_half:
            copy(
                halves.at[:, pl.ds(kind * 2 * TILE, 2 * TILE)],
                weight.at[f, :, pl.ds(kind * hidden + 4 * TILE, 2 * TILE)],
                1,
            )
    copy(
        w_down.at[:, pl.ds(pl.multiple_of(tile_of_core * TILE, TILE), TILE)],
        drop.at[:, pl.ds(pl.multiple_of(f * TILE, TILE), TILE)],
        1,
    )
    if with_half:
        copy(half_down, drop_half.at[f], 1)
    for q, ref in enumerate(messages):
        pp = jnp.bitwise_xor(p, q)
        for r in range(3):
            z = jnp.bitwise_xor(f, r + 1)
            rows = pl.ds(r * ROWS, ROWS)
            for kind in range(2):
                lane = pl.multiple_of(kind * hidden + pp * TILE, TILE)
                copy(
                    ref.at[rows, pl.ds(kind * TILE, TILE)],
                    weight.at[z, :, pl.ds(lane, TILE)],
                    1,
                )
            rows_at = pl.ds(pl.multiple_of(pp * ROWS, 16), ROWS)
            copy(
                ref.at[rows, pl.ds(down_at * TILE, TILE)],
                drop.at[rows_at, pl.ds(pl.multiple_of(z * TILE, TILE), TILE)],
                1,
            )
            if with_half:
                lane = jnp.right_shift(pp, 1) * hidden + 4 * TILE + jnp.bitwise_and(pp, 1) * TILE
                copy(
                    ref.at[rows, pl.ds(2 * TILE, TILE)],
                    weight.at[z, :, pl.ds(pl.multiple_of(lane, TILE), TILE)],
                    1,
                )
                copy(ref.at[rows, pl.ds(4 * TILE, TILE)], drop_half.at[z, rows_at], 1)
    for group in groups:
        for each in group:
            each.start()
    for each in groups[0]:
        each.wait()
    x[...] = x_t[...].T
    for each in groups[1]:
        each.wait()
    dy[...] = dy_t[...].T
    if with_half:
        for z in range(4):
            lane = 4 * TILE + z * HALF
            drop[:, lane : lane + HALF] = drop_half[z, :, :HALF]

    for t in range(2 * TOK_DEV // ROW_TILE):
        rows = slice(t * ROW_TILE, (t + 1) * ROW_TILE)
        both = weight[...].reshape(D, 2 * hidden)
        gu = jnp.dot(x[rows, :], both, preferred_element_type=F32)
        da = jnp.dot(dy[rows, :], drop[...], preferred_element_type=F32)
        g, u = gu[:, :hidden], gu[:, hidden:]
        sig = jax.nn.sigmoid(g)
        silu = g * sig
        a = (silu * u).astype(BF16)
        act[rows, :] = a
        dgu[rows, :hidden] = (da * u * (sig + silu * (1.0 - sig))).astype(BF16)
        dgu[rows, hidden:] = (da * silu).astype(BF16)
        out = lax.dot_general(drop[...], a, NT, preferred_element_type=F32)
        dn = lax.dot_general(both, dgu[rows, :], NT, preferred_element_type=F32)
        if chunk and t * ROW_TILE >= TOK_DEV:
            out = out + out_t[:, rows].astype(F32)
            dn = dn + dn_t[:, rows].astype(F32)
        out_t[:, rows] = out.astype(BF16)
        dn_t[:, rows] = dn.astype(BF16)

    groups = ([], [], [])
    for at, ref in enumerate((out_t, dn_t)):
        for half in range(2):
            copy(ref.at[:, pl.ds(half * TOK_DEV, TOK_DEV)], results[2 * at + half], 2)
    for each in groups[2]:
        each.start()

    step = 2 * TILE
    for start in range(0, hidden, step):
        grad = jnp.dot(
            dy_t[...], act[:, start : start + step], preferred_element_type=F32
        ).astype(BF16)
        if start < 4 * TILE:
            for part in range(2):
                z = start // TILE + part
                units[:, z, :, down_at * TILE : (down_at + 1) * TILE] = grad[
                    :, part * TILE : (part + 1) * TILE
                ].reshape(4, ROWS, TILE)
        else:
            for z in range(4):
                units[:, z, :, 4 * TILE : 4 * TILE + HALF] = grad[
                    :, z * HALF : (z + 1) * HALF
                ].reshape(4, ROWS, HALF)
    for pair in range(2):
        columns = [(kind * hidden + pair * step, kind) for kind in range(2)]
        if with_half:
            columns.append((pair * hidden + 4 * TILE, 2))
        for start, column in columns:
            grad = jnp.dot(
                x_t[...], dgu[:, start : start + step], preferred_element_type=F32
            ).astype(BF16)
            for part in range(2):
                units[2 * pair + part, :, :, column * TILE : (column + 1) * TILE] = grad[
                    :, part * TILE : (part + 1) * TILE
                ].reshape(4, ROWS, TILE)
        for pp in (2 * pair, 2 * pair + 1):
            q = jnp.bitwise_xor(p, pp)
            for bits in range(4):
                left = (keep_x, send_x)[bits & 1].at[bits >> 1]
                right = (keep_y, send_y)[bits >> 1].at[bits & 1]

                def send(pp=pp, left=left, right=right):
                    for r in range(4):
                        pltpu.make_async_copy(
                            units.at[pp, jnp.bitwise_xor(f, r)],
                            (left, right)[r & 1].at[pl.ds((r >> 1) * ROWS, ROWS)],
                            sems.at[2],
                        ).start()

                pl.when(q == bits)(send)
    for each in groups[2]:
        each.wait()
    for target in (keep_x, keep_y, send_x, send_y):
        for at in range(2):
            for r in range(2):
                pltpu.make_async_copy(
                    units.at[0, 0], target.at[at, pl.ds(r * ROWS, ROWS)], sems.at[2]
                ).wait()


def mlp_chunk(place, chunk, tokens, weights, messages, carried=()):
    hidden = HIDDEN[chunk]
    width = UNIT_TILES[chunk] * TILE
    part = jax.ShapeDtypeStruct((2, 2 * ROWS, width), BF16)
    operands = [place, *tokens, *weights, *messages, *carried]
    out = pl.pallas_call(
        functools.partial(mlp_kernel, chunk),
        out_shape=[jax.ShapeDtypeStruct((D, TOK_DEV), BF16)] * 4 + [part] * 4,
        in_specs=[SMEM] + [ANY] * (len(operands) - 1),
        out_specs=[ANY] * 8,
        scratch_shapes=[
            pltpu.VMEM((4, ROWS, 2 * hidden), BF16),
            pltpu.VMEM((D, hidden), BF16),
            pltpu.VMEM((4, D, TILE), BF16),
            pltpu.VMEM((2 * TOK_DEV, hidden), BF16),
            pltpu.VMEM((2 * TOK_DEV, 2 * hidden), BF16),
            pltpu.VMEM((4, 4, ROWS, width), BF16),
            pltpu.VMEM((D, 2 * TOK_DEV), BF16),
            pltpu.VMEM((D, 2 * TOK_DEV), BF16),
            pltpu.VMEM((2 * TOK_DEV, D), BF16),
            pltpu.VMEM((2 * TOK_DEV, D), BF16),
            pltpu.VMEM((D, 2 * TOK_DEV), BF16),
            pltpu.VMEM((D, 2 * TOK_DEV), BF16),
            pltpu.SemaphoreType.DMA((3,)),
        ],
        compiler_params=pltpu.CompilerParams(vmem_limit_bytes=VMEM_LIMIT),
        cost_estimate=LONG,
    )(*operands)
    return out[:4], out[4:6], out[6:8]


def finish_mlp_kernel(place, m0, m1, m2, m3, three_oth, xy_oth, up, down):
    p, k = place[0], place[1]
    for q, mine in enumerate((m0, m1, m2, m3)):
        theirs = three_oth.at[q] if q < 3 else xy_oth
        pp = jnp.bitwise_xor(p, q)
        rows = pl.ds(pl.multiple_of(pp * ROWS, 16), ROWS)
        for other, ref in enumerate((mine, theirs)):
            kk = jnp.bitwise_xor(k, other)
            for chunk in range(2):
                at = chunk * UNIT_TILES[0] * TILE
                for kind in range(2):
                    col = kind * FF + pp * FF_SHARD + (2 * kk + chunk) * TILE
                    lane = at + kind * TILE
                    up[:, pl.ds(pl.multiple_of(col, TILE), TILE)] = ref[
                        :, lane : lane + TILE
                    ].astype(F32)
                lane = at + DOWN_AT[chunk] * TILE
                col = pl.multiple_of((2 * kk + chunk) * TILE, TILE)
                down[rows, pl.ds(col, TILE)] = ref[:, lane : lane + TILE].astype(F32)
        own, oth = (ref[:, 2 * TILE : 3 * TILE].astype(F32) for ref in (mine, theirs))
        low, high = jnp.where(k == 0, own, oth), jnp.where(k == 0, oth, own)
        for half in range(2):
            lanes = slice(half * HALF, (half + 1) * HALF)
            z = 2 * jnp.bitwise_and(pp, 1) + half
            col = jnp.right_shift(pp, 1) * FF + z * FF_SHARD + 4 * TILE
            up[:, pl.ds(pl.multiple_of(col, TILE), TILE)] = jnp.concatenate(
                [low[:, lanes], high[:, lanes]], axis=1
            )
        lanes = slice(4 * TILE, 4 * TILE + HALF)
        own, oth = (ref[:, lanes].astype(F32) for ref in (mine, theirs))
        low, high = jnp.where(k == 0, own, oth), jnp.where(k == 0, oth, own)
        down[rows, 4 * TILE :] = jnp.concatenate([low, high], axis=1)


def finish_mlp(place, pieces):
    return pl.pallas_call(
        finish_mlp_kernel,
        out_shape=[
            jax.ShapeDtypeStruct((ROWS, 2 * FF), F32),
            jax.ShapeDtypeStruct((D, FF_SHARD), F32),
        ],
        in_specs=[SMEM] + [VMEM] * 6,
        out_specs=[VMEM] * 2,
        compiler_params=pltpu.CompilerParams(vmem_limit_bytes=VMEM_LIMIT),
        cost_estimate=SHORT,
    )(place, *pieces)


def load_rows(place, own, mine, theirs, full, sem):
    p, k, f = place[0], place[1], place[2]
    for start in (True, False):

        def run(copy, start=start):
            if start:
                copy.start()
            else:
                copy.wait()

        run(pltpu.make_async_copy(own, full.at[f], sem))
        for other in range(2):
            kk = jnp.bitwise_xor(k, other)
            for q in range(4):
                ref = theirs.at[q] if other else mine[q]
                pp = jnp.bitwise_xor(p, q)
                row = pl.multiple_of(kk * 128 + pp * SLICE, 16)
                short = (kk * 4 + pp) == 7
                for r in range(3):
                    z = jnp.bitwise_xor(f, r + 1)

                    def go(count, ref=ref, r=r, z=z, row=row):
                        run(
                            pltpu.make_async_copy(
                                ref.at[r, pl.ds(0, count)], full.at[z, pl.ds(row, count)], sem
                            )
                        )

                    pl.when(short)(functools.partial(go, 16))
                    pl.when(jnp.logical_not(short))(functools.partial(go, SLICE))


def store_rows(place, grad, halves, theirs, sem):
    p, k, f = place[0], place[1], place[2]

    def target_of(other, q, r):
        at, index = (2 * (q & 1), q >> 1) if r & 1 == 0 else (1 + 2 * (q >> 1), q & 1)
        half = theirs.at[at] if other else halves[at]
        return half.at[index, pl.ds((r >> 1) * SLICE, SLICE)]

    for start in (True, False):
        for other in range(2):
            kk = jnp.bitwise_xor(k, other)
            for q in range(4):
                pp = jnp.bitwise_xor(p, q)
                row = pl.multiple_of(kk * 128 + pp * SLICE, 16)
                short = (kk * 4 + pp) == 7
                for r in range(4):
                    z = jnp.bitwise_xor(f, r)

                    def go(count, target=target_of(other, q, r), z=z, row=row):
                        copy = pltpu.make_async_copy(
                            grad.at[z, pl.ds(row, count)], target.at[pl.ds(0, count)], sem
                        )
                        if start:
                            copy.start()
                        else:
                            copy.wait()

                    pl.when(short)(functools.partial(go, 16))
                    pl.when(jnp.logical_not(short))(functools.partial(go, SLICE))


def finish_rows_kernel(first, place, near, far, near_oth, far_oth, behind, qkv, out, gain, columns):
    p, k = place[0], place[1]
    pairs = (near, far, near_oth, far_oth)
    for other in range(2):
        kk = jnp.bitwise_xor(k, other)
        for q in range(4):
            pp = jnp.bitwise_xor(p, q)
            row = pl.multiple_of(kk * 128 + pp * SLICE, 16)
            short = (kk * 4 + pp) == 7
            side, index = piece_index(first, q)
            value = pairs[2 * other + side][index].astype(F32)

            def go(count, value=value, row=row):
                rows = pl.ds(row, count)
                qkv[rows, :CUT] = value[:count, :CUT]
                qkv[rows, CUT:] = value[:count, EARLY_WIDE : EARLY_WIDE + QKV - CUT]
                out[rows, :] = value[:count, CUT : CUT + D]
                columns[rows, : QKV_WIDE - QKV] = value[:count, EARLY_WIDE + QKV - CUT :]

            pl.when(short)(functools.partial(go, 16))
            pl.when(jnp.logical_not(short))(functools.partial(go, SLICE))
    gain[...] = columns[...].T[:8]


def finish_rows(place, pairs, first, behind):
    return pl.pallas_call(
        functools.partial(finish_rows_kernel, first),
        out_shape=[
            jax.ShapeDtypeStruct((ROWS, QKV), F32),
            jax.ShapeDtypeStruct((ROWS, D), F32),
            jax.ShapeDtypeStruct((8, 2 * TILE), F32),
        ],
        in_specs=[SMEM] + [VMEM] * 4 + [ANY],
        out_specs=[VMEM] * 3,
        scratch_shapes=[pltpu.VMEM((2 * TILE, TILE), F32)],
        compiler_params=pltpu.CompilerParams(vmem_limit_bytes=VMEM_LIMIT),
        cost_estimate=SHORT,
    )(place, *pairs, behind)


def token_scale(values):
    return lax.rsqrt(jnp.mean(values * values, axis=0, keepdims=True) + EPSILON)


def tables_kernel(positions, frequency, cosines, sines):
    angles = frequency[:, :1] * positions[...].astype(F32)
    cosines[...] = jnp.cos(angles)
    sines[...] = jnp.sin(angles)


def tables(positions):
    frequency = jnp.broadcast_to(frequencies()[:, None], (HEAD_DIM // 2, TILE))
    return pl.pallas_call(
        tables_kernel,
        out_shape=[jax.ShapeDtypeStruct((HEAD_DIM // 2, TOK_DEV), F32)] * 2,
        in_specs=[VMEM] * 2,
        out_specs=[VMEM] * 2,
        cost_estimate=LONG,
    )(positions, frequency)


def project_kernel(
    place, x, cosines, sines, own, m0, m1, m2, m3, theirs, full, gains, normed, q_t, kv, sem
):
    load_rows(place, own, (m0, m1, m2, m3), theirs, full, sem)
    weight = full[...].reshape(D, QKV_WIDE)
    columns = weight[:, QKV - HALF :].astype(F32)
    gains[...] = columns
    source = x[...].astype(F32)
    normed[...] = (source * token_scale(source) * columns[:, HALF : HALF + 1]).astype(BF16)
    mixed = lax.dot_general(weight[:, :QKV], normed[...], TN, preferred_element_type=F32)
    cos, sin = cosines[...], sines[...]
    half = HEAD_DIM // 2
    for head in range(HEADS + KV_HEADS):
        row = head * HEAD_DIM
        low, high = mixed[row : row + half], mixed[row + half : row + HEAD_DIM]
        low, high = (low * cos - high * sin).astype(BF16), (high * cos + low * sin).astype(BF16)
        if head < HEADS:
            q_t[row : row + half, :] = low
            q_t[row + half : row + HEAD_DIM, :] = high
        else:
            row -= D
            for block in range(TOK_DEV // BLK):
                lanes = slice(block * BLK, (block + 1) * BLK)
                kv[block, row : row + half, :] = low[:, lanes]
                kv[block, row + half : row + HEAD_DIM, :] = high[:, lanes]
    for block in range(TOK_DEV // BLK):
        lanes = slice(block * BLK, (block + 1) * BLK)
        kv[block, KV_DIM:, :] = mixed[D + KV_DIM :, lanes].astype(BF16)


def project(place, x, cosines, sines, own, mine, theirs):
    return pl.pallas_call(
        project_kernel,
        out_shape=[
            jax.ShapeDtypeStruct((4, ROWS, QKV_WIDE), BF16),
            jax.ShapeDtypeStruct((D, TILE), F32),
            jax.ShapeDtypeStruct((D, TOK_DEV), BF16),
            jax.ShapeDtypeStruct((D, TOK_DEV), BF16),
            jax.ShapeDtypeStruct((TOK_DEV // BLK, 2 * KV_DIM, BLK), BF16),
        ],
        in_specs=[SMEM] + [VMEM] * 3 + [ANY] * 6,
        out_specs=[VMEM] * 5,
        scratch_shapes=[pltpu.SemaphoreType.DMA(())],
        compiler_params=pltpu.CompilerParams(vmem_limit_bytes=VMEM_LIMIT),
        cost_estimate=LONG,
    )(place, x, cosines, sines, own, *mine, theirs)


def three_heads(ref, group, lanes):
    first = group * (HEADS // KV_HEADS) * HEAD_DIM
    return jnp.concatenate(
        [
            ref[first + r * HEAD_DIM : first + (r + 1) * HEAD_DIM, lanes]
            for r in range(HEADS // KV_HEADS)
        ],
        axis=1,
    )


def diagonal_mask():
    shape = (BLK, BLK * (HEADS // KV_HEADS))
    keys = lax.broadcasted_iota(jnp.int32, shape, 0)
    queries = jnp.bitwise_and(lax.broadcasted_iota(jnp.int32, shape, 1), BLK - 1)
    return keys <= queries


def attend_kernel(lows, q_t, *rest):
    spans = rest[:-6]
    attn_t, log_total, kv, best, total, accum = rest[-6:]
    blocks = TOK_DEV // BLK
    for at, ref in enumerate(spans):
        kv[at * blocks : (at + 1) * blocks] = ref[...]
    own_at = (len(spans) - 1) * blocks
    mask = diagonal_mask()
    for i in range(blocks):
        lanes = slice(i * BLK, (i + 1) * BLK)
        queries = [
            three_heads(q_t, group, lanes) * jnp.asarray(HEAD_DIM**-0.5, BF16)
            for group in range(KV_HEADS)
        ]

        def step(j, diagonal, queries=queries):
            for group in range(KV_HEADS):
                keys = kv[j, group * HEAD_DIM : (group + 1) * HEAD_DIM, :]
                values = kv[j, KV_DIM + group * HEAD_DIM : KV_DIM + (group + 1) * HEAD_DIM, :]
                scores = lax.dot_general(keys, queries[group], TN, preferred_element_type=F32)
                if diagonal:
                    scores = jnp.where(mask, scores, MASKED_SCORE)
                    top = jnp.max(scores, axis=0, keepdims=True)
                    expo = jnp.exp(scores - top)
                    total[group] = jnp.sum(expo, axis=0, keepdims=True)
                    accum[group] = jnp.dot(values, expo.astype(BF16), preferred_element_type=F32)
                else:
                    old = best[group]
                    top = jnp.maximum(old, jnp.max(scores, axis=0, keepdims=True))
                    decay = jnp.exp(old - top)
                    expo = jnp.exp(scores - top)
                    total[group] = total[group] * decay + jnp.sum(expo, axis=0, keepdims=True)
                    accum[group] = accum[group] * decay + jnp.dot(
                        values, expo.astype(BF16), preferred_element_type=F32
                    )
                best[group] = top

        step(own_at + i, True)

        @pl.loop(lows[i], own_at + i)
        def earlier(j):
            step(j, False)

        for group in range(KV_HEADS):
            attn = (accum[group] / total[group]).astype(BF16)
            first = group * (HEADS // KV_HEADS) * HEAD_DIM
            for r in range(HEADS // KV_HEADS):
                attn_t[first + r * HEAD_DIM : first + (r + 1) * HEAD_DIM, lanes] = attn[
                    :, r * BLK : (r + 1) * BLK
                ]
            log_total[i * KV_HEADS + group] = best[group] + jnp.log(total[group])


def attend(lows, q_t, spans):
    blocks = TOK_DEV // BLK
    wide = BLK * (HEADS // KV_HEADS)
    return pl.pallas_call(
        attend_kernel,
        out_shape=[
            jax.ShapeDtypeStruct((D, TOK_DEV), BF16),
            jax.ShapeDtypeStruct((blocks * KV_HEADS, 1, wide), F32),
        ],
        in_specs=[SMEM] + [VMEM] * (1 + len(spans)),
        out_specs=[VMEM] * 2,
        scratch_shapes=[
            pltpu.VMEM((len(spans) * blocks, 2 * KV_DIM, BLK), BF16),
            pltpu.VMEM((KV_HEADS, 1, wide), F32),
            pltpu.VMEM((KV_HEADS, 1, wide), F32),
            pltpu.VMEM((KV_HEADS, HEAD_DIM, wide), F32),
        ],
        compiler_params=pltpu.CompilerParams(vmem_limit_bytes=VMEM_LIMIT),
        cost_estimate=LONG,
    )(lows, q_t, *spans)


def out_kernel(place, x, gains, attn_t, own, m0, m1, m2, m3, theirs, full, hidden, normed, sem):
    load_rows(place, own, (m0, m1, m2, m3), theirs, full, sem)
    value = x[...].astype(F32) + lax.dot_general(
        full[...].reshape(D, D), attn_t[...], TN, preferred_element_type=F32
    )
    hidden[...] = value
    normed[...] = (value * token_scale(value) * gains[:, HALF + 1 : HALF + 2]).astype(BF16)


def project_out(place, x, gains, attn_t, own, mine, theirs):
    return pl.pallas_call(
        out_kernel,
        out_shape=[
            jax.ShapeDtypeStruct((4, ROWS, D), BF16),
            jax.ShapeDtypeStruct((D, TOK_DEV), F32),
            jax.ShapeDtypeStruct((D, TOK_DEV), BF16),
        ],
        in_specs=[SMEM] + [VMEM] * 3 + [ANY] * 6,
        out_specs=[VMEM] * 3,
        scratch_shapes=[pltpu.SemaphoreType.DMA(())],
        compiler_params=pltpu.CompilerParams(vmem_limit_bytes=VMEM_LIMIT),
        cost_estimate=SHORT,
    )(place, x, gains, attn_t, own, *mine, theirs)


def norm_back(value, scale, gain, dn):
    unit = value * scale
    weighted = dn * gain
    d_value = scale * (weighted - unit * jnp.mean(weighted * unit, axis=0, keepdims=True))
    return d_value, jnp.sum(dn * unit, axis=1, keepdims=True)


def middle_kernel(
    hidden, dy, gains, dn0, dn1, dn2, dn3, full, d_hidden, d_hidden_b, d_attn_t, grad_gain
):
    value = hidden[...]
    dn = jnp.concatenate([dn2[...], dn3[...]], axis=0).astype(F32)
    dn = dn0[...].astype(F32) + dn1[...].astype(F32) + dn
    d_value, column = norm_back(value, token_scale(value), gains[:, HALF + 1 : HALF + 2], dn)
    grad_gain[...] = jnp.broadcast_to(column, (D, TILE))
    dh = dy[...].astype(F32) + d_value
    d_hidden[...] = dh
    dh = dh.astype(BF16)
    d_hidden_b[...] = dh
    d_attn_t[...] = jnp.dot(
        full[...].reshape(D, D), dh, preferred_element_type=F32
    ).astype(BF16)


def middle(hidden, dy, gains, dns, full):
    return pl.pallas_call(
        middle_kernel,
        out_shape=[
            jax.ShapeDtypeStruct((D, TOK_DEV), F32),
            jax.ShapeDtypeStruct((D, TOK_DEV), BF16),
            jax.ShapeDtypeStruct((D, TOK_DEV), BF16),
            jax.ShapeDtypeStruct((D, TILE), F32),
        ],
        in_specs=[VMEM] * 8,
        out_specs=[VMEM] * 4,
        compiler_params=pltpu.CompilerParams(vmem_limit_bytes=VMEM_LIMIT),
        cost_estimate=SHORT,
    )(hidden, dy, gains, *dns, full)


def attend_back_kernel(count, lows, q_t, attn_t, d_attn_t, log_total, cosines, sines, *rest):
    spans, rest = rest[:count], rest[count:]
    dq_t, d_spans, (kv, d_kv, d_query) = rest[0], rest[1 : 1 + count], rest[1 + count :]
    blocks = TOK_DEV // BLK
    groups = HEADS // KV_HEADS
    half = HEAD_DIM // 2
    for at, ref in enumerate(spans):
        kv[at * blocks : (at + 1) * blocks] = ref[...]
    d_kv[...] = jnp.zeros_like(d_kv)
    own_at = (count - 1) * blocks
    mask = diagonal_mask()
    for i in range(blocks):
        lanes = slice(i * BLK, (i + 1) * BLK)
        queries, d_outs, deltas = [], [], []
        for group in range(KV_HEADS):
            queries.append(three_heads(q_t, group, lanes) * jnp.asarray(HEAD_DIM**-0.5, BF16))
            d_out = three_heads(d_attn_t, group, lanes)
            attn = three_heads(attn_t, group, lanes)
            d_outs.append(d_out)
            deltas.append(
                jnp.sum(d_out.astype(F32) * attn.astype(F32), axis=0, keepdims=True)
            )

        def step(j, diagonal, i=i, queries=queries, d_outs=d_outs, deltas=deltas):
            for group in range(KV_HEADS):
                key_rows = slice(group * HEAD_DIM, (group + 1) * HEAD_DIM)
                value_rows = slice(KV_DIM + group * HEAD_DIM, KV_DIM + (group + 1) * HEAD_DIM)
                keys, values = kv[j, key_rows, :], kv[j, value_rows, :]
                scores = lax.dot_general(keys, queries[group], TN, preferred_element_type=F32)
                if diagonal:
                    scores = jnp.where(mask, scores, MASKED_SCORE)
                prob = jnp.exp(scores - log_total[i * KV_HEADS + group])
                d_prob = lax.dot_general(values, d_outs[group], TN, preferred_element_type=F32)
                d_scores = (prob * (d_prob - deltas[group])).astype(BF16)
                d_kv[j, value_rows, :] += lax.dot_general(
                    d_outs[group], prob.astype(BF16), NT, preferred_element_type=F32
                )
                d_kv[j, key_rows, :] += lax.dot_general(
                    queries[group], d_scores, NT, preferred_element_type=F32
                )
                more = jnp.dot(keys, d_scores, preferred_element_type=F32)
                if diagonal:
                    d_query[group] = more
                else:
                    d_query[group] += more

        step(own_at + i, True)

        @pl.loop(lows[i], own_at + i)
        def earlier(j):
            step(j, False)

        cos, sin = cosines[:, lanes], sines[:, lanes]
        for group in range(KV_HEADS):
            for r in range(groups):
                row = (group * groups + r) * HEAD_DIM
                side = slice(r * BLK, (r + 1) * BLK)
                low = d_query[group, :half, side] * HEAD_DIM**-0.5
                high = d_query[group, half:, side] * HEAD_DIM**-0.5
                dq_t[row : row + half, lanes] = (low * cos + high * sin).astype(BF16)
                dq_t[row + half : row + HEAD_DIM, lanes] = (high * cos - low * sin).astype(BF16)
    for at, ref in enumerate(d_spans):
        ref[...] = d_kv[at * blocks : (at + 1) * blocks].astype(ref.dtype)


def attend_back(lows, q_t, attn_t, d_attn_t, log_total, cosines, sines, spans):
    blocks = TOK_DEV // BLK
    wide = BLK * (HEADS // KV_HEADS)
    count = len(spans)
    shape = (blocks, 2 * KV_DIM, BLK)
    out = pl.pallas_call(
        functools.partial(attend_back_kernel, count),
        out_shape=[jax.ShapeDtypeStruct((D, TOK_DEV), BF16)]
        + [jax.ShapeDtypeStruct(shape, BF16)] * (count - 1)
        + [jax.ShapeDtypeStruct(shape, F32)],
        in_specs=[SMEM] + [VMEM] * (6 + count),
        out_specs=[VMEM] * (1 + count),
        scratch_shapes=[
            pltpu.VMEM((count * blocks, 2 * KV_DIM, BLK), BF16),
            pltpu.VMEM((count * blocks, 2 * KV_DIM, BLK), F32),
            pltpu.VMEM((KV_HEADS, HEAD_DIM, wide), F32),
        ],
        compiler_params=pltpu.CompilerParams(vmem_limit_bytes=VMEM_LIMIT),
        cost_estimate=LONG,
    )(lows, q_t, attn_t, d_attn_t, log_total, cosines, sines, *spans)
    return out[0], out[1:]


def early_kernel(place, normed, dq_t, attn_t, dh, *rest):
    halves, theirs, grad, sem = rest[:4], rest[4], rest[5], rest[6]
    product = lax.dot_general(attn_t[...], dh[...], NT, preferred_element_type=F32)
    grad[:, :, CUT : CUT + D] = product.astype(BF16).reshape(4, ROWS, D)
    product = lax.dot_general(normed[...], dq_t[:CUT, :], NT, preferred_element_type=F32)
    grad[:, :, :CUT] = product.astype(BF16).reshape(4, ROWS, CUT)
    store_rows(place, grad, halves, theirs, sem)


def early(place, normed, dq_t, attn_t, dh):
    piece = jax.ShapeDtypeStruct((2, 2 * SLICE, EARLY_WIDE), BF16)
    out = pl.pallas_call(
        early_kernel,
        out_shape=[*[piece] * 4, jax.ShapeDtypeStruct((4, 2, 2 * SLICE, EARLY_WIDE), BF16)],
        in_specs=[SMEM] + [VMEM] * 4,
        out_specs=[ANY] * 5,
        scratch_shapes=[pltpu.VMEM((4, ROWS, EARLY_WIDE), BF16), pltpu.SemaphoreType.DMA(())],
        compiler_params=pltpu.CompilerParams(vmem_limit_bytes=VMEM_LIMIT),
        cost_estimate=LONG,
    )(place, normed, dq_t, attn_t, dh)
    return out[:4], out[4]


def last_kernel(
    count, place, x, gains, normed, dq_t, cosines, sines, full, d_hidden, mlp_gain_grad, d_own, *rest
):
    arrived, rest = rest[:count], rest[count:]
    input_grad, halves, theirs, d_mixed, grad, sem = rest[0], rest[1:5], rest[5], *rest[6:]
    half = HEAD_DIM // 2
    d_mixed[:D, :] = dq_t[...]
    for block in range(TOK_DEV // BLK):
        lanes = slice(block * BLK, (block + 1) * BLK)
        value = d_own[block]
        for ref in arrived:
            value = value + ref[block].astype(F32)
        cos, sin = cosines[:, lanes], sines[:, lanes]
        for head in range(KV_HEADS):
            row = head * HEAD_DIM
            low, high = value[row : row + half], value[row + half : row + HEAD_DIM]
            d_mixed[D + row : D + row + half, lanes] = (low * cos + high * sin).astype(BF16)
            d_mixed[D + row + half : D + row + HEAD_DIM, lanes] = (high * cos - low * sin).astype(
                BF16
            )
        d_mixed[D + KV_DIM :, lanes] = value[KV_DIM:].astype(BF16)
    product = lax.dot_general(normed[...], d_mixed[CUT:, :], NT, preferred_element_type=F32)
    grad[:, :, : QKV - CUT] = product.astype(BF16).reshape(4, ROWS, QKV - CUT)
    weight = full[...].reshape(D, QKV_WIDE)[:, :QKV]
    dn = jnp.dot(weight, d_mixed[...], preferred_element_type=F32)
    source = x[...].astype(F32)
    d_value, column = norm_back(source, token_scale(source), gains[:, HALF : HALF + 1], dn)
    input_grad[...] = (d_hidden[...] + d_value).astype(BF16)
    lane = lax.broadcasted_iota(jnp.int32, (D, QKV_WIDE - QKV), 1)
    both = jnp.where(lane == 0, column, mlp_gain_grad[:, : QKV_WIDE - QKV])
    grad[:, :, QKV - CUT :] = both.astype(BF16).reshape(4, ROWS, QKV_WIDE - QKV)
    store_rows(place, grad, halves, theirs, sem)


def last(place, x, gains, normed, dq_t, cosines, sines, full, d_hidden, mlp_gain_grad, d_own, arrived):
    width = QKV_WIDE - CUT
    piece = jax.ShapeDtypeStruct((2, 2 * SLICE, width), BF16)
    out = pl.pallas_call(
        functools.partial(last_kernel, len(arrived)),
        out_shape=[
            jax.ShapeDtypeStruct((D, TOK_DEV), BF16),
            *[piece] * 4,
            jax.ShapeDtypeStruct((4, 2, 2 * SLICE, width), BF16),
        ],
        in_specs=[SMEM] + [VMEM] * (10 + len(arrived)),
        out_specs=[VMEM] + [ANY] * 5,
        scratch_shapes=[
            pltpu.VMEM((QKV, TOK_DEV), BF16),
            pltpu.VMEM((4, ROWS, width), BF16),
            pltpu.SemaphoreType.DMA(()),
        ],
        compiler_params=pltpu.CompilerParams(vmem_limit_bytes=VMEM_LIMIT),
        cost_estimate=LONG,
    )(place, x, gains, normed, dq_t, cosines, sines, full, d_hidden, mlp_gain_grad, d_own, *arrived)
    return out[0], out[1:5], out[5]


def shards(
    links,
    tokens,
    cotangent,
    positions,
    doc_ids,
    gain_attn,
    w_qkv,
    w_out,
    gain_mlp,
    w_gate_up,
    w_down,
):
    seq_at, ctx_at, f = (lax.axis_index(name) for name in AXES)
    k = jnp.bitwise_and(seq_at, 1)
    p = 2 * jnp.right_shift(seq_at, 1) + jnp.bitwise_and(ctx_at, 1)
    place = jnp.stack([p, k, f]).astype(jnp.int32)
    n_ctx = links.sizes[1]
    x_in, dy_own = tokens[0].T, cotangent[0].T

    def row_slice(weight):
        padded = jnp.pad(weight, ((0, ROWS_PAD - ROWS), (0, 0)))
        return lax.dynamic_slice_in_dim(padded, k * 128 + p * SLICE, SLICE, 0)

    def core_half(pair):
        return jnp.where(k == 0, pair[:, :HALF], pair[:, HALF:])

    halves = jnp.concatenate(
        [core_half(w_gate_up[:, at : at + TILE]) for at in range(4 * TILE, 2 * FF, FF_SHARD)],
        axis=1,
    )
    down_t = w_down.T
    half_down = jnp.pad(core_half(down_t[:, 4 * TILE :]), ((0, 0), (0, HALF)))

    def unit(chunk):
        tiles = []
        for kind in range(2):
            col = kind * FF + p * FF_SHARD + (2 * k + chunk) * TILE
            tiles.append(lax.dynamic_slice_in_dim(w_gate_up, col, TILE, 1))
        if chunk == 0:
            tiles.append(lax.dynamic_slice_in_dim(halves, p * TILE, TILE, 1))
        tiles.append(
            lax.dynamic_slice(down_t, (p * ROWS, (2 * k + chunk) * TILE), (ROWS, TILE))
        )
        if chunk == 0:
            tiles.append(lax.dynamic_slice_in_dim(half_down, p * ROWS, ROWS, 0))
        return jnp.concatenate(tiles, axis=1)

    pair = jnp.stack([gain_attn, gain_mlp], axis=1)
    gain_columns = jnp.pad(pair, ((0, 0), (0, QKV_WIDE - QKV - 2)))
    qkv_own = jnp.concatenate([w_qkv, gain_columns], axis=1)
    qkv_slice = jnp.concatenate([row_slice(w_qkv), row_slice(gain_columns)], axis=1)
    out_slice = row_slice(w_out)
    unit_a, unit_b = unit(0), unit(1)
    qkv_z = links.gather_z(qkv_slice)
    far_o = links.swap(out_slice, df=2)
    qkv_mine = links.gather_plane(jnp.stack(qkv_z))
    near_a = links.swap(after(unit_a, *qkv_z), df=1)
    cosines, sines = tables(after(positions, *qkv_z))
    near_a, far_o, *qkv_mine = gate([near_a, far_o, *qkv_mine], cosines)
    qkv_sent = jnp.stack(qkv_mine)
    pair_a = jnp.concatenate([unit_a, near_a], axis=0)
    pair_o = jnp.stack([out_slice, far_o])
    qkv_theirs = links.core(qkv_sent)
    far_a = links.swap(pair_a, df=2)
    near_o = links.swap(pair_o, df=1)
    token = step(qkv_sent, pair_a, pair_o)
    qkv_theirs, near_o = gate([qkv_theirs, near_o], token)
    blocks = TOK_DEV // BLK
    docs = doc_ids[0]
    own_docs = lax.dynamic_slice_in_dim(docs, ctx_at * blocks, blocks)
    lows = jnp.sum((docs[None, :] < own_docs[:, None]).astype(jnp.int32), axis=1)
    lows = lows + (n_ctx - 1 - ctx_at) * blocks
    out_z = jnp.stack([near_o[0], far_o, near_o[1]])
    out_mine = links.gather_plane(out_z)

    def three_z(own, far, near):
        return jnp.concatenate([first_half(near), far, second_half(near)], axis=0)

    qkv_full, gains, normed, q_t, kv = project(
        place, x_in, cosines, sines, after(qkv_own, token, out_z), qkv_mine, qkv_theirs
    )
    spans = [links.later(kv, d, 1) for d in range(n_ctx - 1, 0, -1)] + [kv]
    token = step(kv)
    *spans, far_a = gate([*spans[:-1], far_a], token)
    spans = [*spans, kv]
    out_mine = gate(out_mine, token)
    out_theirs = links.core(jnp.stack(out_mine))
    first_a = jnp.concatenate([near_a, far_a], axis=0)
    rest_a = [links.plane(first_a, bits) for bits in (1, 2, 3)]
    far_b = links.swap(after(unit_b, first_a), df=2)
    attn_t, log_total = attend(lows, after(q_t, first_a), spans)
    far_b, out_theirs = gate([far_b, out_theirs], attn_t)
    pair_b = jnp.concatenate([unit_b, far_b], axis=0)
    near_b = links.swap(pair_b, df=1)
    dy_oth = links.core(dy_own)
    out_full, hidden, normed_mlp = project_out(
        place, x_in, gains, after(attn_t, step(pair_b)), w_out, out_mine, out_theirs
    )

    x_oth = links.core(normed_mlp)
    near_b, *rest_a = gate([near_b, *rest_a], hidden)
    first_b = three_z(unit_b, far_b, near_b)
    rest_b = [links.plane(first_b, bits) for bits in (1, 2, 3)]
    mlp_weights = (w_gate_up, down_t, halves, half_down)
    tokens_mlp = (after(normed_mlp, first_b), x_oth, dy_own, dy_oth)
    results_a, keep_a, send_a = mlp_chunk(
        place, 0, tokens_mlp, mlp_weights, [first_a, *rest_a]
    )
    arrived_a = links.send_one(send_a)
    rest_b = gate(rest_b, results_a[0])
    results_b, keep_b, send_b = mlp_chunk(
        place,
        1,
        (normed_mlp, x_oth, dy_own, dy_oth),
        mlp_weights,
        [first_b, *rest_b],
        (results_a[1], results_a[3]),
    )

    dn_oth = [links.core(part) for part in (first_half(results_b[3]), second_half(results_b[3]))]
    out_oth = links.core(results_b[1])
    d_hidden, d_hidden_b, d_attn_t, mlp_gain_grad = middle(
        hidden, dy_own, gains, (results_a[2], results_b[2], *dn_oth), out_full
    )
    stay_a, move_a = sum_one(keep_a, gate(arrived_a, d_hidden))
    arrived_a = links.send_two(move_a)
    arrived_b = links.send_one(gate(send_b, *move_a))
    dq_t, d_spans = attend_back(
        lows, q_t, attn_t, after(d_attn_t, *move_a), log_total, cosines, sines, spans
    )
    arrived = [
        links.later(value, d, -1) for value, d in zip(d_spans, range(n_ctx - 1, 0, -1))
    ]
    total_a = links.sum_two(stay_a, gate(arrived_a, dq_t))
    arrived_a = links.swap(total_a[1], df=1)
    stay_b, move_b = sum_one(keep_b, gate(arrived_b, dq_t))
    arrived_b = links.send_two(move_b)
    halves_o, theirs_o = early(
        place, normed, after(dq_t, *total_a, *move_b), attn_t, d_hidden_b
    )
    arrived_o = links.core(theirs_o)
    left_a = add(total_a[0], after(arrived_a, halves_o[0]))
    arrived_a = links.swap(second_half(left_a), df=2)
    total_b = links.sum_two(stay_b, gate(arrived_b, halves_o[0]))
    arrived_b = links.swap(total_b[1], df=1)
    halves_o = [add(value, more) for value, more in zip(halves_o, arrived_o)]
    arrived_o = links.send_one(halves_o[2:])
    input_grad, halves_q, theirs_q = last(
        place,
        x_in,
        gains,
        normed,
        after(dq_t, left_a, *halves_o),
        cosines,
        sines,
        qkv_full,
        d_hidden,
        mlp_gain_grad,
        d_spans[-1],
        arrived,
    )
    arrived_q = links.core(theirs_q)
    stay_o, move_o = sum_one(halves_o[:2], gate(arrived_o, input_grad))
    arrived_o = links.send_two(move_o)
    left_b = add(total_b[0], after(arrived_b, input_grad))
    arrived_b = links.swap(second_half(left_b), df=2)
    total_a = add(first_half(left_a), after(arrived_a, input_grad))
    halves_q = [add(value, more) for value, more in zip(halves_q, arrived_q)]
    arrived_q = links.send_one(halves_q[2:])
    token = step(*halves_q, *move_o, left_b, total_a)
    stay_q, move_q = sum_one(halves_q[:2], gate(arrived_q, token))
    arrived_q = links.send_two(move_q)
    total_o = links.sum_two(stay_o, gate(arrived_o, token))
    arrived_o = links.swap(total_o[1], df=1)
    total_b = add(first_half(left_b), after(arrived_b, token))
    unit_mlp = jnp.concatenate([total_a, total_b], axis=1)
    mlp_x = links.plane(after(unit_mlp, *move_q), 1)
    mlp_y = links.plane(after(unit_mlp, *move_q), 2)
    token = step(*move_q, *total_o, unit_mlp)
    total_q = links.sum_two(stay_q, gate(arrived_q, token))
    units_q = [first_half(total_q[0]), first_half(total_q[1])]
    units_q += [second_half(total_q[0]), second_half(total_q[1])]
    arrived_q = [links.swap(units_q[bits], df=bits) for bits in (1, 2, 3)]
    result = hidden + results_a[0].astype(F32) + results_b[0].astype(F32)
    result = result + out_oth.astype(F32)
    output = result.astype(BF16).T[None]
    left_o = add(total_o[0], after(arrived_o, output))
    arrived_o = links.swap(second_half(left_o), df=2)
    token = step(*units_q, left_o)
    done_q = units_q[0].astype(F32)
    for value in gate(arrived_q, token):
        done_q = done_q + value.astype(F32)
    done_o = add(first_half(left_o), after(arrived_o, token))
    rows = jnp.concatenate([done_o, done_q.astype(BF16)], axis=1)
    row_far = links.plane(rows, 2)
    mlp_top = links.plane(after(mlp_y[:TILE], rows), 1)
    mlp_low = links.plane(after(mlp_x[TILE:], rows), 2)
    mlp_oth = links.core(jnp.stack([unit_mlp, mlp_x, mlp_y]))
    near = jnp.stack([rows, row_far])
    far = links.plane(near, 1)
    near_oth = links.core(near)
    mlp_xy = jnp.concatenate([mlp_top, mlp_low], axis=0)
    xy_oth = links.core(mlp_xy)
    grad_gate_up, grad_down = finish_mlp(
        place, [unit_mlp, mlp_x, mlp_y, mlp_xy, mlp_oth, xy_oth]
    )
    far = after(far, grad_gate_up)
    far_oth = links.core(far)
    grad_qkv, grad_out, gain_rows = finish_rows(
        place, [near, far, near_oth, far_oth], 2, grad_gate_up
    )
    return (
        output,
        input_grad.T[None],
        gain_rows[0, :ROWS],
        grad_qkv,
        grad_out,
        gain_rows[1, :ROWS],
        grad_gate_up,
        grad_down.T,
    )


def solution(mesh):
    placed = (
        P(("seq", "fsdp"), "ctx", None),
        P(("seq", "fsdp"), "ctx", None),
        P(("seq", "fsdp"), "ctx"),
        P(("seq", "fsdp"), None),
        P("fsdp"),
        P("fsdp", None),
        P("fsdp", None),
        P("fsdp"),
        P("fsdp", None),
        P("fsdp", None),
    )
    links = Links([mesh.shape[name] for name in AXES])
    return jax.shard_map(
        functools.partial(shards, links),
        mesh=mesh,
        in_specs=placed,
        out_specs=(
            P(("seq", "fsdp"), "ctx", None),
            P(("seq", "fsdp"), "ctx", None),
            P("fsdp"),
            P("fsdp", None),
            P("fsdp", None),
            P("fsdp"),
            P("fsdp", None),
            P("fsdp", None),
        ),
        check_vma=False,
    )
```

```python
import functools

import jax
import jax.numpy as jnp
from jax import lax
from jax.experimental import pallas as pl
from jax.experimental.pallas import tpu as pltpu
from jax.sharding import PartitionSpec as P

D = 960
HEADS = 15
KV_HEADS = 5
HEAD_DIM = 64
FF = 2560
BLK = 128
TOK_DEV = 512
KV_DIM = 320
QKV = D + 2 * KV_DIM
QKV_WIDE = 1664
CUT = 896
EARLY_WIDE = 1920
FF_SHARD = FF // 4
ROWS = D // 4
ROWS_PAD = 256
SLICE = 32
TILE = 128
HALF = 64
ROW_TILE = 256
VMEM_LIMIT = 56 * 1024 * 1024

EPSILON = 1e-05
ROPE_BASE = 100000.0
MASKED_SCORE = -1e30
AXES = ("seq", "ctx", "fsdp")
F32 = jnp.float32
BF16 = jnp.bfloat16
ANY = pl.BlockSpec(memory_space=pl.ANY)
SMEM = pl.BlockSpec(memory_space=pltpu.SMEM)
VMEM = pl.BlockSpec(memory_space=pltpu.VMEM)
LONG = pl.CostEstimate(flops=40_000_000_000, bytes_accessed=1000, transcendentals=0)
SHORT = pl.CostEstimate(flops=1000, bytes_accessed=1000, transcendentals=0)
NT = (((1,), (1,)), ((), ()))
TN = (((0,), (0,)), ((), ()))


def frequencies():
    steps = jnp.arange(HEAD_DIM // 2, dtype=F32) * 2.0 / HEAD_DIM
    return ROPE_BASE ** (-steps)


def after(value, *earlier):
    return lax.optimization_barrier((value, *earlier))[0]


def gate(values, *earlier):
    return [after(value, *earlier) for value in values]


def step_kernel(before, behind):
    behind[...] = before[...]


def step(*needed):
    shape = jax.ShapeDtypeStruct((8, 128), F32)
    token = after(jnp.zeros(shape.shape, F32), *needed)
    return pl.pallas_call(
        step_kernel, out_shape=shape, in_specs=[VMEM], out_specs=VMEM, cost_estimate=LONG
    )(token)


def add(first, second):
    return (first.astype(F32) + second.astype(F32)).astype(BF16)


def sum_one(keep, arrived):
    pairs = list(zip(keep, arrived))
    stay = [value[0].astype(F32) + more[0].astype(F32) for value, more in pairs]
    return stay, [add(value[1], more[1]) for value, more in pairs]


def first_half(value):
    return value[: value.shape[0] // 2]


def second_half(value):
    return value[value.shape[0] // 2 :]


class Links:
    def __init__(self, sizes):
        self.sizes = sizes

    def index(self, s, c, f):
        return (s * self.sizes[1] + c) * self.sizes[2] + f

    def swap(self, value, ds=0, dc=0, df=0):
        n_s, n_c, n_f = self.sizes
        pairs = [
            (self.index(s, c, f), self.index(s ^ ds, c ^ dc, f ^ df))
            for s in range(n_s)
            for c in range(n_c)
            for f in range(n_f)
        ]
        return lax.ppermute(value, AXES, pairs)

    def later(self, value, blocks, sign):
        n_s, n_c, n_f = self.sizes
        pairs = []
        for s in range(n_s):
            for c in range(n_c - blocks):
                for f in range(n_f):
                    pair = (self.index(s, c, f), self.index(s, c + blocks, f))
                    pairs.append(pair if sign > 0 else pair[::-1])
        return lax.ppermute(value, AXES, pairs)

    def core(self, value):
        return self.swap(value, ds=1)

    def plane(self, value, bits):
        return self.swap(value, ds=bits & 2, dc=bits & 1)

    def gather_plane(self, own):
        return [own] + [self.plane(own, bits) for bits in (1, 2, 3)]

    def gather_z(self, own):
        return [self.swap(own, df=bits) for bits in (1, 2, 3)]

    def send_one(self, send):
        return [self.plane(value, bits) for value, bits in zip(send, (1, 2))]

    def send_two(self, move):
        return [self.plane(value, bits) for value, bits in zip(move, (2, 1))]

    def sum_two(self, stay, arrived):
        pairs = zip(stay, arrived)
        return [self.sum_ctx((value + more.astype(F32)).astype(BF16)) for value, more in pairs]

    def sum_ctx(self, value):
        step = 2
        while step < self.sizes[1]:
            value = add(value, self.swap(value, dc=step))
            step *= 2
        return value

    def gather_pairs(self, own, first):
        near = jnp.stack([own, self.plane(own, first)])
        far = self.plane(near, 3 - first)
        return near, far, self.core(near), self.core(far)


def piece_index(first, q):
    return (q & (3 - first)) // (3 - first), (q & first) // first


UNIT_TILES = (5, 3)
HIDDEN = (768, 512)
DOWN_AT = (3, 2)


def mlp_kernel(chunk, place, x_own, x_oth, dy_own, dy_oth, gate_up, w_down, halves, half_down, *rest):
    messages, rest = rest[:4], rest[4:]
    if chunk:
        carried, rest = rest[:2], rest[2:]
    results, (keep_x, keep_y, send_x, send_y), rest = rest[:4], rest[4:8], rest[8:]
    weight, drop, drop_half, act, dgu, units, x_t, dy_t, x, dy, out_t, dn_t, sems = rest
    hidden, down_at = HIDDEN[chunk], DOWN_AT[chunk]
    with_half = chunk == 0
    p, k, f = place[0], place[1], place[2]
    groups = ([], [], [])

    def copy(source, target, group):
        groups[group].append(pltpu.make_async_copy(source, target, sems.at[group]))

    for half, (xs, ds) in enumerate(((x_own, dy_own), (x_oth, dy_oth))):
        lanes = pl.ds(half * TOK_DEV, TOK_DEV)
        copy(xs, x_t.at[:, lanes], 0)
        copy(ds, dy_t.at[:, lanes], 1)
    if chunk:
        for source, target in zip(carried, (out_t, dn_t)):
            copy(source, target.at[:, pl.ds(TOK_DEV, TOK_DEV)], 1)
    tile_of_core = 2 * k + chunk
    for kind in range(2):
        for z in range(4):
            col = pl.multiple_of(kind * FF + z * FF_SHARD + tile_of_core * TILE, TILE)
            copy(
                gate_up.at[:, pl.ds(col, TILE)],
                weight.at[f, :, pl.ds(kind * hidden + z * TILE, TILE)],
                1,
            )
        if with_half:
            copy(
                halves.at[:, pl.ds(kind * 2 * TILE, 2 * TILE)],
                weight.at[f, :, pl.ds(kind * hidden + 4 * TILE, 2 * TILE)],
                1,
            )
    copy(
        w_down.at[:, pl.ds(pl.multiple_of(tile_of_core * TILE, TILE), TILE)],
        drop.at[:, pl.ds(pl.multiple_of(f * TILE, TILE), TILE)],
        1,
    )
    if with_half:
        copy(half_down, drop_half.at[f], 1)
    for q, ref in enumerate(messages):
        pp = jnp.bitwise_xor(p, q)
        for r in range(3):
            z = jnp.bitwise_xor(f, r + 1)
            rows = pl.ds(r * ROWS, ROWS)
            for kind in range(2):
                lane = pl.multiple_of(kind * hidden + pp * TILE, TILE)
                copy(
                    ref.at[rows, pl.ds(kind * TILE, TILE)],
                    weight.at[z, :, pl.ds(lane, TILE)],
                    1,
                )
            rows_at = pl.ds(pl.multiple_of(pp * ROWS, 16), ROWS)
            copy(
                ref.at[rows, pl.ds(down_at * TILE, TILE)],
                drop.at[rows_at, pl.ds(pl.multiple_of(z * TILE, TILE), TILE)],
                1,
            )
            if with_half:
                lane = jnp.right_shift(pp, 1) * hidden + 4 * TILE + jnp.bitwise_and(pp, 1) * TILE
                copy(
                    ref.at[rows, pl.ds(2 * TILE, TILE)],
                    weight.at[z, :, pl.ds(pl.multiple_of(lane, TILE), TILE)],
                    1,
                )
                copy(ref.at[rows, pl.ds(4 * TILE, TILE)], drop_half.at[z, rows_at], 1)
    for group in groups:
        for each in group:
            each.start()
    for each in groups[0]:
        each.wait()
    x[...] = x_t[...].T
    for each in groups[1]:
        each.wait()
    dy[...] = dy_t[...].T
    if with_half:
        for z in range(4):
            lane = 4 * TILE + z * HALF
            drop[:, lane : lane + HALF] = drop_half[z, :, :HALF]

    for t in range(2 * TOK_DEV // ROW_TILE):
        rows = slice(t * ROW_TILE, (t + 1) * ROW_TILE)
        both = weight[...].reshape(D, 2 * hidden)
        gu = jnp.dot(x[rows, :], both, preferred_element_type=F32)
        da = jnp.dot(dy[rows, :], drop[...], preferred_element_type=F32)
        g, u = gu[:, :hidden], gu[:, hidden:]
        sig = jax.nn.sigmoid(g)
        silu = g * sig
        a = (silu * u).astype(BF16)
        act[rows, :] = a
        dgu[rows, :hidden] = (da * u * (sig + silu * (1.0 - sig))).astype(BF16)
        dgu[rows, hidden:] = (da * silu).astype(BF16)
        out = lax.dot_general(drop[...], a, NT, preferred_element_type=F32)
        dn = lax.dot_general(both, dgu[rows, :], NT, preferred_element_type=F32)
        if chunk and t * ROW_TILE >= TOK_DEV:
            out = out + out_t[:, rows].astype(F32)
            dn = dn + dn_t[:, rows].astype(F32)
        out_t[:, rows] = out.astype(BF16)
        dn_t[:, rows] = dn.astype(BF16)

    groups = ([], [], [])
    for at, ref in enumerate((out_t, dn_t)):
        for half in range(2):
            copy(ref.at[:, pl.ds(half * TOK_DEV, TOK_DEV)], results[2 * at + half], 2)
    for each in groups[2]:
        each.start()

    step = 2 * TILE
    for start in range(0, hidden, step):
        grad = jnp.dot(
            dy_t[...], act[:, start : start + step], preferred_element_type=F32
        ).astype(BF16)
        if start < 4 * TILE:
            for part in range(2):
                z = start // TILE + part
                units[:, z, :, down_at * TILE : (down_at + 1) * TILE] = grad[
                    :, part * TILE : (part + 1) * TILE
                ].reshape(4, ROWS, TILE)
        else:
            for z in range(4):
                units[:, z, :, 4 * TILE : 4 * TILE + HALF] = grad[
                    :, z * HALF : (z + 1) * HALF
                ].reshape(4, ROWS, HALF)
    for pair in range(2):
        columns = [(kind * hidden + pair * step, kind) for kind in range(2)]
        if with_half:
            columns.append((pair * hidden + 4 * TILE, 2))
        for start, column in columns:
            grad = jnp.dot(
                x_t[...], dgu[:, start : start + step], preferred_element_type=F32
            ).astype(BF16)
            for part in range(2):
                units[2 * pair + part, :, :, column * TILE : (column + 1) * TILE] = grad[
                    :, part * TILE : (part + 1) * TILE
                ].reshape(4, ROWS, TILE)
        for pp in (2 * pair, 2 * pair + 1):
            q = jnp.bitwise_xor(p, pp)
            for bits in range(4):
                left = (keep_x, send_x)[bits & 1].at[bits >> 1]
                right = (keep_y, send_y)[bits >> 1].at[bits & 1]

                def send(pp=pp, left=left, right=right):
                    for r in range(4):
                        pltpu.make_async_copy(
                            units.at[pp, jnp.bitwise_xor(f, r)],
                            (left, right)[r & 1].at[pl.ds((r >> 1) * ROWS, ROWS)],
                            sems.at[2],
                        ).start()

                pl.when(q == bits)(send)
    for each in groups[2]:
        each.wait()
    for target in (keep_x, keep_y, send_x, send_y):
        for at in range(2):
            for r in range(2):
                pltpu.make_async_copy(
                    units.at[0, 0], target.at[at, pl.ds(r * ROWS, ROWS)], sems.at[2]
                ).wait()


def mlp_chunk(place, chunk, tokens, weights, messages, carried=()):
    hidden = HIDDEN[chunk]
    width = UNIT_TILES[chunk] * TILE
    part = jax.ShapeDtypeStruct((2, 2 * ROWS, width), BF16)
    operands = [place, *tokens, *weights, *messages, *carried]
    out = pl.pallas_call(
        functools.partial(mlp_kernel, chunk),
        out_shape=[jax.ShapeDtypeStruct((D, TOK_DEV), BF16)] * 4 + [part] * 4,
        in_specs=[SMEM] + [ANY] * (len(operands) - 1),
        out_specs=[ANY] * 8,
        scratch_shapes=[
            pltpu.VMEM((4, ROWS, 2 * hidden), BF16),
            pltpu.VMEM((D, hidden), BF16),
            pltpu.VMEM((4, D, TILE), BF16),
            pltpu.VMEM((2 * TOK_DEV, hidden), BF16),
            pltpu.VMEM((2 * TOK_DEV, 2 * hidden), BF16),
            pltpu.VMEM((4, 4, ROWS, width), BF16),
            pltpu.VMEM((D, 2 * TOK_DEV), BF16),
            pltpu.VMEM((D, 2 * TOK_DEV), BF16),
            pltpu.VMEM((2 * TOK_DEV, D), BF16),
            pltpu.VMEM((2 * TOK_DEV, D), BF16),
            pltpu.VMEM((D, 2 * TOK_DEV), BF16),
            pltpu.VMEM((D, 2 * TOK_DEV), BF16),
            pltpu.SemaphoreType.DMA((3,)),
        ],
        compiler_params=pltpu.CompilerParams(vmem_limit_bytes=VMEM_LIMIT),
        cost_estimate=LONG,
    )(*operands)
    return out[:4], out[4:6], out[6:8]


def finish_mlp_kernel(place, m0, m1, m2, m3, three_oth, xy_oth, up, down):
    p, k = place[0], place[1]
    for q, mine in enumerate((m0, m1, m2, m3)):
        theirs = three_oth.at[q] if q < 3 else xy_oth
        pp = jnp.bitwise_xor(p, q)
        rows = pl.ds(pl.multiple_of(pp * ROWS, 16), ROWS)
        for other, ref in enumerate((mine, theirs)):
            kk = jnp.bitwise_xor(k, other)
            for chunk in range(2):
                at = chunk * UNIT_TILES[0] * TILE
                for kind in range(2):
                    col = kind * FF + pp * FF_SHARD + (2 * kk + chunk) * TILE
                    lane = at + kind * TILE
                    up[:, pl.ds(pl.multiple_of(col, TILE), TILE)] = ref[
                        :, lane : lane + TILE
                    ].astype(F32)
                lane = at + DOWN_AT[chunk] * TILE
                col = pl.multiple_of((2 * kk + chunk) * TILE, TILE)
                down[rows, pl.ds(col, TILE)] = ref[:, lane : lane + TILE].astype(F32)
        own, oth = (ref[:, 2 * TILE : 3 * TILE].astype(F32) for ref in (mine, theirs))
        low, high = jnp.where(k == 0, own, oth), jnp.where(k == 0, oth, own)
        for half in range(2):
            lanes = slice(half * HALF, (half + 1) * HALF)
            z = 2 * jnp.bitwise_and(pp, 1) + half
            col = jnp.right_shift(pp, 1) * FF + z * FF_SHARD + 4 * TILE
            up[:, pl.ds(pl.multiple_of(col, TILE), TILE)] = jnp.concatenate(
                [low[:, lanes], high[:, lanes]], axis=1
            )
        lanes = slice(4 * TILE, 4 * TILE + HALF)
        own, oth = (ref[:, lanes].astype(F32) for ref in (mine, theirs))
        low, high = jnp.where(k == 0, own, oth), jnp.where(k == 0, oth, own)
        down[rows, 4 * TILE :] = jnp.concatenate([low, high], axis=1)


def finish_mlp(place, pieces):
    return pl.pallas_call(
        finish_mlp_kernel,
        out_shape=[
            jax.ShapeDtypeStruct((ROWS, 2 * FF), F32),
            jax.ShapeDtypeStruct((D, FF_SHARD), F32),
        ],
        in_specs=[SMEM] + [VMEM] * 6,
        out_specs=[VMEM] * 2,
        compiler_params=pltpu.CompilerParams(vmem_limit_bytes=VMEM_LIMIT),
        cost_estimate=SHORT,
    )(place, *pieces)


def load_rows(place, own, mine, theirs, full, sem):
    p, k, f = place[0], place[1], place[2]
    for start in (True, False):

        def run(copy, start=start):
            if start:
                copy.start()
            else:
                copy.wait()

        run(pltpu.make_async_copy(own, full.at[f], sem))
        for other in range(2):
            kk = jnp.bitwise_xor(k, other)
            for q in range(4):
                ref = theirs.at[q] if other else mine[q]
                pp = jnp.bitwise_xor(p, q)
                row = pl.multiple_of(kk * 128 + pp * SLICE, 16)
                short = (kk * 4 + pp) == 7
                for r in range(3):
                    z = jnp.bitwise_xor(f, r + 1)

                    def go(count, ref=ref, r=r, z=z, row=row):
                        run(
                            pltpu.make_async_copy(
                                ref.at[r, pl.ds(0, count)], full.at[z, pl.ds(row, count)], sem
                            )
                        )

                    pl.when(short)(functools.partial(go, 16))
                    pl.when(jnp.logical_not(short))(functools.partial(go, SLICE))


def store_rows(place, grad, halves, theirs, sem):
    p, k, f = place[0], place[1], place[2]

    def target_of(other, q, r):
        at, index = (2 * (q & 1), q >> 1) if r & 1 == 0 else (1 + 2 * (q >> 1), q & 1)
        half = theirs.at[at] if other else halves[at]
        return half.at[index, pl.ds((r >> 1) * SLICE, SLICE)]

    for start in (True, False):
        for other in range(2):
            kk = jnp.bitwise_xor(k, other)
            for q in range(4):
                pp = jnp.bitwise_xor(p, q)
                row = pl.multiple_of(kk * 128 + pp * SLICE, 16)
                short = (kk * 4 + pp) == 7
                for r in range(4):
                    z = jnp.bitwise_xor(f, r)

                    def go(count, target=target_of(other, q, r), z=z, row=row):
                        copy = pltpu.make_async_copy(
                            grad.at[z, pl.ds(row, count)], target.at[pl.ds(0, count)], sem
                        )
                        if start:
                            copy.start()
                        else:
                            copy.wait()

                    pl.when(short)(functools.partial(go, 16))
                    pl.when(jnp.logical_not(short))(functools.partial(go, SLICE))


def finish_rows_kernel(first, place, near, far, near_oth, far_oth, behind, qkv, out, gain, columns):
    p, k = place[0], place[1]
    pairs = (near, far, near_oth, far_oth)
    for other in range(2):
        kk = jnp.bitwise_xor(k, other)
        for q in range(4):
            pp = jnp.bitwise_xor(p, q)
            row = pl.multiple_of(kk * 128 + pp * SLICE, 16)
            short = (kk * 4 + pp) == 7
            side, index = piece_index(first, q)
            value = pairs[2 * other + side][index].astype(F32)

            def go(count, value=value, row=row):
                rows = pl.ds(row, count)
                qkv[rows, :CUT] = value[:count, :CUT]
                qkv[rows, CUT:] = value[:count, EARLY_WIDE : EARLY_WIDE + QKV - CUT]
                out[rows, :] = value[:count, CUT : CUT + D]
                columns[rows, : QKV_WIDE - QKV] = value[:count, EARLY_WIDE + QKV - CUT :]

            pl.when(short)(functools.partial(go, 16))
            pl.when(jnp.logical_not(short))(functools.partial(go, SLICE))
    gain[...] = columns[...].T[:8]


def finish_rows(place, pairs, first, behind):
    return pl.pallas_call(
        functools.partial(finish_rows_kernel, first),
        out_shape=[
            jax.ShapeDtypeStruct((ROWS, QKV), F32),
            jax.ShapeDtypeStruct((ROWS, D), F32),
            jax.ShapeDtypeStruct((8, 2 * TILE), F32),
        ],
        in_specs=[SMEM] + [VMEM] * 4 + [ANY],
        out_specs=[VMEM] * 3,
        scratch_shapes=[pltpu.VMEM((2 * TILE, TILE), F32)],
        compiler_params=pltpu.CompilerParams(vmem_limit_bytes=VMEM_LIMIT),
        cost_estimate=SHORT,
    )(place, *pairs, behind)


def token_scale(values):
    return lax.rsqrt(jnp.mean(values * values, axis=0, keepdims=True) + EPSILON)


def tables_kernel(positions, frequency, cosines, sines):
    angles = frequency[:, :1] * positions[...].astype(F32)
    cosines[...] = jnp.cos(angles)
    sines[...] = jnp.sin(angles)


def tables(positions):
    frequency = jnp.broadcast_to(frequencies()[:, None], (HEAD_DIM // 2, TILE))
    return pl.pallas_call(
        tables_kernel,
        out_shape=[jax.ShapeDtypeStruct((HEAD_DIM // 2, TOK_DEV), F32)] * 2,
        in_specs=[VMEM] * 2,
        out_specs=[VMEM] * 2,
        cost_estimate=LONG,
    )(positions, frequency)


def project_kernel(
    place, x, cosines, sines, own, m0, m1, m2, m3, theirs, full, gains, normed, q_t, kv, sem
):
    load_rows(place, own, (m0, m1, m2, m3), theirs, full, sem)
    weight = full[...].reshape(D, QKV_WIDE)
    columns = weight[:, QKV - HALF :].astype(F32)
    gains[...] = columns
    source = x[...].astype(F32)
    normed[...] = (source * token_scale(source) * columns[:, HALF : HALF + 1]).astype(BF16)
    mixed = lax.dot_general(weight[:, :QKV], normed[...], TN, preferred_element_type=F32)
    cos, sin = cosines[...], sines[...]
    half = HEAD_DIM // 2
    for head in range(HEADS + KV_HEADS):
        row = head * HEAD_DIM
        low, high = mixed[row : row + half], mixed[row + half : row + HEAD_DIM]
        low, high = (low * cos - high * sin).astype(BF16), (high * cos + low * sin).astype(BF16)
        if head < HEADS:
            q_t[row : row + half, :] = low
            q_t[row + half : row + HEAD_DIM, :] = high
        else:
            row -= D
            for block in range(TOK_DEV // BLK):
                lanes = slice(block * BLK, (block + 1) * BLK)
                kv[block, row : row + half, :] = low[:, lanes]
                kv[block, row + half : row + HEAD_DIM, :] = high[:, lanes]
    for block in range(TOK_DEV // BLK):
        lanes = slice(block * BLK, (block + 1) * BLK)
        kv[block, KV_DIM:, :] = mixed[D + KV_DIM :, lanes].astype(BF16)


def project(place, x, cosines, sines, own, mine, theirs):
    return pl.pallas_call(
        project_kernel,
        out_shape=[
            jax.ShapeDtypeStruct((4, ROWS, QKV_WIDE), BF16),
            jax.ShapeDtypeStruct((D, TILE), F32),
            jax.ShapeDtypeStruct((D, TOK_DEV), BF16),
            jax.ShapeDtypeStruct((D, TOK_DEV), BF16),
            jax.ShapeDtypeStruct((TOK_DEV // BLK, 2 * KV_DIM, BLK), BF16),
        ],
        in_specs=[SMEM] + [VMEM] * 3 + [ANY] * 6,
        out_specs=[VMEM] * 5,
        scratch_shapes=[pltpu.SemaphoreType.DMA(())],
        compiler_params=pltpu.CompilerParams(vmem_limit_bytes=VMEM_LIMIT),
        cost_estimate=LONG,
    )(place, x, cosines, sines, own, *mine, theirs)


def three_heads(ref, group, lanes):
    first = group * (HEADS // KV_HEADS) * HEAD_DIM
    return jnp.concatenate(
        [
            ref[first + r * HEAD_DIM : first + (r + 1) * HEAD_DIM, lanes]
            for r in range(HEADS // KV_HEADS)
        ],
        axis=1,
    )


def diagonal_mask():
    shape = (BLK, BLK * (HEADS // KV_HEADS))
    keys = lax.broadcasted_iota(jnp.int32, shape, 0)
    queries = jnp.bitwise_and(lax.broadcasted_iota(jnp.int32, shape, 1), BLK - 1)
    return keys <= queries


def attend_kernel(lows, q_t, *rest):
    spans = rest[:-6]
    attn_t, log_total, kv, best, total, accum = rest[-6:]
    blocks = TOK_DEV // BLK
    for at, ref in enumerate(spans):
        kv[at * blocks : (at + 1) * blocks] = ref[...]
    own_at = (len(spans) - 1) * blocks
    mask = diagonal_mask()
    for i in range(blocks):
        lanes = slice(i * BLK, (i + 1) * BLK)
        queries = [
            three_heads(q_t, group, lanes) * jnp.asarray(HEAD_DIM**-0.5, BF16)
            for group in range(KV_HEADS)
        ]

        def step(j, diagonal, queries=queries):
            for group in range(KV_HEADS):
                keys = kv[j, group * HEAD_DIM : (group + 1) * HEAD_DIM, :]
                values = kv[j, KV_DIM + group * HEAD_DIM : KV_DIM + (group + 1) * HEAD_DIM, :]
                scores = lax.dot_general(keys, queries[group], TN, preferred_element_type=F32)
                if diagonal:
                    scores = jnp.where(mask, scores, MASKED_SCORE)
                    top = jnp.max(scores, axis=0, keepdims=True)
                    expo = jnp.exp(scores - top)
                    total[group] = jnp.sum(expo, axis=0, keepdims=True)
                    accum[group] = jnp.dot(values, expo.astype(BF16), preferred_element_type=F32)
                else:
                    old = best[group]
                    top = jnp.maximum(old, jnp.max(scores, axis=0, keepdims=True))
                    decay = jnp.exp(old - top)
                    expo = jnp.exp(scores - top)
                    total[group] = total[group] * decay + jnp.sum(expo, axis=0, keepdims=True)
                    accum[group] = accum[group] * decay + jnp.dot(
                        values, expo.astype(BF16), preferred_element_type=F32
                    )
                best[group] = top

        step(own_at + i, True)

        @pl.loop(lows[i], own_at + i)
        def earlier(j):
            step(j, False)

        for group in range(KV_HEADS):
            attn = (accum[group] / total[group]).astype(BF16)
            first = group * (HEADS // KV_HEADS) * HEAD_DIM
            for r in range(HEADS // KV_HEADS):
                attn_t[first + r * HEAD_DIM : first + (r + 1) * HEAD_DIM, lanes] = attn[
                    :, r * BLK : (r + 1) * BLK
                ]
            log_total[i * KV_HEADS + group] = best[group] + jnp.log(total[group])


def attend(lows, q_t, spans):
    blocks = TOK_DEV // BLK
    wide = BLK * (HEADS // KV_HEADS)
    return pl.pallas_call(
        attend_kernel,
        out_shape=[
            jax.ShapeDtypeStruct((D, TOK_DEV), BF16),
            jax.ShapeDtypeStruct((blocks * KV_HEADS, 1, wide), F32),
        ],
        in_specs=[SMEM] + [VMEM] * (1 + len(spans)),
        out_specs=[VMEM] * 2,
        scratch_shapes=[
            pltpu.VMEM((len(spans) * blocks, 2 * KV_DIM, BLK), BF16),
            pltpu.VMEM((KV_HEADS, 1, wide), F32),
            pltpu.VMEM((KV_HEADS, 1, wide), F32),
            pltpu.VMEM((KV_HEADS, HEAD_DIM, wide), F32),
        ],
        compiler_params=pltpu.CompilerParams(vmem_limit_bytes=VMEM_LIMIT),
        cost_estimate=LONG,
    )(lows, q_t, *spans)


def out_kernel(place, x, gains, attn_t, own, m0, m1, m2, m3, theirs, full, hidden, normed, sem):
    load_rows(place, own, (m0, m1, m2, m3), theirs, full, sem)
    value = x[...].astype(F32) + lax.dot_general(
        full[...].reshape(D, D), attn_t[...], TN, preferred_element_type=F32
    )
    hidden[...] = value
    normed[...] = (value * token_scale(value) * gains[:, HALF + 1 : HALF + 2]).astype(BF16)


def project_out(place, x, gains, attn_t, own, mine, theirs):
    return pl.pallas_call(
        out_kernel,
        out_shape=[
            jax.ShapeDtypeStruct((4, ROWS, D), BF16),
            jax.ShapeDtypeStruct((D, TOK_DEV), F32),
            jax.ShapeDtypeStruct((D, TOK_DEV), BF16),
        ],
        in_specs=[SMEM] + [VMEM] * 3 + [ANY] * 6,
        out_specs=[VMEM] * 3,
        scratch_shapes=[pltpu.SemaphoreType.DMA(())],
        compiler_params=pltpu.CompilerParams(vmem_limit_bytes=VMEM_LIMIT),
        cost_estimate=SHORT,
    )(place, x, gains, attn_t, own, *mine, theirs)


def norm_back(value, scale, gain, dn):
    unit = value * scale
    weighted = dn * gain
    d_value = scale * (weighted - unit * jnp.mean(weighted * unit, axis=0, keepdims=True))
    return d_value, jnp.sum(dn * unit, axis=1, keepdims=True)


def middle_kernel(
    hidden, dy, gains, dn0, dn1, dn2, dn3, full, d_hidden, d_hidden_b, d_attn_t, grad_gain
):
    value = hidden[...]
    dn = jnp.concatenate([dn2[...], dn3[...]], axis=0).astype(F32)
    dn = dn0[...].astype(F32) + dn1[...].astype(F32) + dn
    d_value, column = norm_back(value, token_scale(value), gains[:, HALF + 1 : HALF + 2], dn)
    grad_gain[...] = jnp.broadcast_to(column, (D, TILE))
    dh = dy[...].astype(F32) + d_value
    d_hidden[...] = dh
    dh = dh.astype(BF16)
    d_hidden_b[...] = dh
    d_attn_t[...] = jnp.dot(
        full[...].reshape(D, D), dh, preferred_element_type=F32
    ).astype(BF16)


def middle(hidden, dy, gains, dns, full):
    return pl.pallas_call(
        middle_kernel,
        out_shape=[
            jax.ShapeDtypeStruct((D, TOK_DEV), F32),
            jax.ShapeDtypeStruct((D, TOK_DEV), BF16),
            jax.ShapeDtypeStruct((D, TOK_DEV), BF16),
            jax.ShapeDtypeStruct((D, TILE), F32),
        ],
        in_specs=[VMEM] * 8,
        out_specs=[VMEM] * 4,
        compiler_params=pltpu.CompilerParams(vmem_limit_bytes=VMEM_LIMIT),
        cost_estimate=SHORT,
    )(hidden, dy, gains, *dns, full)


def attend_back_kernel(count, lows, q_t, attn_t, d_attn_t, log_total, cosines, sines, *rest):
    spans, rest = rest[:count], rest[count:]
    dq_t, d_spans, (kv, d_kv, d_query) = rest[0], rest[1 : 1 + count], rest[1 + count :]
    blocks = TOK_DEV // BLK
    groups = HEADS // KV_HEADS
    half = HEAD_DIM // 2
    for at, ref in enumerate(spans):
        kv[at * blocks : (at + 1) * blocks] = ref[...]
    d_kv[...] = jnp.zeros_like(d_kv)
    own_at = (count - 1) * blocks
    mask = diagonal_mask()
    for i in range(blocks):
        lanes = slice(i * BLK, (i + 1) * BLK)
        queries, d_outs, deltas = [], [], []
        for group in range(KV_HEADS):
            queries.append(three_heads(q_t, group, lanes) * jnp.asarray(HEAD_DIM**-0.5, BF16))
            d_out = three_heads(d_attn_t, group, lanes)
            attn = three_heads(attn_t, group, lanes)
            d_outs.append(d_out)
            deltas.append(
                jnp.sum(d_out.astype(F32) * attn.astype(F32), axis=0, keepdims=True)
            )

        def step(j, diagonal, i=i, queries=queries, d_outs=d_outs, deltas=deltas):
            for group in range(KV_HEADS):
                key_rows = slice(group * HEAD_DIM, (group + 1) * HEAD_DIM)
                value_rows = slice(KV_DIM + group * HEAD_DIM, KV_DIM + (group + 1) * HEAD_DIM)
                keys, values = kv[j, key_rows, :], kv[j, value_rows, :]
                scores = lax.dot_general(keys, queries[group], TN, preferred_element_type=F32)
                if diagonal:
                    scores = jnp.where(mask, scores, MASKED_SCORE)
                prob = jnp.exp(scores - log_total[i * KV_HEADS + group])
                d_prob = lax.dot_general(values, d_outs[group], TN, preferred_element_type=F32)
                d_scores = (prob * (d_prob - deltas[group])).astype(BF16)
                d_kv[j, value_rows, :] += lax.dot_general(
                    d_outs[group], prob.astype(BF16), NT, preferred_element_type=F32
                )
                d_kv[j, key_rows, :] += lax.dot_general(
                    queries[group], d_scores, NT, preferred_element_type=F32
                )
                more = jnp.dot(keys, d_scores, preferred_element_type=F32)
                if diagonal:
                    d_query[group] = more
                else:
                    d_query[group] += more

        step(own_at + i, True)

        @pl.loop(lows[i], own_at + i)
        def earlier(j):
            step(j, False)

        cos, sin = cosines[:, lanes], sines[:, lanes]
        for group in range(KV_HEADS):
            for r in range(groups):
                row = (group * groups + r) * HEAD_DIM
                side = slice(r * BLK, (r + 1) * BLK)
                low = d_query[group, :half, side] * HEAD_DIM**-0.5
                high = d_query[group, half:, side] * HEAD_DIM**-0.5
                dq_t[row : row + half, lanes] = (low * cos + high * sin).astype(BF16)
                dq_t[row + half : row + HEAD_DIM, lanes] = (high * cos - low * sin).astype(BF16)
    for at, ref in enumerate(d_spans):
        ref[...] = d_kv[at * blocks : (at + 1) * blocks].astype(ref.dtype)


def attend_back(lows, q_t, attn_t, d_attn_t, log_total, cosines, sines, spans):
    blocks = TOK_DEV // BLK
    wide = BLK * (HEADS // KV_HEADS)
    count = len(spans)
    shape = (blocks, 2 * KV_DIM, BLK)
    out = pl.pallas_call(
        functools.partial(attend_back_kernel, count),
        out_shape=[jax.ShapeDtypeStruct((D, TOK_DEV), BF16)]
        + [jax.ShapeDtypeStruct(shape, BF16)] * (count - 1)
        + [jax.ShapeDtypeStruct(shape, F32)],
        in_specs=[SMEM] + [VMEM] * (6 + count),
        out_specs=[VMEM] * (1 + count),
        scratch_shapes=[
            pltpu.VMEM((count * blocks, 2 * KV_DIM, BLK), BF16),
            pltpu.VMEM((count * blocks, 2 * KV_DIM, BLK), F32),
            pltpu.VMEM((KV_HEADS, HEAD_DIM, wide), F32),
        ],
        compiler_params=pltpu.CompilerParams(vmem_limit_bytes=VMEM_LIMIT),
        cost_estimate=LONG,
    )(lows, q_t, attn_t, d_attn_t, log_total, cosines, sines, *spans)
    return out[0], out[1:]


def early_kernel(place, normed, dq_t, attn_t, dh, *rest):
    halves, theirs, grad, sem = rest[:4], rest[4], rest[5], rest[6]
    product = lax.dot_general(attn_t[...], dh[...], NT, preferred_element_type=F32)
    grad[:, :, CUT : CUT + D] = product.astype(BF16).reshape(4, ROWS, D)
    product = lax.dot_general(normed[...], dq_t[:CUT, :], NT, preferred_element_type=F32)
    grad[:, :, :CUT] = product.astype(BF16).reshape(4, ROWS, CUT)
    store_rows(place, grad, halves, theirs, sem)


def early(place, normed, dq_t, attn_t, dh):
    piece = jax.ShapeDtypeStruct((2, 2 * SLICE, EARLY_WIDE), BF16)
    out = pl.pallas_call(
        early_kernel,
        out_shape=[*[piece] * 4, jax.ShapeDtypeStruct((4, 2, 2 * SLICE, EARLY_WIDE), BF16)],
        in_specs=[SMEM] + [VMEM] * 4,
        out_specs=[ANY] * 5,
        scratch_shapes=[pltpu.VMEM((4, ROWS, EARLY_WIDE), BF16), pltpu.SemaphoreType.DMA(())],
        compiler_params=pltpu.CompilerParams(vmem_limit_bytes=VMEM_LIMIT),
        cost_estimate=LONG,
    )(place, normed, dq_t, attn_t, dh)
    return out[:4], out[4]


def last_kernel(
    count, place, x, gains, normed, dq_t, cosines, sines, full, d_hidden, mlp_gain_grad, d_own, *rest
):
    arrived, rest = rest[:count], rest[count:]
    input_grad, halves, theirs, d_mixed, grad, sem = rest[0], rest[1:5], rest[5], *rest[6:]
    half = HEAD_DIM // 2
    d_mixed[:D, :] = dq_t[...]
    for block in range(TOK_DEV // BLK):
        lanes = slice(block * BLK, (block + 1) * BLK)
        value = d_own[block]
        for ref in arrived:
            value = value + ref[block].astype(F32)
        cos, sin = cosines[:, lanes], sines[:, lanes]
        for head in range(KV_HEADS):
            row = head * HEAD_DIM
            low, high = value[row : row + half], value[row + half : row + HEAD_DIM]
            d_mixed[D + row : D + row + half, lanes] = (low * cos + high * sin).astype(BF16)
            d_mixed[D + row + half : D + row + HEAD_DIM, lanes] = (high * cos - low * sin).astype(
                BF16
            )
        d_mixed[D + KV_DIM :, lanes] = value[KV_DIM:].astype(BF16)
    product = lax.dot_general(normed[...], d_mixed[CUT:, :], NT, preferred_element_type=F32)
    grad[:, :, : QKV - CUT] = product.astype(BF16).reshape(4, ROWS, QKV - CUT)
    weight = full[...].reshape(D, QKV_WIDE)[:, :QKV]
    dn = jnp.dot(weight, d_mixed[...], preferred_element_type=F32)
    source = x[...].astype(F32)
    d_value, column = norm_back(source, token_scale(source), gains[:, HALF : HALF + 1], dn)
    input_grad[...] = (d_hidden[...] + d_value).astype(BF16)
    lane = lax.broadcasted_iota(jnp.int32, (D, QKV_WIDE - QKV), 1)
    both = jnp.where(lane == 0, column, mlp_gain_grad[:, : QKV_WIDE - QKV])
    grad[:, :, QKV - CUT :] = both.astype(BF16).reshape(4, ROWS, QKV_WIDE - QKV)
    store_rows(place, grad, halves, theirs, sem)


def last(place, x, gains, normed, dq_t, cosines, sines, full, d_hidden, mlp_gain_grad, d_own, arrived):
    width = QKV_WIDE - CUT
    piece = jax.ShapeDtypeStruct((2, 2 * SLICE, width), BF16)
    out = pl.pallas_call(
        functools.partial(last_kernel, len(arrived)),
        out_shape=[
            jax.ShapeDtypeStruct((D, TOK_DEV), BF16),
            *[piece] * 4,
            jax.ShapeDtypeStruct((4, 2, 2 * SLICE, width), BF16),
        ],
        in_specs=[SMEM] + [VMEM] * (10 + len(arrived)),
        out_specs=[VMEM] + [ANY] * 5,
        scratch_shapes=[
            pltpu.VMEM((QKV, TOK_DEV), BF16),
            pltpu.VMEM((4, ROWS, width), BF16),
            pltpu.SemaphoreType.DMA(()),
        ],
        compiler_params=pltpu.CompilerParams(vmem_limit_bytes=VMEM_LIMIT),
        cost_estimate=LONG,
    )(place, x, gains, normed, dq_t, cosines, sines, full, d_hidden, mlp_gain_grad, d_own, *arrived)
    return out[0], out[1:5], out[5]


def shards(
    links,
    tokens,
    cotangent,
    positions,
    doc_ids,
    gain_attn,
    w_qkv,
    w_out,
    gain_mlp,
    w_gate_up,
    w_down,
):
    seq_at, ctx_at, f = (lax.axis_index(name) for name in AXES)
    k = jnp.bitwise_and(seq_at, 1)
    p = 2 * jnp.right_shift(seq_at, 1) + jnp.bitwise_and(ctx_at, 1)
    place = jnp.stack([p, k, f]).astype(jnp.int32)
    n_ctx = links.sizes[1]
    x_in, dy_own = tokens[0].T, cotangent[0].T

    def row_slice(weight):
        padded = jnp.pad(weight, ((0, ROWS_PAD - ROWS), (0, 0)))
        return lax.dynamic_slice_in_dim(padded, k * 128 + p * SLICE, SLICE, 0)

    def core_half(pair):
        return jnp.where(k == 0, pair[:, :HALF], pair[:, HALF:])

    halves = jnp.concatenate(
        [core_half(w_gate_up[:, at : at + TILE]) for at in range(4 * TILE, 2 * FF, FF_SHARD)],
        axis=1,
    )
    down_t = w_down.T
    half_down = jnp.pad(core_half(down_t[:, 4 * TILE :]), ((0, 0), (0, HALF)))

    def unit(chunk):
        tiles = []
        for kind in range(2):
            col = kind * FF + p * FF_SHARD + (2 * k + chunk) * TILE
            tiles.append(lax.dynamic_slice_in_dim(w_gate_up, col, TILE, 1))
        if chunk == 0:
            tiles.append(lax.dynamic_slice_in_dim(halves, p * TILE, TILE, 1))
        tiles.append(
            lax.dynamic_slice(down_t, (p * ROWS, (2 * k + chunk) * TILE), (ROWS, TILE))
        )
        if chunk == 0:
            tiles.append(lax.dynamic_slice_in_dim(half_down, p * ROWS, ROWS, 0))
        return jnp.concatenate(tiles, axis=1)

    pair = jnp.stack([gain_attn, gain_mlp], axis=1)
    gain_columns = jnp.pad(pair, ((0, 0), (0, QKV_WIDE - QKV - 2)))
    qkv_own = jnp.concatenate([w_qkv, gain_columns], axis=1)
    qkv_slice = jnp.concatenate([row_slice(w_qkv), row_slice(gain_columns)], axis=1)
    out_slice = row_slice(w_out)
    unit_a, unit_b = unit(0), unit(1)
    qkv_z = links.gather_z(qkv_slice)
    far_o = links.swap(out_slice, df=2)
    qkv_mine = links.gather_plane(jnp.stack(qkv_z))
    near_a = links.swap(after(unit_a, *qkv_z), df=1)
    cosines, sines = tables(after(positions, *qkv_z))
    near_a, far_o, *qkv_mine = gate([near_a, far_o, *qkv_mine], cosines)
    qkv_sent = jnp.stack(qkv_mine)
    pair_a = jnp.concatenate([unit_a, near_a], axis=0)
    pair_o = jnp.stack([out_slice, far_o])
    qkv_theirs = links.core(qkv_sent)
    far_a = links.swap(pair_a, df=2)
    near_o = links.swap(pair_o, df=1)
    token = step(qkv_sent, pair_a, pair_o)
    qkv_theirs, near_o = gate([qkv_theirs, near_o], token)
    blocks = TOK_DEV // BLK
    docs = doc_ids[0]
    own_docs = lax.dynamic_slice_in_dim(docs, ctx_at * blocks, blocks)
    lows = jnp.sum((docs[None, :] < own_docs[:, None]).astype(jnp.int32), axis=1)
    lows = lows + (n_ctx - 1 - ctx_at) * blocks
    out_z = jnp.stack([near_o[0], far_o, near_o[1]])
    out_mine = links.gather_plane(out_z)

    def three_z(own, far, near):
        return jnp.concatenate([first_half(near), far, second_half(near)], axis=0)

    qkv_full, gains, normed, q_t, kv = project(
        place, x_in, cosines, sines, after(qkv_own, token, out_z), qkv_mine, qkv_theirs
    )
    spans = [links.later(kv, d, 1) for d in range(n_ctx - 1, 0, -1)] + [kv]
    token = step(kv)
    *spans, far_a = gate([*spans[:-1], far_a], token)
    spans = [*spans, kv]
    out_mine = gate(out_mine, token)
    out_theirs = links.core(jnp.stack(out_mine))
    first_a = jnp.concatenate([near_a, far_a], axis=0)
    rest_a = [links.plane(first_a, bits) for bits in (1, 2, 3)]
    far_b = links.swap(after(unit_b, first_a), df=2)
    attn_t, log_total = attend(lows, after(q_t, first_a), spans)
    far_b, out_theirs = gate([far_b, out_theirs], attn_t)
    pair_b = jnp.concatenate([unit_b, far_b], axis=0)
    near_b = links.swap(pair_b, df=1)
    dy_oth = links.core(dy_own)
    out_full, hidden, normed_mlp = project_out(
        place, x_in, gains, after(attn_t, step(pair_b)), w_out, out_mine, out_theirs
    )

    x_oth = links.core(normed_mlp)
    near_b, *rest_a = gate([near_b, *rest_a], hidden)
    first_b = three_z(unit_b, far_b, near_b)
    rest_b = [links.plane(first_b, bits) for bits in (1, 2, 3)]
    mlp_weights = (w_gate_up, down_t, halves, half_down)
    tokens_mlp = (after(normed_mlp, first_b), x_oth, dy_own, dy_oth)
    results_a, keep_a, send_a = mlp_chunk(
        place, 0, tokens_mlp, mlp_weights, [first_a, *rest_a]
    )
    arrived_a = links.send_one(send_a)
    rest_b = gate(rest_b, results_a[0])
    results_b, keep_b, send_b = mlp_chunk(
        place,
        1,
        (normed_mlp, x_oth, dy_own, dy_oth),
        mlp_weights,
        [first_b, *rest_b],
        (results_a[1], results_a[3]),
    )

    dn_oth = [links.core(part) for part in (first_half(results_b[3]), second_half(results_b[3]))]
    d_hidden, d_hidden_b, d_attn_t, mlp_gain_grad = middle(
        hidden, dy_own, gains, (results_a[2], results_b[2], *dn_oth), out_full
    )
    stay_a, move_a = sum_one(keep_a, gate(arrived_a, d_hidden))
    arrived_a = links.send_two(move_a)
    arrived_b = links.send_one(gate(send_b, *move_a))
    dq_t, d_spans = attend_back(
        lows, q_t, attn_t, after(d_attn_t, *move_a), log_total, cosines, sines, spans
    )
    arrived = [
        links.later(value, d, -1) for value, d in zip(d_spans, range(n_ctx - 1, 0, -1))
    ]
    total_a = links.sum_two(stay_a, gate(arrived_a, dq_t))
    arrived_a = links.swap(total_a[1], df=1)
    stay_b, move_b = sum_one(keep_b, gate(arrived_b, dq_t))
    arrived_b = links.send_two(move_b)
    halves_o, theirs_o = early(
        place, normed, after(dq_t, *total_a), attn_t, d_hidden_b
    )
    arrived_o = links.core(theirs_o)
    left_a = add(total_a[0], after(arrived_a, halves_o[0]))
    arrived_a = links.swap(second_half(left_a), df=2)
    total_b = links.sum_two(stay_b, gate(arrived_b, halves_o[0]))
    arrived_b = links.swap(total_b[1], df=1)
    halves_o = [add(value, more) for value, more in zip(halves_o, arrived_o)]
    arrived_o = links.send_one(halves_o[2:])
    input_grad, halves_q, theirs_q = last(
        place,
        x_in,
        gains,
        normed,
        after(dq_t, left_a, *halves_o),
        cosines,
        sines,
        qkv_full,
        d_hidden,
        mlp_gain_grad,
        d_spans[-1],
        arrived,
    )
    arrived_q = links.core(theirs_q)
    stay_o, move_o = sum_one(halves_o[:2], gate(arrived_o, input_grad))
    arrived_o = links.send_two(move_o)
    left_b = add(total_b[0], after(arrived_b, input_grad))
    arrived_b = links.swap(second_half(left_b), df=2)
    total_a = add(first_half(left_a), after(arrived_a, input_grad))
    halves_q = [add(value, more) for value, more in zip(halves_q, arrived_q)]
    arrived_q = links.send_one(halves_q[2:])
    token = step(*halves_q, *move_o, left_b, total_a)
    stay_q, move_q = sum_one(halves_q[:2], gate(arrived_q, token))
    arrived_q = links.send_two(move_q)
    total_o = links.sum_two(stay_o, gate(arrived_o, token))
    arrived_o = links.swap(total_o[1], df=1)
    total_b = add(first_half(left_b), after(arrived_b, token))
    unit_mlp = jnp.concatenate([total_a, total_b], axis=1)
    mlp_x = links.plane(after(unit_mlp, *move_q), 1)
    mlp_y = links.plane(after(unit_mlp, *move_q), 2)
    token = step(*move_q, *total_o, unit_mlp)
    total_q = links.sum_two(stay_q, gate(arrived_q, token))
    units_q = [first_half(total_q[0]), first_half(total_q[1])]
    units_q += [second_half(total_q[0]), second_half(total_q[1])]
    arrived_q = [links.swap(units_q[bits], df=bits) for bits in (1, 2, 3)]
    left_o = add(total_o[0], arrived_o)
    arrived_o = links.swap(second_half(left_o), df=2)
    token = step(*units_q, left_o)
    done_q = units_q[0].astype(F32)
    for value in gate(arrived_q, token):
        done_q = done_q + value.astype(F32)
    done_o = add(first_half(left_o), after(arrived_o, token))
    rows = jnp.concatenate([done_o, done_q.astype(BF16)], axis=1)
    row_far = links.plane(rows, 2)
    mlp_top = links.plane(after(mlp_y[:TILE], rows), 1)
    mlp_low = links.plane(after(mlp_x[TILE:], rows), 2)
    mlp_oth = links.core(jnp.stack([unit_mlp, mlp_x, mlp_y]))
    out_oth = links.core(after(results_b[1], rows))
    result = hidden + results_a[0].astype(F32) + results_b[0].astype(F32)
    result = result + out_oth.astype(F32)
    output = result.astype(BF16).T[None]
    near = jnp.stack([rows, row_far])
    far = links.plane(near, 1)
    near_oth = links.core(near)
    mlp_xy = jnp.concatenate([mlp_top, mlp_low], axis=0)
    xy_oth = links.core(mlp_xy)
    grad_gate_up, grad_down = finish_mlp(
        place, [unit_mlp, mlp_x, mlp_y, mlp_xy, mlp_oth, xy_oth]
    )
    far = after(far, grad_gate_up, output)
    far_oth = links.core(far)
    grad_qkv, grad_out, gain_rows = finish_rows(
        place, [near, far, near_oth, far_oth], 2, grad_gate_up
    )
    return (
        output,
        input_grad.T[None],
        gain_rows[0, :ROWS],
        grad_qkv,
        grad_out,
        gain_rows[1, :ROWS],
        grad_gate_up,
        grad_down.T,
    )


def solution(mesh):
    placed = (
        P(("seq", "fsdp"), "ctx", None),
        P(("seq", "fsdp"), "ctx", None),
        P(("seq", "fsdp"), "ctx"),
        P(("seq", "fsdp"), None),
        P("fsdp"),
        P("fsdp", None),
        P("fsdp", None),
        P("fsdp"),
        P("fsdp", None),
        P("fsdp", None),
    )
    links = Links([mesh.shape[name] for name in AXES])
    return jax.shard_map(
        functools.partial(shards, links),
        mesh=mesh,
        in_specs=placed,
        out_specs=(
            P(("seq", "fsdp"), "ctx", None),
            P(("seq", "fsdp"), "ctx", None),
            P("fsdp"),
            P("fsdp", None),
            P("fsdp", None),
            P("fsdp"),
            P("fsdp", None),
            P("fsdp", None),
        ),
        check_vma=False,
    )
```

```python
import functools

import jax
import jax.numpy as jnp
from jax import lax
from jax.experimental import pallas as pl
from jax.experimental.pallas import tpu as pltpu
from jax.sharding import PartitionSpec as P

D = 960
HEADS = 15
KV_HEADS = 5
HEAD_DIM = 64
FF = 2560
BLK = 128
TOK_DEV = 512
KV_DIM = 320
QKV = D + 2 * KV_DIM
QKV_WIDE = 1664
CUT = 896
EARLY_WIDE = 1920
FF_SHARD = FF // 4
ROWS = D // 4
ROWS_PAD = 256
SLICE = 32
TILE = 128
HALF = 64
ROW_TILE = 256
VMEM_LIMIT = 56 * 1024 * 1024

EPSILON = 1e-05
ROPE_BASE = 100000.0
MASKED_SCORE = -1e30
AXES = ("seq", "ctx", "fsdp")
F32 = jnp.float32
BF16 = jnp.bfloat16
ANY = pl.BlockSpec(memory_space=pl.ANY)
SMEM = pl.BlockSpec(memory_space=pltpu.SMEM)
VMEM = pl.BlockSpec(memory_space=pltpu.VMEM)
LONG = pl.CostEstimate(flops=40_000_000_000, bytes_accessed=1000, transcendentals=0)
SHORT = pl.CostEstimate(flops=1000, bytes_accessed=1000, transcendentals=0)
NT = (((1,), (1,)), ((), ()))
TN = (((0,), (0,)), ((), ()))


def frequencies():
    steps = jnp.arange(HEAD_DIM // 2, dtype=F32) * 2.0 / HEAD_DIM
    return ROPE_BASE ** (-steps)


def after(value, *earlier):
    return lax.optimization_barrier((value, *earlier))[0]


def gate(values, *earlier):
    return [after(value, *earlier) for value in values]


def step_kernel(before, behind):
    behind[...] = before[...]


def step(*needed):
    shape = jax.ShapeDtypeStruct((8, 128), F32)
    token = after(jnp.zeros(shape.shape, F32), *needed)
    return pl.pallas_call(
        step_kernel, out_shape=shape, in_specs=[VMEM], out_specs=VMEM, cost_estimate=LONG
    )(token)


def add(first, second):
    return (first.astype(F32) + second.astype(F32)).astype(BF16)


def sum_one(keep, arrived):
    pairs = list(zip(keep, arrived))
    stay = [value[0].astype(F32) + more[0].astype(F32) for value, more in pairs]
    return stay, [add(value[1], more[1]) for value, more in pairs]


def first_half(value):
    return value[: value.shape[0] // 2]


def second_half(value):
    return value[value.shape[0] // 2 :]


class Links:
    def __init__(self, sizes):
        self.sizes = sizes

    def index(self, s, c, f):
        return (s * self.sizes[1] + c) * self.sizes[2] + f

    def swap(self, value, ds=0, dc=0, df=0):
        n_s, n_c, n_f = self.sizes
        pairs = [
            (self.index(s, c, f), self.index(s ^ ds, c ^ dc, f ^ df))
            for s in range(n_s)
            for c in range(n_c)
            for f in range(n_f)
        ]
        return lax.ppermute(value, AXES, pairs)

    def later(self, value, blocks, sign):
        n_s, n_c, n_f = self.sizes
        pairs = []
        for s in range(n_s):
            for c in range(n_c - blocks):
                for f in range(n_f):
                    pair = (self.index(s, c, f), self.index(s, c + blocks, f))
                    pairs.append(pair if sign > 0 else pair[::-1])
        return lax.ppermute(value, AXES, pairs)

    def core(self, value):
        return self.swap(value, ds=1)

    def plane(self, value, bits):
        return self.swap(value, ds=bits & 2, dc=bits & 1)

    def gather_plane(self, own):
        return [own] + [self.plane(own, bits) for bits in (1, 2, 3)]

    def gather_z(self, own):
        return [self.swap(own, df=bits) for bits in (1, 2, 3)]

    def send_one(self, send):
        return [self.plane(value, bits) for value, bits in zip(send, (1, 2))]

    def send_two(self, move):
        return [self.plane(value, bits) for value, bits in zip(move, (2, 1))]

    def sum_two(self, stay, arrived):
        pairs = zip(stay, arrived)
        return [self.sum_ctx((value + more.astype(F32)).astype(BF16)) for value, more in pairs]

    def sum_ctx(self, value):
        step = 2
        while step < self.sizes[1]:
            value = add(value, self.swap(value, dc=step))
            step *= 2
        return value

    def gather_pairs(self, own, first):
        near = jnp.stack([own, self.plane(own, first)])
        far = self.plane(near, 3 - first)
        return near, far, self.core(near), self.core(far)


def piece_index(first, q):
    return (q & (3 - first)) // (3 - first), (q & first) // first


UNIT_TILES = (5, 3)
HIDDEN = (768, 512)
DOWN_AT = (3, 2)


def mlp_kernel(chunk, place, x_own, x_oth, dy_own, dy_oth, gate_up, w_down, halves, half_down, *rest):
    messages, rest = rest[:4], rest[4:]
    if chunk:
        carried, rest = rest[:2], rest[2:]
    results, (keep_x, keep_y, send_x, send_y), rest = rest[:4], rest[4:8], rest[8:]
    weight, drop, drop_half, act, dgu, units, x_t, dy_t, x, dy, out_t, dn_t, sems = rest
    hidden, down_at = HIDDEN[chunk], DOWN_AT[chunk]
    with_half = chunk == 0
    p, k, f = place[0], place[1], place[2]
    groups = ([], [], [], [])

    def copy(source, target, group):
        groups[group].append(pltpu.make_async_copy(source, target, sems.at[group]))

    for half, (xs, ds) in enumerate(((x_own, dy_own), (x_oth, dy_oth))):
        lanes = pl.ds(half * TOK_DEV, TOK_DEV)
        copy(xs, x_t.at[:, lanes], 0)
        copy(ds, dy_t.at[:, lanes], 3)
    if chunk:
        for source, target in zip(carried, (out_t, dn_t)):
            copy(source, target.at[:, pl.ds(TOK_DEV, TOK_DEV)], 3)
    tile_of_core = 2 * k + chunk
    for kind in range(2):
        for z in range(4):
            col = pl.multiple_of(kind * FF + z * FF_SHARD + tile_of_core * TILE, TILE)
            copy(
                gate_up.at[:, pl.ds(col, TILE)],
                weight.at[f, :, pl.ds(kind * hidden + z * TILE, TILE)],
                1,
            )
        if with_half:
            copy(
                halves.at[:, pl.ds(kind * 2 * TILE, 2 * TILE)],
                weight.at[f, :, pl.ds(kind * hidden + 4 * TILE, 2 * TILE)],
                1,
            )
    copy(
        w_down.at[:, pl.ds(pl.multiple_of(tile_of_core * TILE, TILE), TILE)],
        drop.at[:, pl.ds(pl.multiple_of(f * TILE, TILE), TILE)],
        3,
    )
    if with_half:
        copy(half_down, drop_half.at[f], 3)
    for q, ref in enumerate(messages):
        pp = jnp.bitwise_xor(p, q)
        for r in range(3):
            z = jnp.bitwise_xor(f, r + 1)
            rows = pl.ds(r * ROWS, ROWS)
            for kind in range(2):
                lane = pl.multiple_of(kind * hidden + pp * TILE, TILE)
                copy(
                    ref.at[rows, pl.ds(kind * TILE, TILE)],
                    weight.at[z, :, pl.ds(lane, TILE)],
                    1,
                )
            rows_at = pl.ds(pl.multiple_of(pp * ROWS, 16), ROWS)
            copy(
                ref.at[rows, pl.ds(down_at * TILE, TILE)],
                drop.at[rows_at, pl.ds(pl.multiple_of(z * TILE, TILE), TILE)],
                3,
            )
            if with_half:
                lane = jnp.right_shift(pp, 1) * hidden + 4 * TILE + jnp.bitwise_and(pp, 1) * TILE
                copy(
                    ref.at[rows, pl.ds(2 * TILE, TILE)],
                    weight.at[z, :, pl.ds(pl.multiple_of(lane, TILE), TILE)],
                    1,
                )
                copy(ref.at[rows, pl.ds(4 * TILE, TILE)], drop_half.at[z, rows_at], 3)
    for group in groups:
        for each in group:
            each.start()
    for each in groups[0]:
        each.wait()
    x[...] = x_t[...].T
    for each in groups[1]:
        each.wait()

    for t in range(2 * TOK_DEV // ROW_TILE):
        rows = slice(t * ROW_TILE, (t + 1) * ROW_TILE)
        both = weight[...].reshape(D, 2 * hidden)
        gu = jnp.dot(x[rows, :], both, preferred_element_type=F32)
        if t == 0:
            for each in groups[3]:
                each.wait()
            dy[...] = dy_t[...].T
            if with_half:
                for z in range(4):
                    lane = 4 * TILE + z * HALF
                    drop[:, lane : lane + HALF] = drop_half[z, :, :HALF]
        da = jnp.dot(dy[rows, :], drop[...], preferred_element_type=F32)
        g, u = gu[:, :hidden], gu[:, hidden:]
        sig = jax.nn.sigmoid(g)
        silu = g * sig
        a = (silu * u).astype(BF16)
        act[rows, :] = a
        dgu[rows, :hidden] = (da * u * (sig + silu * (1.0 - sig))).astype(BF16)
        dgu[rows, hidden:] = (da * silu).astype(BF16)
        out = lax.dot_general(drop[...], a, NT, preferred_element_type=F32)
        dn = lax.dot_general(both, dgu[rows, :], NT, preferred_element_type=F32)
        if chunk and t * ROW_TILE >= TOK_DEV:
            out = out + out_t[:, rows].astype(F32)
            dn = dn + dn_t[:, rows].astype(F32)
        out_t[:, rows] = out.astype(BF16)
        dn_t[:, rows] = dn.astype(BF16)

    groups = ([], [], [])
    for at, ref in enumerate((out_t, dn_t)):
        for half in range(2):
            copy(ref.at[:, pl.ds(half * TOK_DEV, TOK_DEV)], results[2 * at + half], 2)
    for each in groups[2]:
        each.start()

    step = 2 * TILE
    for start in range(0, hidden, step):
        grad = jnp.dot(
            dy_t[...], act[:, start : start + step], preferred_element_type=F32
        ).astype(BF16)
        if start < 4 * TILE:
            for part in range(2):
                z = start // TILE + part
                units[:, z, :, down_at * TILE : (down_at + 1) * TILE] = grad[
                    :, part * TILE : (part + 1) * TILE
                ].reshape(4, ROWS, TILE)
        else:
            for z in range(4):
                units[:, z, :, 4 * TILE : 4 * TILE + HALF] = grad[
                    :, z * HALF : (z + 1) * HALF
                ].reshape(4, ROWS, HALF)
    for pair in range(2):
        columns = [(kind * hidden + pair * step, kind) for kind in range(2)]
        if with_half:
            columns.append((pair * hidden + 4 * TILE, 2))
        for start, column in columns:
            grad = jnp.dot(
                x_t[...], dgu[:, start : start + step], preferred_element_type=F32
            ).astype(BF16)
            for part in range(2):
                units[2 * pair + part, :, :, column * TILE : (column + 1) * TILE] = grad[
                    :, part * TILE : (part + 1) * TILE
                ].reshape(4, ROWS, TILE)
        for pp in (2 * pair, 2 * pair + 1):
            q = jnp.bitwise_xor(p, pp)
            for bits in range(4):
                left = (keep_x, send_x)[bits & 1].at[bits >> 1]
                right = (keep_y, send_y)[bits >> 1].at[bits & 1]

                def send(pp=pp, left=left, right=right):
                    for r in range(4):
                        pltpu.make_async_copy(
                            units.at[pp, jnp.bitwise_xor(f, r)],
                            (left, right)[r & 1].at[pl.ds((r >> 1) * ROWS, ROWS)],
                            sems.at[2],
                        ).start()

                pl.when(q == bits)(send)
    for each in groups[2]:
        each.wait()
    for target in (keep_x, keep_y, send_x, send_y):
        for at in range(2):
            for r in range(2):
                pltpu.make_async_copy(
                    units.at[0, 0], target.at[at, pl.ds(r * ROWS, ROWS)], sems.at[2]
                ).wait()


def mlp_chunk(place, chunk, tokens, weights, messages, carried=()):
    hidden = HIDDEN[chunk]
    width = UNIT_TILES[chunk] * TILE
    part = jax.ShapeDtypeStruct((2, 2 * ROWS, width), BF16)
    operands = [place, *tokens, *weights, *messages, *carried]
    out = pl.pallas_call(
        functools.partial(mlp_kernel, chunk),
        out_shape=[jax.ShapeDtypeStruct((D, TOK_DEV), BF16)] * 4 + [part] * 4,
        in_specs=[SMEM] + [ANY] * (len(operands) - 1),
        out_specs=[ANY] * 8,
        scratch_shapes=[
            pltpu.VMEM((4, ROWS, 2 * hidden), BF16),
            pltpu.VMEM((D, hidden), BF16),
            pltpu.VMEM((4, D, TILE), BF16),
            pltpu.VMEM((2 * TOK_DEV, hidden), BF16),
            pltpu.VMEM((2 * TOK_DEV, 2 * hidden), BF16),
            pltpu.VMEM((4, 4, ROWS, width), BF16),
            pltpu.VMEM((D, 2 * TOK_DEV), BF16),
            pltpu.VMEM((D, 2 * TOK_DEV), BF16),
            pltpu.VMEM((2 * TOK_DEV, D), BF16),
            pltpu.VMEM((2 * TOK_DEV, D), BF16),
            pltpu.VMEM((D, 2 * TOK_DEV), BF16),
            pltpu.VMEM((D, 2 * TOK_DEV), BF16),
            pltpu.SemaphoreType.DMA((4,)),
        ],
        compiler_params=pltpu.CompilerParams(vmem_limit_bytes=VMEM_LIMIT),
        cost_estimate=LONG,
    )(*operands)
    return out[:4], out[4:6], out[6:8]


def finish_mlp_kernel(place, m0, m1, m2, m3, three_oth, xy_oth, up, down):
    p, k = place[0], place[1]
    for q, mine in enumerate((m0, m1, m2, m3)):
        theirs = three_oth.at[q] if q < 3 else xy_oth
        pp = jnp.bitwise_xor(p, q)
        rows = pl.ds(pl.multiple_of(pp * ROWS, 16), ROWS)
        for other, ref in enumerate((mine, theirs)):
            kk = jnp.bitwise_xor(k, other)
            for chunk in range(2):
                at = chunk * UNIT_TILES[0] * TILE
                for kind in range(2):
                    col = kind * FF + pp * FF_SHARD + (2 * kk + chunk) * TILE
                    lane = at + kind * TILE
                    up[:, pl.ds(pl.multiple_of(col, TILE), TILE)] = ref[
                        :, lane : lane + TILE
                    ].astype(F32)
                lane = at + DOWN_AT[chunk] * TILE
                col = pl.multiple_of((2 * kk + chunk) * TILE, TILE)
                down[rows, pl.ds(col, TILE)] = ref[:, lane : lane + TILE].astype(F32)
        own, oth = (ref[:, 2 * TILE : 3 * TILE].astype(F32) for ref in (mine, theirs))
        low, high = jnp.where(k == 0, own, oth), jnp.where(k == 0, oth, own)
        for half in range(2):
            lanes = slice(half * HALF, (half + 1) * HALF)
            z = 2 * jnp.bitwise_and(pp, 1) + half
            col = jnp.right_shift(pp, 1) * FF + z * FF_SHARD + 4 * TILE
            up[:, pl.ds(pl.multiple_of(col, TILE), TILE)] = jnp.concatenate(
                [low[:, lanes], high[:, lanes]], axis=1
            )
        lanes = slice(4 * TILE, 4 * TILE + HALF)
        own, oth = (ref[:, lanes].astype(F32) for ref in (mine, theirs))
        low, high = jnp.where(k == 0, own, oth), jnp.where(k == 0, oth, own)
        down[rows, 4 * TILE :] = jnp.concatenate([low, high], axis=1)


def finish_mlp(place, pieces):
    return pl.pallas_call(
        finish_mlp_kernel,
        out_shape=[
            jax.ShapeDtypeStruct((ROWS, 2 * FF), F32),
            jax.ShapeDtypeStruct((D, FF_SHARD), F32),
        ],
        in_specs=[SMEM] + [VMEM] * 6,
        out_specs=[VMEM] * 2,
        compiler_params=pltpu.CompilerParams(vmem_limit_bytes=VMEM_LIMIT),
        cost_estimate=SHORT,
    )(place, *pieces)


def load_rows(place, own, mine, theirs, full, sem):
    p, k, f = place[0], place[1], place[2]
    for start in (True, False):

        def run(copy, start=start):
            if start:
                copy.start()
            else:
                copy.wait()

        run(pltpu.make_async_copy(own, full.at[f], sem))
        for other in range(2):
            kk = jnp.bitwise_xor(k, other)
            for q in range(4):
                ref = theirs.at[q] if other else mine[q]
                pp = jnp.bitwise_xor(p, q)
                row = pl.multiple_of(kk * 128 + pp * SLICE, 16)
                short = (kk * 4 + pp) == 7
                for r in range(3):
                    z = jnp.bitwise_xor(f, r + 1)

                    def go(count, ref=ref, r=r, z=z, row=row):
                        run(
                            pltpu.make_async_copy(
                                ref.at[r, pl.ds(0, count)], full.at[z, pl.ds(row, count)], sem
                            )
                        )

                    pl.when(short)(functools.partial(go, 16))
                    pl.when(jnp.logical_not(short))(functools.partial(go, SLICE))


def store_rows(place, grad, halves, theirs, sem):
    p, k, f = place[0], place[1], place[2]

    def target_of(other, q, r):
        at, index = (2 * (q & 1), q >> 1) if r & 1 == 0 else (1 + 2 * (q >> 1), q & 1)
        half = theirs.at[at] if other else halves[at]
        return half.at[index, pl.ds((r >> 1) * SLICE, SLICE)]

    for start in (True, False):
        for other in range(2):
            kk = jnp.bitwise_xor(k, other)
            for q in range(4):
                pp = jnp.bitwise_xor(p, q)
                row = pl.multiple_of(kk * 128 + pp * SLICE, 16)
                short = (kk * 4 + pp) == 7
                for r in range(4):
                    z = jnp.bitwise_xor(f, r)

                    def go(count, target=target_of(other, q, r), z=z, row=row):
                        copy = pltpu.make_async_copy(
                            grad.at[z, pl.ds(row, count)], target.at[pl.ds(0, count)], sem
                        )
                        if start:
                            copy.start()
                        else:
                            copy.wait()

                    pl.when(short)(functools.partial(go, 16))
                    pl.when(jnp.logical_not(short))(functools.partial(go, SLICE))


def finish_rows_kernel(first, place, near, far, near_oth, far_oth, behind, qkv, out, gain, columns):
    p, k = place[0], place[1]
    pairs = (near, far, near_oth, far_oth)
    for other in range(2):
        kk = jnp.bitwise_xor(k, other)
        for q in range(4):
            pp = jnp.bitwise_xor(p, q)
            row = pl.multiple_of(kk * 128 + pp * SLICE, 16)
            short = (kk * 4 + pp) == 7
            side, index = piece_index(first, q)
            value = pairs[2 * other + side][index].astype(F32)

            def go(count, value=value, row=row):
                rows = pl.ds(row, count)
                qkv[rows, :CUT] = value[:count, :CUT]
                qkv[rows, CUT:] = value[:count, EARLY_WIDE : EARLY_WIDE + QKV - CUT]
                out[rows, :] = value[:count, CUT : CUT + D]
                columns[rows, : QKV_WIDE - QKV] = value[:count, EARLY_WIDE + QKV - CUT :]

            pl.when(short)(functools.partial(go, 16))
            pl.when(jnp.logical_not(short))(functools.partial(go, SLICE))
    gain[...] = columns[...].T[:8]


def finish_rows(place, pairs, first, behind):
    return pl.pallas_call(
        functools.partial(finish_rows_kernel, first),
        out_shape=[
            jax.ShapeDtypeStruct((ROWS, QKV), F32),
            jax.ShapeDtypeStruct((ROWS, D), F32),
            jax.ShapeDtypeStruct((8, 2 * TILE), F32),
        ],
        in_specs=[SMEM] + [VMEM] * 4 + [ANY],
        out_specs=[VMEM] * 3,
        scratch_shapes=[pltpu.VMEM((2 * TILE, TILE), F32)],
        compiler_params=pltpu.CompilerParams(vmem_limit_bytes=VMEM_LIMIT),
        cost_estimate=SHORT,
    )(place, *pairs, behind)


def token_scale(values):
    return lax.rsqrt(jnp.mean(values * values, axis=0, keepdims=True) + EPSILON)


def tables_kernel(positions, frequency, cosines, sines):
    angles = frequency[:, :1] * positions[...].astype(F32)
    cosines[...] = jnp.cos(angles)
    sines[...] = jnp.sin(angles)


def tables(positions):
    frequency = jnp.broadcast_to(frequencies()[:, None], (HEAD_DIM // 2, TILE))
    return pl.pallas_call(
        tables_kernel,
        out_shape=[jax.ShapeDtypeStruct((HEAD_DIM // 2, TOK_DEV), F32)] * 2,
        in_specs=[VMEM] * 2,
        out_specs=[VMEM] * 2,
        cost_estimate=LONG,
    )(positions, frequency)


def project_kernel(
    place, x, cosines, sines, own, m0, m1, m2, m3, theirs, full, gains, normed, q_t, kv, sem
):
    load_rows(place, own, (m0, m1, m2, m3), theirs, full, sem)
    weight = full[...].reshape(D, QKV_WIDE)
    columns = weight[:, QKV - HALF :].astype(F32)
    gains[...] = columns
    source = x[...].astype(F32)
    normed[...] = (source * token_scale(source) * columns[:, HALF : HALF + 1]).astype(BF16)
    mixed = lax.dot_general(weight[:, :QKV], normed[...], TN, preferred_element_type=F32)
    cos, sin = cosines[...], sines[...]
    half = HEAD_DIM // 2
    for head in range(HEADS + KV_HEADS):
        row = head * HEAD_DIM
        low, high = mixed[row : row + half], mixed[row + half : row + HEAD_DIM]
        low, high = (low * cos - high * sin).astype(BF16), (high * cos + low * sin).astype(BF16)
        if head < HEADS:
            q_t[row : row + half, :] = low
            q_t[row + half : row + HEAD_DIM, :] = high
        else:
            row -= D
            for block in range(TOK_DEV // BLK):
                lanes = slice(block * BLK, (block + 1) * BLK)
                kv[block, row : row + half, :] = low[:, lanes]
                kv[block, row + half : row + HEAD_DIM, :] = high[:, lanes]
    for block in range(TOK_DEV // BLK):
        lanes = slice(block * BLK, (block + 1) * BLK)
        kv[block, KV_DIM:, :] = mixed[D + KV_DIM :, lanes].astype(BF16)


def project(place, x, cosines, sines, own, mine, theirs):
    return pl.pallas_call(
        project_kernel,
        out_shape=[
            jax.ShapeDtypeStruct((4, ROWS, QKV_WIDE), BF16),
            jax.ShapeDtypeStruct((D, TILE), F32),
            jax.ShapeDtypeStruct((D, TOK_DEV), BF16),
            jax.ShapeDtypeStruct((D, TOK_DEV), BF16),
            jax.ShapeDtypeStruct((TOK_DEV // BLK, 2 * KV_DIM, BLK), BF16),
        ],
        in_specs=[SMEM] + [VMEM] * 3 + [ANY] * 6,
        out_specs=[VMEM] * 5,
        scratch_shapes=[pltpu.SemaphoreType.DMA(())],
        compiler_params=pltpu.CompilerParams(vmem_limit_bytes=VMEM_LIMIT),
        cost_estimate=LONG,
    )(place, x, cosines, sines, own, *mine, theirs)


def three_heads(ref, group, lanes):
    first = group * (HEADS // KV_HEADS) * HEAD_DIM
    return jnp.concatenate(
        [
            ref[first + r * HEAD_DIM : first + (r + 1) * HEAD_DIM, lanes]
            for r in range(HEADS // KV_HEADS)
        ],
        axis=1,
    )


def diagonal_mask():
    shape = (BLK, BLK * (HEADS // KV_HEADS))
    keys = lax.broadcasted_iota(jnp.int32, shape, 0)
    queries = jnp.bitwise_and(lax.broadcasted_iota(jnp.int32, shape, 1), BLK - 1)
    return keys <= queries


def attend_kernel(lows, q_t, *rest):
    spans = rest[:-6]
    attn_t, log_total, kv, best, total, accum = rest[-6:]
    blocks = TOK_DEV // BLK
    for at, ref in enumerate(spans):
        kv[at * blocks : (at + 1) * blocks] = ref[...]
    own_at = (len(spans) - 1) * blocks
    mask = diagonal_mask()
    for i in range(blocks):
        lanes = slice(i * BLK, (i + 1) * BLK)
        queries = [
            three_heads(q_t, group, lanes) * jnp.asarray(HEAD_DIM**-0.5, BF16)
            for group in range(KV_HEADS)
        ]

        def step(j, diagonal, queries=queries):
            for group in range(KV_HEADS):
                keys = kv[j, group * HEAD_DIM : (group + 1) * HEAD_DIM, :]
                values = kv[j, KV_DIM + group * HEAD_DIM : KV_DIM + (group + 1) * HEAD_DIM, :]
                scores = lax.dot_general(keys, queries[group], TN, preferred_element_type=F32)
                if diagonal:
                    scores = jnp.where(mask, scores, MASKED_SCORE)
                    top = jnp.max(scores, axis=0, keepdims=True)
                    expo = jnp.exp(scores - top)
                    total[group] = jnp.sum(expo, axis=0, keepdims=True)
                    accum[group] = jnp.dot(values, expo.astype(BF16), preferred_element_type=F32)
                else:
                    old = best[group]
                    top = jnp.maximum(old, jnp.max(scores, axis=0, keepdims=True))
                    decay = jnp.exp(old - top)
                    expo = jnp.exp(scores - top)
                    total[group] = total[group] * decay + jnp.sum(expo, axis=0, keepdims=True)
                    accum[group] = accum[group] * decay + jnp.dot(
                        values, expo.astype(BF16), preferred_element_type=F32
                    )
                best[group] = top

        step(own_at + i, True)

        @pl.loop(lows[i], own_at + i)
        def earlier(j):
            step(j, False)

        for group in range(KV_HEADS):
            attn = (accum[group] / total[group]).astype(BF16)
            first = group * (HEADS // KV_HEADS) * HEAD_DIM
            for r in range(HEADS // KV_HEADS):
                attn_t[first + r * HEAD_DIM : first + (r + 1) * HEAD_DIM, lanes] = attn[
                    :, r * BLK : (r + 1) * BLK
                ]
            log_total[i * KV_HEADS + group] = best[group] + jnp.log(total[group])


def attend(lows, q_t, spans):
    blocks = TOK_DEV // BLK
    wide = BLK * (HEADS // KV_HEADS)
    return pl.pallas_call(
        attend_kernel,
        out_shape=[
            jax.ShapeDtypeStruct((D, TOK_DEV), BF16),
            jax.ShapeDtypeStruct((blocks * KV_HEADS, 1, wide), F32),
        ],
        in_specs=[SMEM] + [VMEM] * (1 + len(spans)),
        out_specs=[VMEM] * 2,
        scratch_shapes=[
            pltpu.VMEM((len(spans) * blocks, 2 * KV_DIM, BLK), BF16),
            pltpu.VMEM((KV_HEADS, 1, wide), F32),
            pltpu.VMEM((KV_HEADS, 1, wide), F32),
            pltpu.VMEM((KV_HEADS, HEAD_DIM, wide), F32),
        ],
        compiler_params=pltpu.CompilerParams(vmem_limit_bytes=VMEM_LIMIT),
        cost_estimate=LONG,
    )(lows, q_t, *spans)


def out_kernel(place, x, gains, attn_t, own, m0, m1, m2, m3, theirs, full, hidden, normed, sem):
    load_rows(place, own, (m0, m1, m2, m3), theirs, full, sem)
    value = x[...].astype(F32) + lax.dot_general(
        full[...].reshape(D, D), attn_t[...], TN, preferred_element_type=F32
    )
    hidden[...] = value
    normed[...] = (value * token_scale(value) * gains[:, HALF + 1 : HALF + 2]).astype(BF16)


def project_out(place, x, gains, attn_t, own, mine, theirs):
    return pl.pallas_call(
        out_kernel,
        out_shape=[
            jax.ShapeDtypeStruct((4, ROWS, D), BF16),
            jax.ShapeDtypeStruct((D, TOK_DEV), F32),
            jax.ShapeDtypeStruct((D, TOK_DEV), BF16),
        ],
        in_specs=[SMEM] + [VMEM] * 3 + [ANY] * 6,
        out_specs=[VMEM] * 3,
        scratch_shapes=[pltpu.SemaphoreType.DMA(())],
        compiler_params=pltpu.CompilerParams(vmem_limit_bytes=VMEM_LIMIT),
        cost_estimate=SHORT,
    )(place, x, gains, attn_t, own, *mine, theirs)


def norm_back(value, scale, gain, dn):
    unit = value * scale
    weighted = dn * gain
    d_value = scale * (weighted - unit * jnp.mean(weighted * unit, axis=0, keepdims=True))
    return d_value, jnp.sum(dn * unit, axis=1, keepdims=True)


def middle_kernel(
    hidden, dy, gains, dn0, dn1, dn2, dn3, full, d_hidden, d_hidden_b, d_attn_t, grad_gain
):
    value = hidden[...]
    dn = jnp.concatenate([dn2[...], dn3[...]], axis=0).astype(F32)
    dn = dn0[...].astype(F32) + dn1[...].astype(F32) + dn
    d_value, column = norm_back(value, token_scale(value), gains[:, HALF + 1 : HALF + 2], dn)
    grad_gain[...] = jnp.broadcast_to(column, (D, TILE))
    dh = dy[...].astype(F32) + d_value
    d_hidden[...] = dh
    dh = dh.astype(BF16)
    d_hidden_b[...] = dh
    d_attn_t[...] = jnp.dot(
        full[...].reshape(D, D), dh, preferred_element_type=F32
    ).astype(BF16)


def middle(hidden, dy, gains, dns, full):
    return pl.pallas_call(
        middle_kernel,
        out_shape=[
            jax.ShapeDtypeStruct((D, TOK_DEV), F32),
            jax.ShapeDtypeStruct((D, TOK_DEV), BF16),
            jax.ShapeDtypeStruct((D, TOK_DEV), BF16),
            jax.ShapeDtypeStruct((D, TILE), F32),
        ],
        in_specs=[VMEM] * 8,
        out_specs=[VMEM] * 4,
        compiler_params=pltpu.CompilerParams(vmem_limit_bytes=VMEM_LIMIT),
        cost_estimate=SHORT,
    )(hidden, dy, gains, *dns, full)


def attend_back_kernel(count, lows, q_t, attn_t, d_attn_t, log_total, cosines, sines, *rest):
    spans, rest = rest[:count], rest[count:]
    dq_t, d_spans, (kv, d_kv, d_query) = rest[0], rest[1 : 1 + count], rest[1 + count :]
    blocks = TOK_DEV // BLK
    groups = HEADS // KV_HEADS
    half = HEAD_DIM // 2
    for at, ref in enumerate(spans):
        kv[at * blocks : (at + 1) * blocks] = ref[...]
    d_kv[...] = jnp.zeros_like(d_kv)
    own_at = (count - 1) * blocks
    mask = diagonal_mask()
    for i in range(blocks):
        lanes = slice(i * BLK, (i + 1) * BLK)
        queries, d_outs, deltas = [], [], []
        for group in range(KV_HEADS):
            queries.append(three_heads(q_t, group, lanes) * jnp.asarray(HEAD_DIM**-0.5, BF16))
            d_out = three_heads(d_attn_t, group, lanes)
            attn = three_heads(attn_t, group, lanes)
            d_outs.append(d_out)
            deltas.append(
                jnp.sum(d_out.astype(F32) * attn.astype(F32), axis=0, keepdims=True)
            )

        def step(j, diagonal, i=i, queries=queries, d_outs=d_outs, deltas=deltas):
            for group in range(KV_HEADS):
                key_rows = slice(group * HEAD_DIM, (group + 1) * HEAD_DIM)
                value_rows = slice(KV_DIM + group * HEAD_DIM, KV_DIM + (group + 1) * HEAD_DIM)
                keys, values = kv[j, key_rows, :], kv[j, value_rows, :]
                scores = lax.dot_general(keys, queries[group], TN, preferred_element_type=F32)
                if diagonal:
                    scores = jnp.where(mask, scores, MASKED_SCORE)
                prob = jnp.exp(scores - log_total[i * KV_HEADS + group])
                d_prob = lax.dot_general(values, d_outs[group], TN, preferred_element_type=F32)
                d_scores = (prob * (d_prob - deltas[group])).astype(BF16)
                d_kv[j, value_rows, :] += lax.dot_general(
                    d_outs[group], prob.astype(BF16), NT, preferred_element_type=F32
                )
                d_kv[j, key_rows, :] += lax.dot_general(
                    queries[group], d_scores, NT, preferred_element_type=F32
                )
                more = jnp.dot(keys, d_scores, preferred_element_type=F32)
                if diagonal:
                    d_query[group] = more
                else:
                    d_query[group] += more

        step(own_at + i, True)

        @pl.loop(lows[i], own_at + i)
        def earlier(j):
            step(j, False)

        cos, sin = cosines[:, lanes], sines[:, lanes]
        for group in range(KV_HEADS):
            for r in range(groups):
                row = (group * groups + r) * HEAD_DIM
                side = slice(r * BLK, (r + 1) * BLK)
                low = d_query[group, :half, side] * HEAD_DIM**-0.5
                high = d_query[group, half:, side] * HEAD_DIM**-0.5
                dq_t[row : row + half, lanes] = (low * cos + high * sin).astype(BF16)
                dq_t[row + half : row + HEAD_DIM, lanes] = (high * cos - low * sin).astype(BF16)
    for at, ref in enumerate(d_spans):
        ref[...] = d_kv[at * blocks : (at + 1) * blocks].astype(ref.dtype)


def attend_back(lows, q_t, attn_t, d_attn_t, log_total, cosines, sines, spans):
    blocks = TOK_DEV // BLK
    wide = BLK * (HEADS // KV_HEADS)
    count = len(spans)
    shape = (blocks, 2 * KV_DIM, BLK)
    out = pl.pallas_call(
        functools.partial(attend_back_kernel, count),
        out_shape=[jax.ShapeDtypeStruct((D, TOK_DEV), BF16)]
        + [jax.ShapeDtypeStruct(shape, BF16)] * (count - 1)
        + [jax.ShapeDtypeStruct(shape, F32)],
        in_specs=[SMEM] + [VMEM] * (6 + count),
        out_specs=[VMEM] * (1 + count),
        scratch_shapes=[
            pltpu.VMEM((count * blocks, 2 * KV_DIM, BLK), BF16),
            pltpu.VMEM((count * blocks, 2 * KV_DIM, BLK), F32),
            pltpu.VMEM((KV_HEADS, HEAD_DIM, wide), F32),
        ],
        compiler_params=pltpu.CompilerParams(vmem_limit_bytes=VMEM_LIMIT),
        cost_estimate=LONG,
    )(lows, q_t, attn_t, d_attn_t, log_total, cosines, sines, *spans)
    return out[0], out[1:]


def early_kernel(place, normed, dq_t, attn_t, dh, *rest):
    halves, theirs, grad, sem = rest[:4], rest[4], rest[5], rest[6]
    product = lax.dot_general(attn_t[...], dh[...], NT, preferred_element_type=F32)
    grad[:, :, CUT : CUT + D] = product.astype(BF16).reshape(4, ROWS, D)
    product = lax.dot_general(normed[...], dq_t[:CUT, :], NT, preferred_element_type=F32)
    grad[:, :, :CUT] = product.astype(BF16).reshape(4, ROWS, CUT)
    store_rows(place, grad, halves, theirs, sem)


def early(place, normed, dq_t, attn_t, dh):
    piece = jax.ShapeDtypeStruct((2, 2 * SLICE, EARLY_WIDE), BF16)
    out = pl.pallas_call(
        early_kernel,
        out_shape=[*[piece] * 4, jax.ShapeDtypeStruct((4, 2, 2 * SLICE, EARLY_WIDE), BF16)],
        in_specs=[SMEM] + [VMEM] * 4,
        out_specs=[ANY] * 5,
        scratch_shapes=[pltpu.VMEM((4, ROWS, EARLY_WIDE), BF16), pltpu.SemaphoreType.DMA(())],
        compiler_params=pltpu.CompilerParams(vmem_limit_bytes=VMEM_LIMIT),
        cost_estimate=LONG,
    )(place, normed, dq_t, attn_t, dh)
    return out[:4], out[4]


def last_kernel(
    count, place, x, gains, normed, dq_t, cosines, sines, full, d_hidden, mlp_gain_grad, d_own, *rest
):
    arrived, rest = rest[:count], rest[count:]
    input_grad, halves, theirs, d_mixed, grad, sem = rest[0], rest[1:5], rest[5], *rest[6:]
    half = HEAD_DIM // 2
    d_mixed[:D, :] = dq_t[...]
    for block in range(TOK_DEV // BLK):
        lanes = slice(block * BLK, (block + 1) * BLK)
        value = d_own[block]
        for ref in arrived:
            value = value + ref[block].astype(F32)
        cos, sin = cosines[:, lanes], sines[:, lanes]
        for head in range(KV_HEADS):
            row = head * HEAD_DIM
            low, high = value[row : row + half], value[row + half : row + HEAD_DIM]
            d_mixed[D + row : D + row + half, lanes] = (low * cos + high * sin).astype(BF16)
            d_mixed[D + row + half : D + row + HEAD_DIM, lanes] = (high * cos - low * sin).astype(
                BF16
            )
        d_mixed[D + KV_DIM :, lanes] = value[KV_DIM:].astype(BF16)
    product = lax.dot_general(normed[...], d_mixed[CUT:, :], NT, preferred_element_type=F32)
    grad[:, :, : QKV - CUT] = product.astype(BF16).reshape(4, ROWS, QKV - CUT)
    weight = full[...].reshape(D, QKV_WIDE)[:, :QKV]
    dn = jnp.dot(weight, d_mixed[...], preferred_element_type=F32)
    source = x[...].astype(F32)
    d_value, column = norm_back(source, token_scale(source), gains[:, HALF : HALF + 1], dn)
    input_grad[...] = (d_hidden[...] + d_value).astype(BF16)
    lane = lax.broadcasted_iota(jnp.int32, (D, QKV_WIDE - QKV), 1)
    both = jnp.where(lane == 0, column, mlp_gain_grad[:, : QKV_WIDE - QKV])
    grad[:, :, QKV - CUT :] = both.astype(BF16).reshape(4, ROWS, QKV_WIDE - QKV)
    store_rows(place, grad, halves, theirs, sem)


def last(place, x, gains, normed, dq_t, cosines, sines, full, d_hidden, mlp_gain_grad, d_own, arrived):
    width = QKV_WIDE - CUT
    piece = jax.ShapeDtypeStruct((2, 2 * SLICE, width), BF16)
    out = pl.pallas_call(
        functools.partial(last_kernel, len(arrived)),
        out_shape=[
            jax.ShapeDtypeStruct((D, TOK_DEV), BF16),
            *[piece] * 4,
            jax.ShapeDtypeStruct((4, 2, 2 * SLICE, width), BF16),
        ],
        in_specs=[SMEM] + [VMEM] * (10 + len(arrived)),
        out_specs=[VMEM] + [ANY] * 5,
        scratch_shapes=[
            pltpu.VMEM((QKV, TOK_DEV), BF16),
            pltpu.VMEM((4, ROWS, width), BF16),
            pltpu.SemaphoreType.DMA(()),
        ],
        compiler_params=pltpu.CompilerParams(vmem_limit_bytes=VMEM_LIMIT),
        cost_estimate=LONG,
    )(place, x, gains, normed, dq_t, cosines, sines, full, d_hidden, mlp_gain_grad, d_own, *arrived)
    return out[0], out[1:5], out[5]


def shards(
    links,
    tokens,
    cotangent,
    positions,
    doc_ids,
    gain_attn,
    w_qkv,
    w_out,
    gain_mlp,
    w_gate_up,
    w_down,
):
    seq_at, ctx_at, f = (lax.axis_index(name) for name in AXES)
    k = jnp.bitwise_and(seq_at, 1)
    p = 2 * jnp.right_shift(seq_at, 1) + jnp.bitwise_and(ctx_at, 1)
    place = jnp.stack([p, k, f]).astype(jnp.int32)
    n_ctx = links.sizes[1]
    x_in, dy_own = tokens[0].T, cotangent[0].T

    def row_slice(weight):
        padded = jnp.pad(weight, ((0, ROWS_PAD - ROWS), (0, 0)))
        return lax.dynamic_slice_in_dim(padded, k * 128 + p * SLICE, SLICE, 0)

    def core_half(pair):
        return jnp.where(k == 0, pair[:, :HALF], pair[:, HALF:])

    halves = jnp.concatenate(
        [core_half(w_gate_up[:, at : at + TILE]) for at in range(4 * TILE, 2 * FF, FF_SHARD)],
        axis=1,
    )
    down_t = w_down.T
    half_down = jnp.pad(core_half(down_t[:, 4 * TILE :]), ((0, 0), (0, HALF)))

    def unit(chunk):
        tiles = []
        for kind in range(2):
            col = kind * FF + p * FF_SHARD + (2 * k + chunk) * TILE
            tiles.append(lax.dynamic_slice_in_dim(w_gate_up, col, TILE, 1))
        if chunk == 0:
            tiles.append(lax.dynamic_slice_in_dim(halves, p * TILE, TILE, 1))
        tiles.append(
            lax.dynamic_slice(down_t, (p * ROWS, (2 * k + chunk) * TILE), (ROWS, TILE))
        )
        if chunk == 0:
            tiles.append(lax.dynamic_slice_in_dim(half_down, p * ROWS, ROWS, 0))
        return jnp.concatenate(tiles, axis=1)

    pair = jnp.stack([gain_attn, gain_mlp], axis=1)
    gain_columns = jnp.pad(pair, ((0, 0), (0, QKV_WIDE - QKV - 2)))
    qkv_own = jnp.concatenate([w_qkv, gain_columns], axis=1)
    qkv_slice = jnp.concatenate([row_slice(w_qkv), row_slice(gain_columns)], axis=1)
    out_slice = row_slice(w_out)
    unit_a, unit_b = unit(0), unit(1)
    qkv_z = links.gather_z(qkv_slice)
    far_o = links.swap(out_slice, df=2)
    qkv_mine = links.gather_plane(jnp.stack(qkv_z))
    near_a = links.swap(after(unit_a, *qkv_z), df=1)
    cosines, sines = tables(after(positions, *qkv_z))
    near_a, far_o, *qkv_mine = gate([near_a, far_o, *qkv_mine], cosines)
    qkv_sent = jnp.stack(qkv_mine)
    pair_a = jnp.concatenate([unit_a, near_a], axis=0)
    pair_o = jnp.stack([out_slice, far_o])
    qkv_theirs = links.core(qkv_sent)
    far_a = links.swap(pair_a, df=2)
    near_o = links.swap(pair_o, df=1)
    token = step(qkv_sent, pair_a, pair_o)
    qkv_theirs, near_o = gate([qkv_theirs, near_o], token)
    blocks = TOK_DEV // BLK
    docs = doc_ids[0]
    own_docs = lax.dynamic_slice_in_dim(docs, ctx_at * blocks, blocks)
    lows = jnp.sum((docs[None, :] < own_docs[:, None]).astype(jnp.int32), axis=1)
    lows = lows + (n_ctx - 1 - ctx_at) * blocks
    out_z = jnp.stack([near_o[0], far_o, near_o[1]])
    out_mine = links.gather_plane(out_z)

    def three_z(own, far, near):
        return jnp.concatenate([first_half(near), far, second_half(near)], axis=0)

    qkv_full, gains, normed, q_t, kv = project(
        place, x_in, cosines, sines, after(qkv_own, token, out_z), qkv_mine, qkv_theirs
    )
    spans = [links.later(kv, d, 1) for d in range(n_ctx - 1, 0, -1)] + [kv]
    token = step(kv)
    *spans, far_a = gate([*spans[:-1], far_a], token)
    spans = [*spans, kv]
    out_mine = gate(out_mine, token)
    out_theirs = links.core(jnp.stack(out_mine))
    first_a = jnp.concatenate([near_a, far_a], axis=0)
    rest_a = [links.plane(first_a, bits) for bits in (1, 2, 3)]
    far_b = links.swap(after(unit_b, first_a), df=2)
    attn_t, log_total = attend(lows, after(q_t, first_a), spans)
    far_b, out_theirs = gate([far_b, out_theirs], attn_t)
    pair_b = jnp.concatenate([unit_b, far_b], axis=0)
    near_b = links.swap(pair_b, df=1)
    dy_oth = links.core(dy_own)
    out_full, hidden, normed_mlp = project_out(
        place, x_in, gains, after(attn_t, step(pair_b)), w_out, out_mine, out_theirs
    )

    x_oth = links.core(normed_mlp)
    near_b, *rest_a = gate([near_b, *rest_a], hidden)
    first_b = three_z(unit_b, far_b, near_b)
    rest_b = [links.plane(first_b, bits) for bits in (1, 2, 3)]
    mlp_weights = (w_gate_up, down_t, halves, half_down)
    tokens_mlp = (after(normed_mlp, first_b), x_oth, dy_own, dy_oth)
    results_a, keep_a, send_a = mlp_chunk(
        place, 0, tokens_mlp, mlp_weights, [first_a, *rest_a]
    )
    arrived_a = links.send_one(send_a)
    rest_b = gate(rest_b, results_a[0])
    results_b, keep_b, send_b = mlp_chunk(
        place,
        1,
        (normed_mlp, x_oth, dy_own, dy_oth),
        mlp_weights,
        [first_b, *rest_b],
        (results_a[1], results_a[3]),
    )

    dn_oth = [links.core(part) for part in (first_half(results_b[3]), second_half(results_b[3]))]
    d_hidden, d_hidden_b, d_attn_t, mlp_gain_grad = middle(
        hidden, dy_own, gains, (results_a[2], results_b[2], *dn_oth), out_full
    )
    stay_a, move_a = sum_one(keep_a, gate(arrived_a, d_hidden))
    arrived_a = links.send_two(move_a)
    arrived_b = links.send_one(gate(send_b, *move_a))
    dq_t, d_spans = attend_back(
        lows, q_t, attn_t, after(d_attn_t, *move_a), log_total, cosines, sines, spans
    )
    arrived = [
        links.later(value, d, -1) for value, d in zip(d_spans, range(n_ctx - 1, 0, -1))
    ]
    total_a = links.sum_two(stay_a, gate(arrived_a, dq_t))
    arrived_a = links.swap(total_a[1], df=1)
    stay_b, move_b = sum_one(keep_b, gate(arrived_b, dq_t))
    arrived_b = links.send_two(move_b)
    halves_o, theirs_o = early(
        place, normed, after(dq_t, *total_a), attn_t, d_hidden_b
    )
    arrived_o = links.core(theirs_o)
    left_a = add(total_a[0], after(arrived_a, halves_o[0]))
    arrived_a = links.swap(second_half(left_a), df=2)
    total_b = links.sum_two(stay_b, gate(arrived_b, halves_o[0]))
    arrived_b = links.swap(total_b[1], df=1)
    halves_o = [add(value, more) for value, more in zip(halves_o, arrived_o)]
    arrived_o = links.send_one(halves_o[2:])
    input_grad, halves_q, theirs_q = last(
        place,
        x_in,
        gains,
        normed,
        after(dq_t, left_a, *halves_o),
        cosines,
        sines,
        qkv_full,
        d_hidden,
        mlp_gain_grad,
        d_spans[-1],
        arrived,
    )
    arrived_q = links.core(theirs_q)
    stay_o, move_o = sum_one(halves_o[:2], gate(arrived_o, input_grad))
    arrived_o = links.send_two(move_o)
    left_b = add(total_b[0], after(arrived_b, input_grad))
    arrived_b = links.swap(second_half(left_b), df=2)
    total_a = add(first_half(left_a), after(arrived_a, input_grad))
    halves_q = [add(value, more) for value, more in zip(halves_q, arrived_q)]
    arrived_q = links.send_one(halves_q[2:])
    token = step(*halves_q, *move_o, left_b, total_a)
    stay_q, move_q = sum_one(halves_q[:2], gate(arrived_q, token))
    arrived_q = links.send_two(move_q)
    total_o = links.sum_two(stay_o, gate(arrived_o, token))
    arrived_o = links.swap(total_o[1], df=1)
    total_b = add(first_half(left_b), after(arrived_b, token))
    unit_mlp = jnp.concatenate([total_a, total_b], axis=1)
    mlp_x = links.plane(after(unit_mlp, *move_q), 1)
    mlp_y = links.plane(after(unit_mlp, *move_q), 2)
    token = step(*move_q, *total_o, unit_mlp)
    total_q = links.sum_two(stay_q, gate(arrived_q, token))
    units_q = [first_half(total_q[0]), first_half(total_q[1])]
    units_q += [second_half(total_q[0]), second_half(total_q[1])]
    arrived_q = [links.swap(units_q[bits], df=bits) for bits in (1, 2, 3)]
    left_o = add(total_o[0], arrived_o)
    arrived_o = links.swap(second_half(left_o), df=2)
    token = step(*units_q, left_o)
    done_q = units_q[0].astype(F32)
    for value in gate(arrived_q, token):
        done_q = done_q + value.astype(F32)
    done_o = add(first_half(left_o), after(arrived_o, token))
    rows = jnp.concatenate([done_o, done_q.astype(BF16)], axis=1)
    row_far = links.plane(rows, 2)
    mlp_top = links.plane(after(mlp_y[:TILE], rows), 1)
    mlp_low = links.plane(after(mlp_x[TILE:], rows), 2)
    mlp_oth = links.core(jnp.stack([unit_mlp, mlp_x, mlp_y]))
    out_oth = links.core(after(results_b[1], rows))
    result = hidden + results_a[0].astype(F32) + results_b[0].astype(F32)
    result = result + out_oth.astype(F32)
    output = result.astype(BF16).T[None]
    near = jnp.stack([rows, row_far])
    far = links.plane(near, 1)
    near_oth = links.core(near)
    mlp_xy = jnp.concatenate([mlp_top, mlp_low], axis=0)
    xy_oth = links.core(mlp_xy)
    grad_gate_up, grad_down = finish_mlp(
        place, [unit_mlp, mlp_x, mlp_y, mlp_xy, mlp_oth, xy_oth]
    )
    far = after(far, grad_gate_up, output)
    far_oth = links.core(far)
    grad_qkv, grad_out, gain_rows = finish_rows(
        place, [near, far, near_oth, far_oth], 2, grad_gate_up
    )
    return (
        output,
        input_grad.T[None],
        gain_rows[0, :ROWS],
        grad_qkv,
        grad_out,
        gain_rows[1, :ROWS],
        grad_gate_up,
        grad_down.T,
    )


def solution(mesh):
    placed = (
        P(("seq", "fsdp"), "ctx", None),
        P(("seq", "fsdp"), "ctx", None),
        P(("seq", "fsdp"), "ctx"),
        P(("seq", "fsdp"), None),
        P("fsdp"),
        P("fsdp", None),
        P("fsdp", None),
        P("fsdp"),
        P("fsdp", None),
        P("fsdp", None),
    )
    links = Links([mesh.shape[name] for name in AXES])
    return jax.shard_map(
        functools.partial(shards, links),
        mesh=mesh,
        in_specs=placed,
        out_specs=(
            P(("seq", "fsdp"), "ctx", None),
            P(("seq", "fsdp"), "ctx", None),
            P("fsdp"),
            P("fsdp", None),
            P("fsdp", None),
            P("fsdp"),
            P("fsdp", None),
            P("fsdp", None),
        ),
        check_vma=False,
    )
```
